32 devices in a mesh: sub: 8 (over y, x, core), grp: 4 (over z).
Axes of the slice: x: 2, y: 2, z: 4, core: 2. Of those that a mesh axis runs over, the one named last changes fastest.
Arguments:
- gap_data: float32 [96, 4, 1024], P(None, 'grp', 'sub'), may hold values from -6 to 6
- local_inverse: bfloat16 [96, 96, 4, 1024], P(None, None, 'grp', 'sub')
- stiffness: bfloat16 [2, 96, 96, 4, 1024], P(None, None, None, 'grp', 'sub')
- stiff_column: int32 [4, 1024], P('grp', 'sub'), may hold values from 0 to 1023, as said below
- neighbour: int32 [4, 1024], P('grp', 'sub'), may hold values from -1 to 1022, as said below
- corner_ops: bfloat16 [24, 96, 4, 1024], P(None, None, 'grp', 'sub'), may hold values from -0.625 to 0.625
- corner_index: int32 [4, 4, 1024], P(None, 'grp', 'sub'), may hold values from 0 to 1023
- coarse_inverse: bfloat16 [8, 768, 6144], P('grp', None, 'sub')
Outputs:
- multipliers: float32 [96, 4, 1024], P(None, 'grp', 'sub')
- residual: float32 [96, 4, 1024], P(None, 'grp', 'sub')
The draws below stay inside these ranges and needn't reach their ends.
Inputs may be any that keep to these rules, and one draw needn't show every extreme that they name: neighbour[y, x] is -1 or lies in [x - 128, x - 1]; every aligned block of 128 subdomains past the first has one entry equal to x - 128. stiff_column[y, x] lies in the same aligned block of 128 subdomains as x, is never x, and stiff_column[y, stiff_column[y, x]] = x; stiffness[1, :, :, y, stiff_column[y, x]] is the transpose of stiffness[1, :, :, y, x].
All inputs are finite; a program needn't handle non-finite values.
Results may differ from the reference program's by a relative error of at most 0.0008.
Values may be sent and summed in bfloat16 or wider, within the bound.
No kernel may reach another device: no remote copies, remote signals or barrier semaphores. Data moves between devices by JAX's collectives and lax.ppermute only.
A program may use at most 128 MiB of HBM per device.

```python
import math
import jax
import jax.numpy as jnp
import numpy as np
from jax import lax

IFACE = 96
SUBS_DEV = 128
CORNER_DOF = 6
CORNERS_SUB = 4
CORNER_BLOCK = 128
ITERS = 5
SUBDOMAINS = 1024
STRIPS = 4
GROUPS = 8
OWNER_BLOCKS = 8
GROUP_CORNERS = 1024
COARSE_ORDER = 768
CORNER_ROWS = 24


def symmetric_block(key, order, batch_shape, lower, upper, spread):
    first, second = jax.random.split(key)
    diagonal = jax.random.uniform(first, (order,) + batch_shape, jnp.float32, lower, upper)
    noise = jax.random.uniform(second, (order, order) + batch_shape, jnp.float32, -spread, spread)
    noise = 0.5 * (noise + jnp.swapaxes(noise, 0, 1))
    identity = jnp.eye(order, dtype=jnp.float32).reshape((order, order) + (1,) * len(batch_shape))
    return noise * (1.0 - identity) + identity * diagonal[None]


def partner_table(key):
    blocks = SUBDOMAINS // SUBS_DEV
    count = STRIPS * blocks
    keys = jax.random.split(jax.random.fold_in(key, 53), count)
    orders = jax.vmap(lambda single: jax.random.permutation(single, SUBS_DEV))(keys).astype(jnp.int32)
    swapped = orders.reshape(count, SUBS_DEV // 2, 2)[:, :, ::-1].reshape(count, SUBS_DEV)
    rows = jnp.arange(count, dtype=jnp.int32)[:, None]
    partner = jnp.zeros((count, SUBS_DEV), jnp.int32).at[rows, orders].set(swapped)
    base = jnp.arange(count, dtype=jnp.int32) % blocks * SUBS_DEV
    return (partner + base[:, None]).reshape(STRIPS, SUBDOMAINS).astype(jnp.int32)


def draw_local_inverse(key, part):
    block = symmetric_block(jax.random.fold_in(key, 11), IFACE, (STRIPS, SUBDOMAINS), 1.0, 2.0, 0.6 / IFACE)
    return block.astype(jnp.bfloat16)


def draw_stiffness(key, part):
    first, second = jax.random.split(jax.random.fold_in(key, 23))
    main = symmetric_block(first, IFACE, (STRIPS, SUBDOMAINS), 3.0, 5.0, 0.6 / IFACE)
    raw = jax.random.uniform(second, (IFACE, IFACE, STRIPS, SUBDOMAINS), jnp.float32, -2.4 / IFACE, 2.4 / IFACE)
    partner = partner_table(key)
    where = jnp.broadcast_to(partner[None, None], raw.shape)
    mirrored = jnp.swapaxes(jnp.take_along_axis(raw, where, axis=3), 0, 1)
    position = jnp.arange(SUBDOMAINS, dtype=jnp.int32)[None, :]
    coupled = jnp.where((position < partner)[None, None], raw, mirrored)
    return jnp.stack([main, coupled]).astype(jnp.bfloat16)


def draw_coarse_inverse(key, part):
    block = symmetric_block(jax.random.fold_in(key, 37), COARSE_ORDER, (OWNER_BLOCKS, GROUPS), 1.0, 2.0, 0.6 / COARSE_ORDER)
    block = jnp.transpose(block, (2, 0, 3, 1))
    return block.reshape(OWNER_BLOCKS, COARSE_ORDER, GROUPS * COARSE_ORDER).astype(jnp.bfloat16)


def draw_neighbour(key, part):
    position = jnp.arange(SUBDOMAINS, dtype=jnp.int32)[None, :]
    inside = position % SUBS_DEV
    offset = jax.random.randint(jax.random.fold_in(key, 41), (STRIPS, SUBDOMAINS), 0, SUBS_DEV, dtype=jnp.int32)
    offset = jnp.where(inside == 0, SUBS_DEV - 1, jnp.where(inside == SUBS_DEV - 1, 0, offset))
    return jnp.maximum(position - 1 - offset, -1).astype(jnp.int32)


def draw_stiff_column(key, part):
    return partner_table(key)


def plant(entries, rng, smallest, high):
    spot = [jax.random.randint(jax.random.fold_in(rng, axis), (), 0, length) for axis, length in enumerate(entries.shape)]
    longest = entries.shape.index(max(entries.shape))
    beside = spot[:longest] + [(spot[longest] + 1) % entries.shape[longest]] + spot[longest + 1:]
    return entries.at[tuple(spot)].set(smallest).at[tuple(beside)].set(high)


def steps_of(rng, extent, shards, least, top_value):
    factor_of = 1.0
    for axis_at, shards_of in shards:
        heights = jax.random.uniform(jax.random.fold_in(jax.random.fold_in(rng, 6), axis_at), (shards_of,), jnp.float32, least / len(shards), top_value / len(shards))
        factor_of = factor_of * jnp.repeat(jnp.exp(heights), extent[axis_at] // shards_of).reshape((-1,) + (1,) * (len(extent) - 1 - axis_at))
    return factor_of


def rank_bounds(count, slope):
    portions = [(1 << 20) // math.isqrt(grade ** slope) + 1 for grade in range(1, count + 1)]
    scale = 1 + sum(portions) // (1 << 30)
    return np.cumsum(np.array([max(1, weight // scale) for weight in portions]))


def skewed_ids(stream_key, dims, amount, slope):
    listing = rank_bounds(amount, slope)
    lot = jax.random.randint(jax.random.fold_in(stream_key, 1), dims, 0, int(listing[amount - 1]))
    grade = jnp.searchsorted(jnp.asarray(listing, jnp.int32), lot, side="right")
    return jax.random.permutation(jax.random.fold_in(stream_key, 2), amount)[grade].astype(jnp.int32)


def normal_values(own_key, shape, scale, bound, cuts=(), kind=jnp.bfloat16):
    gain = steps_of(own_key, shape, cuts, -0.22, 0.18) if cuts else 1.0
    result = jax.random.normal(own_key, shape, jnp.float32) * scale * gain
    return jnp.minimum(jnp.maximum(result, -bound), bound).astype(kind)


def setup_inputs(seed: int = 0) -> dict:
    seeds = jax.random.split(jax.random.key(seed), 9)
    gap_data = normal_values(seeds[0], (IFACE, STRIPS, SUBDOMAINS), 1.0, 6.0, ((1, 4), (2, 8)), jnp.float32)
    local_inverse = draw_local_inverse(jax.random.fold_in(seeds[8], 71), 0)
    stiffness = draw_stiffness(jax.random.fold_in(seeds[8], 71), 0)
    stiff_column = draw_stiff_column(jax.random.fold_in(seeds[8], 71), 0)
    neighbour = draw_neighbour(jax.random.fold_in(seeds[8], 71), 0)
    corner_ops = normal_values(seeds[5], (CORNER_ROWS, IFACE, STRIPS, SUBDOMAINS), IFACE ** -0.5, 0.625, ((2, 4), (3, 8)))
    corner_index = plant(skewed_ids(seeds[6], (CORNERS_SUB, STRIPS, SUBDOMAINS), GROUP_CORNERS, 1), jax.random.fold_in(seeds[6], 3), 0, GROUP_CORNERS - 1).astype(jnp.int32)
    coarse_inverse = draw_coarse_inverse(jax.random.fold_in(seeds[8], 71), 0)
    return dict(gap_data=gap_data, local_inverse=local_inverse, stiffness=stiffness, stiff_column=stiff_column, neighbour=neighbour, corner_ops=corner_ops, corner_index=corner_index, coarse_inverse=coarse_inverse)


precise = lax.Precision.HIGHEST


def batched(matrices, vector):
    columns = []
    for strip in range(STRIPS):
        columns.append(jnp.einsum("ijx,jx->ix", matrices[:, :, strip, :].astype(jnp.float32), vector[:, strip, :].astype(jnp.float32), precision=precise))
    return jnp.stack(columns, axis=1)


def transposed(matrices, vector):
    columns = []
    for strip in range(STRIPS):
        columns.append(jnp.einsum("cix,cx->ix", matrices[:, :, strip, :].astype(jnp.float32), vector[:, strip, :].astype(jnp.float32), precision=precise))
    return jnp.stack(columns, axis=1)


def jump_in(vector, neighbour):
    padded = jnp.concatenate([jnp.zeros_like(vector[:, :, :1]), vector], axis=2)
    where = jnp.broadcast_to((neighbour + 1).astype(jnp.int32)[None], vector.shape)
    return vector - jnp.take_along_axis(padded, where, axis=2)


def jump_out(vector, neighbour):
    where = (neighbour + 1).astype(jnp.int32)
    strips = jnp.arange(STRIPS, dtype=jnp.int32)[:, None]
    sums = jnp.zeros((vector.shape[0], STRIPS, SUBDOMAINS + 1), vector.dtype).at[:, strips, where].add(vector)
    return vector - sums[:, :, 1:]


def coarse_step(parts, corner_index, coarse_inverse):
    group = jnp.arange(SUBDOMAINS, dtype=jnp.int32) // SUBS_DEV
    segment = (group[None, None, :] * GROUP_CORNERS + corner_index).astype(jnp.int32)
    data = parts.reshape(CORNERS_SUB, CORNER_DOF, STRIPS, SUBDOMAINS).transpose(0, 2, 3, 1).reshape(-1, CORNER_DOF)
    totals = jax.ops.segment_sum(data, segment.reshape(-1), num_segments=GROUPS * GROUP_CORNERS)
    vector = totals.reshape(GROUPS, OWNER_BLOCKS, CORNER_BLOCK, CORNER_DOF).transpose(0, 1, 3, 2).reshape(GROUPS, OWNER_BLOCKS, COARSE_ORDER)
    blocks = coarse_inverse.reshape(OWNER_BLOCKS, COARSE_ORDER, GROUPS, COARSE_ORDER)
    solved = jnp.einsum("rpsq,srq->srp", blocks.astype(jnp.float32), vector.astype(jnp.float32), precision=precise)
    solved = solved.reshape(GROUPS, OWNER_BLOCKS, CORNER_DOF, CORNER_BLOCK).transpose(0, 1, 3, 2).reshape(GROUPS * GROUP_CORNERS, CORNER_DOF)
    picked = solved[segment]
    return picked.transpose(0, 3, 1, 2).reshape(CORNER_ROWS, STRIPS, SUBDOMAINS)


def reference(gap_data, local_inverse, stiffness, stiff_column, neighbour, corner_ops, corner_index, coarse_inverse):
    def precondition(vector):
        spread = jump_in(vector, neighbour)
        where = jnp.broadcast_to(stiff_column.astype(jnp.int32)[None], spread.shape)
        taken = jnp.take_along_axis(spread, where, axis=2)
        stiff = batched(stiffness[0], spread) + batched(stiffness[1], taken)
        return jump_out(stiff, neighbour)

    def apply_dual(vector):
        gap = jump_in(vector, neighbour)
        local = batched(local_inverse, gap)
        parts = batched(corner_ops, gap)
        picked = coarse_step(parts, corner_index, coarse_inverse)
        lifted = local + transposed(corner_ops, picked)
        return jump_out(lifted, neighbour)

    multipliers = jnp.zeros_like(gap_data)
    residual = gap_data
    direction = precondition(residual)
    norm_now = jnp.sum(residual * direction)
    for iteration in range(ITERS):
        image = apply_dual(direction)
        alpha = norm_now / jnp.sum(direction * image)
        multipliers = multipliers + alpha * direction
        residual = residual - alpha * image
        if iteration + 1 < ITERS:
            prepared = precondition(residual)
            norm_next = jnp.sum(residual * prepared)
            direction = prepared + (norm_next / norm_now) * direction
            norm_now = norm_next
    return multipliers, residual
```

```python
import jax
import jax.numpy as jnp
from jax import lax
from jax.sharding import PartitionSpec as P

CORNER_DOF = 6
CORNERS_SUB = 4
ITERS = 5


precise = lax.Precision.HIGHEST


def shifted(block, distance):
    count = lax.axis_size("sub")
    route = [(i, i + distance) for i in range(count) if 0 <= i + distance < count]
    return lax.ppermute(block, "sub", route)


def rotated(block, distance):
    count = lax.axis_size("grp")
    return lax.ppermute(block, "grp", [(i, (i + distance) % count) for i in range(count)])


def sum_all(parts):
    count = lax.axis_size("sub") * lax.axis_size("grp")
    spread = jnp.broadcast_to(parts[None, :], (count, parts.shape[0]))
    return jnp.sum(lax.all_to_all(spread, ("sub", "grp"), 0, 0, tiled=True), axis=0)


def on_device(
    gap_data,
    local_inverse,
    stiffness,
    stiff_column,
    neighbour,
    corner_ops,
    corner_index,
    coarse_inverse,
):
    cells = gap_data.shape[2]
    start = lax.axis_index("sub") * cells
    right_side = gap_data[:, 0, :]
    inverse = local_inverse[:, :, 0, :]
    main_block = stiffness[0, :, :, 0, :]
    coupled_block = stiffness[1, :, :, 0, :]
    column_local = stiff_column[0] - start
    slots = jnp.where(neighbour[0] < 0, -1, neighbour[0] - (start - cells))
    selector = (slots[None, :] == jnp.arange(2 * cells, dtype=jnp.int32)[:, None]).astype(
        jnp.float32
    )
    operators = corner_ops[:, :, 0, :]
    blocks_own = coarse_inverse.shape[0]
    order = coarse_inverse.shape[1]
    corner_block = order // CORNER_DOF
    owned_count = blocks_own * corner_block
    ranks = lax.axis_size("grp")
    me = lax.axis_index("grp")
    group_count = owned_count * ranks
    corner_table = (
        corner_index[:, 0, :, None] == jnp.arange(group_count, dtype=jnp.int32)[None, None, :]
    ).astype(jnp.float32)

    def spread(joined):
        return joined[:, cells:] - jnp.dot(
            joined, selector, precision=precise, preferred_element_type=jnp.float32
        )

    def collect(vector):
        moved = jnp.dot(vector, selector.T, precision=precise, preferred_element_type=jnp.float32)
        behind = moved[:, :cells]
        kept = vector - moved[:, cells:]
        returned = shifted(behind, -1)
        previous = shifted(kept, 1)
        return jnp.concatenate([previous - behind, kept - returned], axis=1)

    def precondition(joined):
        gap = spread(joined)
        taken = jnp.take(gap, column_local, axis=1)
        stiff = jnp.einsum(
            "ijx,jx->ix", main_block, gap, precision=precise, preferred_element_type=jnp.float32
        )
        stiff = stiff + jnp.einsum(
            "ijx,jx->ix",
            coupled_block,
            taken,
            precision=precise,
            preferred_element_type=jnp.float32,
        )
        return collect(stiff)

    def own_dot(first, second):
        return jnp.sum(first[:, cells:] * second[:, cells:])

    residual = jnp.concatenate([shifted(right_side, 1), right_side], axis=1)
    multipliers = jnp.zeros_like(right_side)
    direction = precondition(residual)
    norm_now = None
    for iteration in range(ITERS):
        gap = spread(direction)
        local = jnp.einsum(
            "ijx,jx->ix", inverse, gap, precision=precise, preferred_element_type=jnp.float32
        )
        parts = jnp.einsum(
            "cix,ix->cx", operators, gap, precision=precise, preferred_element_type=jnp.float32
        )
        parts = parts.reshape(CORNERS_SUB, CORNER_DOF, cells)
        sums = jnp.einsum(
            "kjx,kxm->jm",
            parts,
            corner_table,
            precision=precise,
            preferred_element_type=jnp.float32,
        )
        pieces = sums.reshape(CORNER_DOF, ranks, owned_count).transpose(1, 0, 2)
        owned = jnp.sum(lax.all_to_all(pieces, "grp", 0, 0, tiled=True), axis=0)
        arranged = (
            owned.reshape(CORNER_DOF, blocks_own, corner_block)
            .transpose(1, 0, 2)
            .reshape(blocks_own, order)
        )
        solved = jnp.einsum(
            "bpq,bq->bp",
            coarse_inverse,
            arranged,
            precision=precise,
            preferred_element_type=jnp.float32,
        )
        coarse_solved = (
            solved.reshape(blocks_own, CORNER_DOF, corner_block)
            .transpose(1, 0, 2)
            .reshape(CORNER_DOF, blocks_own * corner_block)
        )
        gathered = jnp.zeros((ranks, CORNER_DOF, owned_count), jnp.float32)
        for distance in range(ranks):
            piece = rotated(coarse_solved, distance) if distance else coarse_solved
            gathered = lax.dynamic_update_slice(
                gathered, piece[None], ((me - distance) % ranks, 0, 0)
            )
        values = gathered.transpose(1, 0, 2).reshape(CORNER_DOF, group_count)
        picked = jnp.einsum(
            "jm,kxm->kjx",
            values,
            corner_table,
            precision=precise,
            preferred_element_type=jnp.float32,
        )
        picked = picked.reshape(CORNERS_SUB * CORNER_DOF, cells)
        lifted = local + jnp.einsum(
            "cix,cx->ix", operators, picked, precision=precise, preferred_element_type=jnp.float32
        )
        image = collect(lifted)
        if iteration == 0:
            both = sum_all(
                jnp.stack([own_dot(residual, direction), own_dot(direction, image)])
            )
            norm_now = both[0]
            curvature = both[1]
        else:
            curvature = sum_all(own_dot(direction, image)[None])[0]
        alpha = norm_now / curvature
        multipliers = multipliers + alpha * direction[:, cells:]
        residual = residual - alpha * image
        if iteration + 1 < ITERS:
            prepared = precondition(residual)
            norm_next = sum_all(own_dot(residual, prepared)[None])[0]
            direction = prepared + norm_next / norm_now * direction
            norm_now = norm_next
    return (multipliers[:, None, :], residual[:, None, cells:])


def solution(mesh):
    in_specs = (
        P(None, "grp", "sub"),
        P(None, None, "grp", "sub"),
        P(None, None, None, "grp", "sub"),
        P("grp", "sub"),
        P("grp", "sub"),
        P(None, None, "grp", "sub"),
        P(None, "grp", "sub"),
        P("grp", None, "sub"),
    )
    out_specs = (P(None, "grp", "sub"), P(None, "grp", "sub"))
    return jax.shard_map(
        on_device, mesh=mesh, in_specs=in_specs, out_specs=out_specs, check_vma=False
    )
```

```python
import jax
import jax.numpy as jnp
from jax import lax
from jax.experimental import pallas as pl
from jax.experimental.pallas import tpu as pltpu
from jax.sharding import PartitionSpec as P

CORNER_DOF = 6
CORNERS_SUB = 4
ITERS = 5
ROWS = 8
NN = (((1,), (0,)), ((), ()))
NT = (((1,), (1,)), ((), ()))
F32 = jnp.float32
BF16 = jnp.bfloat16


def pieces_of(value):
    high = value.astype(BF16).astype(F32)
    rest = value - high
    middle = rest.astype(BF16).astype(F32)
    return [high, middle, rest - middle]


def exact_dot(value, table, dims):
    rows = value.shape[0]
    stacked = jnp.concatenate(pieces_of(value), axis=0).astype(BF16)
    product = lax.dot_general(stacked, table, dims, preferred_element_type=F32)
    return product[:rows] + product[rows : 2 * rows] + product[2 * rows :]


def lane_total(rows):
    return jnp.sum(rows, axis=1, keepdims=True)


def dot_rows(r, u, w, s=None, p=None):
    rows = [jnp.sum(r * u, axis=0, keepdims=True), jnp.sum(u * w, axis=0, keepdims=True)]
    if s is None:
        rows.append(jnp.zeros((ROWS - 2, r.shape[1]), F32))
    else:
        rows.append(jnp.sum(u * s, axis=0, keepdims=True))
        rows.append(jnp.sum(p * w, axis=0, keepdims=True))
        rows.append(jnp.zeros((ROWS - 4, r.shape[1]), F32))
    return jnp.concatenate(rows, axis=0)


def step_sizes(totals, before):
    sums = lane_total(totals)
    norm, curvature = sums[0:1], sums[1:2]
    if before is None:
        beta = None
    else:
        beta = norm / before[0:1, 0:1]
        curvature = curvature + beta * (sums[2:3] + sums[3:4]) + beta * beta * before[1:2, 0:1]
    return norm / curvature, beta, norm, curvature


def collect_to(vector, selector, low_ref, high_ref):
    iface, cells = vector.shape
    moved = exact_dot(vector, selector, NT)
    low_ref[:iface] = moved[:, :cells]
    high_ref[:iface] = vector - moved[:, cells:]


def spread_of(own, previous, selector):
    return own - exact_dot(jnp.concatenate([previous, own], axis=1), selector, NN)


def apply_blocks(blocks, vectors, out_ref):
    def step(index, carry):
        at = pl.ds(index * ROWS, ROWS)
        total = None
        for block, vector in zip(blocks, vectors):
            term = block[at].astype(F32) * vector[None]
            total = term if total is None else total + term
        out_ref[pl.ds(pl.multiple_of(index * ROWS, ROWS), ROWS)] = jnp.sum(total, axis=1)
        return carry

    lax.fori_loop(0, out_ref.shape[0] // ROWS, step, 0)


def table_kernel(slots_ref, column_ref, corner_ref, selector_ref, swap_ref, table_ref):
    def one_hot(row, count):
        places = lax.broadcasted_iota(jnp.int32, (count, row.shape[1]), 0)
        return jnp.where(places == row, 1.0, 0.0).astype(BF16)

    selector_ref[...] = one_hot(slots_ref[...], selector_ref.shape[0])
    swap_ref[...] = one_hot(column_ref[...], swap_ref.shape[0])
    chunk = 128

    def step(index, carry):
        row = corner_ref[...] - index * chunk
        table_ref[pl.ds(pl.multiple_of(index * chunk, chunk), chunk)] = one_hot(row, chunk)
        return carry

    lax.fori_loop(0, table_ref.shape[0] // chunk, step, 0)


def stiffen(own, previous, selector_ref, swap_ref, stiffness_ref, stiff_ref, low_ref, high_ref):
    gap = spread_of(own, previous, selector_ref[...])
    taken = exact_dot(gap, swap_ref[...], NN)
    apply_blocks([stiffness_ref.at[0], stiffness_ref.at[1]], [gap, taken], stiff_ref)
    collect_to(stiff_ref[...], selector_ref[...], low_ref, high_ref)


def first_kernel(own_ref, previous_ref, selector_ref, swap_ref, stiffness_ref, low_ref, high_ref, stiff_ref):
    iface, cells = own_ref.shape
    stiffen(
        own_ref[...], previous_ref[...], selector_ref, swap_ref, stiffness_ref, stiff_ref, low_ref, high_ref
    )
    low_ref[iface:] = jnp.zeros((ROWS, cells), F32)
    high_ref[iface:] = jnp.zeros((ROWS, cells), F32)


def arrived(low_ref, high_ref, from_right_ref, from_left_ref, iface):
    own = high_ref[:iface] - from_right_ref[:iface]
    previous = from_left_ref[:iface] - low_ref[:iface]
    return own, previous


def second_kernel(
    low_ref, high_ref, from_right_ref, from_left_ref, r_ref, u_ref, selector_ref, swap_ref, stiffness_ref,
    low_out, high_out, w_out, stiff_ref,
):
    iface = r_ref.shape[0]
    w, w_previous = arrived(low_ref, high_ref, from_right_ref, from_left_ref, iface)
    w_out[0] = w
    w_out[1] = w_previous
    dots = dot_rows(r_ref[...], u_ref[...], w)
    low_out[iface:] = dots
    high_out[iface:] = dots
    stiffen(w, w_previous, selector_ref, swap_ref, stiffness_ref, stiff_ref, low_out, high_out)


def update(first, last, refs, m, n, n_previous, totals):
    scalars_in, x_in, r_in, u_in, w_in, p_in, s_in, q_in, z_in = refs[:9]
    scalars_out, x_out, r_out, u_out, w_out, p_out, s_out, q_out, z_out = refs[9:]
    alpha, beta, norm, curvature = step_sizes(totals, None if first else scalars_in[...])
    cells = m.shape[1]
    scalars_out[...] = jnp.concatenate(
        [
            jnp.broadcast_to(norm, (1, cells)),
            jnp.broadcast_to(curvature, (1, cells)),
            jnp.zeros((ROWS - 2, cells), F32),
        ],
        axis=0,
    )

    def turned(fresh, kept):
        return fresh if first else fresh + beta * kept[...]

    u, w = u_in[...], w_in[0]
    p = turned(u, p_in)
    s = turned(w, s_in)
    q = turned(m, q_in)
    z = turned(n, None if first else z_in.at[0])
    p_out[...] = p
    s_out[...] = s
    x_out[...] = alpha * p if first else x_in[...] + alpha * p
    r = r_in[...] - alpha * s
    u = u - alpha * q
    w = w - alpha * z
    r_out[...] = r
    u_out[...] = u
    w_out[0] = w
    previous = None
    if not last:
        z_previous = turned(n_previous, None if first else z_in.at[1])
        previous = w_in[1] - alpha * z_previous
        q_out[...] = q
        z_out[0] = z
        z_out[1] = z_previous
        w_out[1] = previous
    return dot_rows(r, u, w, s, p), w, previous


def middle_kernel(first, last, *refs):
    (low_ref, high_ref, from_right_ref, from_left_ref, dots_ref, dots_other_ref, m_ref) = refs[:7]
    (selector_ref, swap_ref, stiffness_ref) = refs[7:10]
    ins = list(refs[10:19])
    outs = list(refs[19:28])
    m = m_ref[...]
    iface = m.shape[0]
    n, n_previous = arrived(low_ref, high_ref, from_right_ref, from_left_ref, iface)
    dots, w, previous = update(
        first, last, ins + outs, m, n, n_previous, dots_ref[...] + dots_other_ref[...]
    )
    if last:
        dots_out = refs[28]
        dots_out[...] = jnp.broadcast_to(dots[None], dots_out.shape)
    else:
        low_out, high_out, stiff_ref = refs[28:31]
        low_out[iface:] = dots
        high_out[iface:] = dots
        stiffen(w, previous, selector_ref, swap_ref, stiffness_ref, stiff_ref, low_out, high_out)


def corner_kernel(
    ranks, low_ref, high_ref, from_right_ref, from_left_ref, place_ref, selector_ref, operators_ref, table_ref,
    m_out, gap_out, *rest,
):
    outs, sums_ref = rest[:ranks], rest[ranks]
    iface, cells = m_out.shape
    own, previous = arrived(low_ref, high_ref, from_right_ref, from_left_ref, iface)
    m_out[...] = own
    odd = place_ref[0] % 2
    other = jnp.where(odd == 1, from_left_ref[iface:], from_right_ref[iface:])
    dots = high_ref[iface:] + other
    gap = spread_of(own, previous, selector_ref[...])
    gap_out[...] = gap
    parts = []
    for corner in range(CORNERS_SUB):
        at = slice(corner * CORNER_DOF, (corner + 1) * CORNER_DOF)
        part = jnp.sum(operators_ref[at].astype(F32) * gap[None], axis=1)
        parts.append(jnp.concatenate([part, jnp.zeros((ROWS - CORNER_DOF, cells), F32)], axis=0))
    sums_ref[...] = exact_dot(jnp.concatenate(parts, axis=1), table_ref[...], NT)
    owned = sums_ref.shape[1] // ranks
    pad = jnp.zeros((1, owned - 2 * cells), F32) if owned > 2 * cells else None
    tail = []
    for row in range(0, ROWS - CORNER_DOF):
        lanes = [dots[2 * row : 2 * row + 1], dots[2 * row + 1 : 2 * row + 2]]
        if pad is not None:
            lanes.append(pad)
        tail.append(jnp.concatenate(lanes, axis=1))
    tail = jnp.concatenate(tail, axis=0)
    for distance in range(ranks):
        rank = (place_ref[1] + distance) % ranks
        piece = sums_ref[:, pl.ds(pl.multiple_of(rank * owned, 128), owned)]
        outs[distance][...] = jnp.concatenate([piece[:CORNER_DOF], tail], axis=0)


def local_kernel(gap_ref, inverse_ref, local_ref):
    apply_blocks([inverse_ref], [gap_ref[...]], local_ref)


def coarse_kernel(ranks, place_ref, coarse_ref, *rest):
    pieces, (solved_ref, dots_ref, sums_ref) = rest[:ranks], rest[ranks:]
    cells = dots_ref.shape[1]
    for distance in range(ranks):
        rank = (place_ref[1] + ranks - distance) % ranks
        sums_ref[rank] = pieces[distance][...]
    total = sums_ref[0]
    for rank in range(1, ranks):
        total = total + sums_ref[rank]
    tail = total[CORNER_DOF:]
    dots_ref[...] = jnp.concatenate(
        [
            tail[0:1, :cells],
            tail[0:1, cells : 2 * cells],
            tail[1:2, :cells],
            tail[1:2, cells : 2 * cells],
            jnp.zeros((ROWS - 4, cells), F32),
        ],
        axis=0,
    )
    blocks, order = coarse_ref.shape[0], coarse_ref.shape[1]
    width = order // CORNER_DOF
    columns = []
    for block in range(blocks):
        lanes = slice(block * width, (block + 1) * width)
        row = jnp.concatenate([total[j : j + 1, lanes] for j in range(CORNER_DOF)], axis=1)
        parts = pieces_of(row) + [jnp.zeros((ROWS - 3, order), F32)]
        stacked = jnp.concatenate(parts, axis=0).astype(BF16)
        product = lax.dot_general(stacked, coarse_ref[block], NT, preferred_element_type=F32)
        result = product[0:1] + product[1:2] + product[2:3]
        rows = [result[:, j * width : (j + 1) * width] for j in range(CORNER_DOF)]
        columns.append(jnp.concatenate(rows, axis=0))
    solved = jnp.concatenate(columns, axis=1)
    solved_ref[...] = jnp.concatenate(
        [solved, jnp.zeros((ROWS - CORNER_DOF, solved.shape[1]), F32)], axis=0
    )


def lift_kernel(ranks, place_ref, local_ref, operators_ref, table_ref, selector_ref, dots_ref, other_ref, *rest):
    pieces, (low_ref, high_ref, dots_out, values_ref) = rest[:ranks], rest[ranks:]
    cells = local_ref.shape[1]
    owned = values_ref.shape[1] // ranks
    dots_out[...] = dots_ref[...] + other_ref[...]
    for distance in range(ranks):
        rank = (place_ref[1] + ranks - distance) % ranks
        values_ref[:, pl.ds(pl.multiple_of(rank * owned, 128), owned)] = pieces[distance][...]
    picked = exact_dot(values_ref[...], table_ref[...], NN)
    lifted = local_ref[...]
    for corner in range(CORNERS_SUB):
        lanes = slice(corner * cells, (corner + 1) * cells)
        for dof in range(CORNER_DOF):
            operator = operators_ref[corner * CORNER_DOF + dof].astype(F32)
            lifted = lifted + operator * picked[dof : dof + 1, lanes]
    collect_to(lifted, selector_ref[...], low_ref, high_ref)


def final_kernel(dots_ref, scalars_ref, x_ref, r_ref, u_ref, w_ref, p_ref, s_ref, x_out, r_out):
    totals = jnp.sum(dots_ref[...], axis=0)
    alpha, beta, _, _ = step_sizes(totals, scalars_ref[...])
    x_out[...] = x_ref[...] + alpha * (u_ref[...] + beta * p_ref[...])
    r_out[...] = r_ref[...] - alpha * (w_ref[0] + beta * s_ref[...])


def shifted(block, distance):
    count = lax.axis_size("sub")
    route = [(i, i + distance) for i in range(count) if 0 <= i + distance < count]
    return lax.ppermute(block, "sub", route)


def swapped(block, bit):
    return lax.ppermute(block, "sub", [(i, i ^ bit) for i in range(lax.axis_size("sub"))])


def rotated(block, distance):
    count = lax.axis_size("grp")
    return lax.ppermute(block, "grp", [(i, (i + distance) % count) for i in range(count)])


def shape(*dims, dtype=F32):
    return jax.ShapeDtypeStruct(dims, dtype)


def call(kernel, out_shape, in_smem=(), count=0, scratch=(), flops=0, moved=0, name=None):
    specs = [
        pl.BlockSpec(memory_space=pltpu.SMEM if i in in_smem else pltpu.VMEM) for i in range(count)
    ]
    out_specs = jax.tree.map(lambda _: pl.BlockSpec(memory_space=pltpu.VMEM), out_shape)
    return pl.pallas_call(
        kernel,
        out_shape=out_shape,
        in_specs=specs,
        out_specs=out_specs,
        scratch_shapes=list(scratch),
        compiler_params=pltpu.CompilerParams(vmem_limit_bytes=24 * 1024 * 1024),
        cost_estimate=pl.CostEstimate(flops=flops, bytes_accessed=moved, transcendentals=0),
        name=name,
    )


def on_device(
    gap_data,
    local_inverse,
    stiffness,
    stiff_column,
    neighbour,
    corner_ops,
    corner_index,
    coarse_inverse,
):
    iface, _, cells = gap_data.shape
    ranks = lax.axis_size("grp")
    sub_count = lax.axis_size("sub")
    start = lax.axis_index("sub") * cells
    place = jnp.stack([lax.axis_index("sub"), lax.axis_index("grp")]).astype(jnp.int32)
    right_side = gap_data[:, 0, :]
    inverse = local_inverse[:, :, 0, :]
    stiff = stiffness[:, :, :, 0, :]
    operators = corner_ops[:, :, 0, :]
    blocks_own, order = coarse_inverse.shape[:2]
    owned = blocks_own * (order // CORNER_DOF)
    group = owned * ranks
    slots = jnp.where(neighbour < 0, -1, neighbour - (start - cells))
    column = stiff_column - start
    corners = corner_index.reshape(1, CORNERS_SUB * cells)

    selector, swap, table = call(
        table_kernel,
        (
            shape(2 * cells, cells, dtype=BF16),
            shape(cells, cells, dtype=BF16),
            shape(group, CORNERS_SUB * cells, dtype=BF16),
        ),
        count=3,
        name="tables",
    )(slots, column, corners)

    field = shape(iface, cells)
    pair = shape(2, iface, cells)
    message = shape(iface + ROWS, cells)
    rows = shape(ROWS, cells)
    piece = shape(ROWS, owned)
    stiff_scratch = [pltpu.VMEM((iface, cells), F32)]
    stiff_cost = dict(flops=4 * iface * iface * cells, moved=4 * iface * iface * cells)

    def apply_operator(low, high):
        from_right = shifted(low, -1)
        from_left = shifted(high, 1)
        m, gap, *parts = call(
            lambda *refs: corner_kernel(ranks, *refs),
            (field, field) + (piece,) * ranks,
            in_smem=(4,),
            count=8,
            scratch=[pltpu.VMEM((ROWS, group), F32)],
            flops=2 * 24 * iface * cells,
            moved=2 * 24 * iface * cells + group * CORNERS_SUB * cells * 2,
            name="corners",
        )(low, high, from_right, from_left, place, selector, operators, table)
        arrivals = [parts[0]] + [rotated(parts[d], d) for d in range(1, ranks)]
        local = call(
            local_kernel,
            field,
            count=2,
            flops=2 * iface * iface * cells,
            moved=2 * iface * iface * cells,
            name="local",
        )(gap, inverse)
        solved, dots = call(
            lambda *refs: coarse_kernel(ranks, *refs),
            (piece, rows),
            in_smem=(0,),
            count=2 + ranks,
            scratch=[pltpu.VMEM((ranks, ROWS, owned), F32)],
            flops=2 * blocks_own * order * order,
            moved=2 * blocks_own * order * order,
            name="coarse",
        )(place, coarse_inverse, *arrivals)
        values = [solved] + [rotated(solved, d) for d in range(1, ranks)]
        other = swapped(dots, 2)
        low, high, dots = call(
            lambda *refs: lift_kernel(ranks, *refs),
            (field, field, rows),
            in_smem=(0,),
            count=7 + ranks,
            scratch=[pltpu.VMEM((ROWS, group), F32)],
            flops=2 * 24 * iface * cells,
            moved=2 * 24 * iface * cells + group * CORNERS_SUB * cells * 2,
            name="lift",
        )(place, local, operators, table, selector, dots, other, *values)
        return m, low, high, dots

    previous = shifted(right_side, 1)
    low, high = call(
        first_kernel, (message, message), count=5, scratch=stiff_scratch, name="first", **stiff_cost
    )(right_side, previous, selector, swap, stiff)
    u, low, high, dots = apply_operator(low, high)
    r = right_side
    from_right, from_left = shifted(low, -1), shifted(high, 1)
    low, high, w = call(
        second_kernel, (message, message, pair), count=9, scratch=stiff_scratch, name="second", **stiff_cost
    )(low, high, from_right, from_left, r, u, selector, swap, stiff)

    scalars, x, p, s, q, z = [jnp.zeros((ROWS, cells), F32)] + [r] * 4 + [w]
    for step in range(ITERS - 1):
        first, last = step == 0, step == ITERS - 2
        m, low, high, dots = apply_operator(low, high)
        from_right, from_left, other = shifted(low, -1), shifted(high, 1), swapped(dots, 4)
        bit = 8
        while bit < sub_count:
            dots = dots + other
            other = swapped(dots, bit)
            bit *= 2
        outs = (rows, field, field, field, pair, field, field, field, pair)
        if last:
            count = sub_count * ranks
            outs += (shape(count, ROWS, cells),)
        else:
            outs += (message, message)
        result = call(
            lambda *refs, first=first, last=last: middle_kernel(first, last, *refs),
            outs,
            count=19,
            scratch=() if last else stiff_scratch,
            name="last" if last else "middle",
            **({} if last else stiff_cost),
        )(
            low, high, from_right, from_left, dots, other, m, selector, swap, stiff,
            scalars, x, r, u, w, p, s, q, z,
        )
        scalars, x, r, u, w, p, s, q, z = result[:9]
        if not last:
            low, high = result[9:]
    everyone = lax.all_to_all(result[9], ("sub", "grp"), 0, 0, tiled=True)
    x, r = call(final_kernel, (field, field), count=8, name="final")(
        everyone, scalars, x, r, u, w, p, s
    )
    return (x[:, None, :], r[:, None, :])


def solution(mesh):
    in_specs = (
        P(None, "grp", "sub"),
        P(None, None, "grp", "sub"),
        P(None, None, None, "grp", "sub"),
        P("grp", "sub"),
        P("grp", "sub"),
        P(None, None, "grp", "sub"),
        P(None, "grp", "sub"),
        P("grp", None, "sub"),
    )
    out_specs = (P(None, "grp", "sub"), P(None, "grp", "sub"))
    return jax.shard_map(
        on_device, mesh=mesh, in_specs=in_specs, out_specs=out_specs, check_vma=False
    )
```

```python
import jax
import jax.numpy as jnp
from jax import lax
from jax.experimental import pallas as pl
from jax.experimental.pallas import tpu as pltpu
from jax.sharding import PartitionSpec as P

CORNER_DOF = 6
CORNERS_SUB = 4
ITERS = 5
ROWS = 8
NN = (((1,), (0,)), ((), ()))
NT = (((1,), (1,)), ((), ()))
F32 = jnp.float32
BF16 = jnp.bfloat16


def pieces_of(value):
    high = value.astype(BF16).astype(F32)
    rest = value - high
    middle = rest.astype(BF16).astype(F32)
    return [high, middle, rest - middle]


def exact_dot(value, table, dims):
    rows = value.shape[0]
    stacked = jnp.concatenate(pieces_of(value), axis=0).astype(BF16)
    product = lax.dot_general(stacked, table, dims, preferred_element_type=F32)
    return product[:rows] + product[rows : 2 * rows] + product[2 * rows :]


def lane_total(rows):
    return jnp.sum(rows, axis=1, keepdims=True)


def dot_rows(r, u, w, s=None, p=None):
    rows = [jnp.sum(r * u, axis=0, keepdims=True), jnp.sum(u * w, axis=0, keepdims=True)]
    if s is None:
        rows.append(jnp.zeros((ROWS - 2, r.shape[1]), F32))
    else:
        rows.append(jnp.sum(u * s, axis=0, keepdims=True))
        rows.append(jnp.sum(p * w, axis=0, keepdims=True))
        rows.append(jnp.zeros((ROWS - 4, r.shape[1]), F32))
    return jnp.concatenate(rows, axis=0)


def step_sizes(totals, before):
    sums = lane_total(totals)
    norm, curvature = sums[0:1], sums[1:2]
    if before is None:
        beta = None
    else:
        beta = norm / before[0:1, 0:1]
        curvature = curvature + beta * (sums[2:3] + sums[3:4]) + beta * beta * before[1:2, 0:1]
    return norm / curvature, beta, norm, curvature


def collect_to(odd, vector, selector, near_ref, far_ref):
    iface, cells = vector.shape
    moved = exact_dot(vector, selector, NT)
    low = moved[:, :cells]
    high = vector - moved[:, cells:]
    near_ref[:iface] = jnp.where(odd, low, high)
    far_ref[:iface] = jnp.where(odd, high, low)


def spread_of(own, previous, selector):
    return own - exact_dot(jnp.concatenate([previous, own], axis=1), selector, NN)


def apply_blocks(blocks, vectors, out_ref):
    def step(index, carry):
        at = pl.ds(index * ROWS, ROWS)
        total = None
        for block, vector in zip(blocks, vectors):
            term = block[at].astype(F32) * vector[None]
            total = term if total is None else total + term
        out_ref[pl.ds(pl.multiple_of(index * ROWS, ROWS), ROWS)] = jnp.sum(total, axis=1)
        return carry

    lax.fori_loop(0, out_ref.shape[0] // ROWS, step, 0)


def table_kernel(slots_ref, column_ref, corner_ref, selector_ref, swap_ref, table_ref):
    def one_hot(row, count):
        places = lax.broadcasted_iota(jnp.int32, (count, row.shape[1]), 0)
        return jnp.where(places == row, 1.0, 0.0).astype(BF16)

    selector_ref[...] = one_hot(slots_ref[...], selector_ref.shape[0])
    swap_ref[...] = one_hot(column_ref[...], swap_ref.shape[0])
    chunk = 128

    def step(index, carry):
        row = corner_ref[...] - index * chunk
        table_ref[pl.ds(pl.multiple_of(index * chunk, chunk), chunk)] = one_hot(row, chunk)
        return carry

    lax.fori_loop(0, table_ref.shape[0] // chunk, step, 0)


def stiffen(odd, own, previous, selector_ref, swap_ref, stiffness_ref, stiff_ref, near_ref, far_ref):
    gap = spread_of(own, previous, selector_ref[...])
    taken = exact_dot(gap, swap_ref[...], NN)
    apply_blocks([stiffness_ref.at[0], stiffness_ref.at[1]], [gap, taken], stiff_ref)
    collect_to(odd, stiff_ref[...], selector_ref[...], near_ref, far_ref)


def first_kernel(
    place_ref, own_ref, previous_ref, selector_ref, swap_ref, stiffness_ref, near_ref, far_ref, stiff_ref
):
    iface, cells = own_ref.shape
    odd = place_ref[0] % 2 == 1
    stiffen(
        odd, own_ref[...], previous_ref[...], selector_ref, swap_ref, stiffness_ref, stiff_ref, near_ref, far_ref
    )
    near_ref[iface:] = jnp.zeros((ROWS, cells), F32)


def arrived(odd, near_ref, far_ref, from_near_ref, from_far_ref, iface):
    near, far = near_ref[:iface], far_ref[...]
    from_near, from_far = from_near_ref[:iface], from_far_ref[...]
    own = jnp.where(odd, far - from_far, near - from_near)
    previous = jnp.where(odd, from_near - near, from_far - far)
    return own, previous


def second_kernel(
    place_ref, near_ref, far_ref, from_near_ref, from_far_ref, r_ref, u_ref, selector_ref, swap_ref, stiffness_ref,
    near_out, far_out, w_out, stiff_ref,
):
    iface = r_ref.shape[0]
    odd = place_ref[0] % 2 == 1
    w, w_previous = arrived(odd, near_ref, far_ref, from_near_ref, from_far_ref, iface)
    w_out[0] = w
    w_out[1] = w_previous
    dots = dot_rows(r_ref[...], u_ref[...], w)
    near_out[iface:] = dots
    stiffen(odd, w, w_previous, selector_ref, swap_ref, stiffness_ref, stiff_ref, near_out, far_out)


def update(first, last, refs, m, n, n_previous, totals):
    scalars_in, x_in, r_in, u_in, w_in, p_in, s_in, q_in, z_in = refs[:9]
    scalars_out, x_out, r_out, u_out, w_out, p_out, s_out, q_out, z_out = refs[9:]
    alpha, beta, norm, curvature = step_sizes(totals, None if first else scalars_in[...])
    cells = m.shape[1]
    scalars_out[...] = jnp.concatenate(
        [
            jnp.broadcast_to(norm, (1, cells)),
            jnp.broadcast_to(curvature, (1, cells)),
            jnp.zeros((ROWS - 2, cells), F32),
        ],
        axis=0,
    )

    def turned(fresh, kept):
        return fresh if first else fresh + beta * kept[...]

    u, w = u_in[...], w_in[0]
    p = turned(u, p_in)
    s = turned(w, s_in)
    q = turned(m, q_in)
    z = turned(n, None if first else z_in.at[0])
    p_out[...] = p
    s_out[...] = s
    x_out[...] = alpha * p if first else x_in[...] + alpha * p
    r = r_in[...] - alpha * s
    u = u - alpha * q
    w = w - alpha * z
    r_out[...] = r
    u_out[...] = u
    w_out[0] = w
    previous = None
    if not last:
        z_previous = turned(n_previous, None if first else z_in.at[1])
        previous = w_in[1] - alpha * z_previous
        q_out[...] = q
        z_out[0] = z
        z_out[1] = z_previous
        w_out[1] = previous
    return dot_rows(r, u, w, s, p), w, previous


def middle_kernel(first, last, *refs):
    (place_ref, near_ref, far_ref, from_near_ref, from_far_ref, dots_ref, dots_other_ref, m_ref) = refs[:8]
    (selector_ref, swap_ref, stiffness_ref) = refs[8:11]
    ins = list(refs[11:20])
    outs = list(refs[20:29])
    m = m_ref[...]
    iface = m.shape[0]
    odd = place_ref[0] % 2 == 1
    n, n_previous = arrived(odd, near_ref, far_ref, from_near_ref, from_far_ref, iface)
    dots, w, previous = update(
        first, last, ins + outs, m, n, n_previous, dots_ref[...] + dots_other_ref[...]
    )
    if last:
        dots_out = refs[29]
        dots_out[...] = jnp.broadcast_to(dots[None], dots_out.shape)
    else:
        near_out, far_out, stiff_ref = refs[29:32]
        near_out[iface:] = dots
        stiffen(odd, w, previous, selector_ref, swap_ref, stiffness_ref, stiff_ref, near_out, far_out)


def corner_kernel(
    ranks, place_ref, near_ref, far_ref, from_near_ref, from_far_ref, selector_ref, operators_ref, table_ref,
    m_out, gap_out, *rest,
):
    outs, sums_ref = rest[:ranks], rest[ranks]
    iface, cells = m_out.shape
    odd = place_ref[0] % 2 == 1
    own, previous = arrived(odd, near_ref, far_ref, from_near_ref, from_far_ref, iface)
    m_out[...] = own
    dots = near_ref[iface:] + from_near_ref[iface:]
    gap = spread_of(own, previous, selector_ref[...])
    gap_out[...] = gap
    parts = []
    for corner in range(CORNERS_SUB):
        at = slice(corner * CORNER_DOF, (corner + 1) * CORNER_DOF)
        part = jnp.sum(operators_ref[at].astype(F32) * gap[None], axis=1)
        parts.append(jnp.concatenate([part, jnp.zeros((ROWS - CORNER_DOF, cells), F32)], axis=0))
    sums_ref[...] = exact_dot(jnp.concatenate(parts, axis=1), table_ref[...], NT)
    owned = sums_ref.shape[1] // ranks
    pad = jnp.zeros((1, owned - 2 * cells), F32) if owned > 2 * cells else None
    tail = []
    for row in range(0, ROWS - CORNER_DOF):
        lanes = [dots[2 * row : 2 * row + 1], dots[2 * row + 1 : 2 * row + 2]]
        if pad is not None:
            lanes.append(pad)
        tail.append(jnp.concatenate(lanes, axis=1))
    tail = jnp.concatenate(tail, axis=0)
    for distance in range(ranks):
        rank = place_ref[1] ^ distance
        piece = sums_ref[:, pl.ds(pl.multiple_of(rank * owned, 128), owned)]
        outs[distance][...] = jnp.concatenate([piece[:CORNER_DOF], tail], axis=0)


def local_kernel(gap_ref, inverse_ref, local_ref):
    apply_blocks([inverse_ref], [gap_ref[...]], local_ref)


def coarse_kernel(ranks, place_ref, coarse_ref, *rest):
    pieces, (solved_ref, dots_ref, sums_ref) = rest[:ranks], rest[ranks:]
    cells = dots_ref.shape[1]
    for distance in range(ranks):
        rank = place_ref[1] ^ distance
        sums_ref[rank] = pieces[distance][...]
    total = sums_ref[0]
    for rank in range(1, ranks):
        total = total + sums_ref[rank]
    tail = total[CORNER_DOF:]
    dots_ref[...] = jnp.concatenate(
        [
            tail[0:1, :cells],
            tail[0:1, cells : 2 * cells],
            tail[1:2, :cells],
            tail[1:2, cells : 2 * cells],
            jnp.zeros((ROWS - 4, cells), F32),
        ],
        axis=0,
    )
    blocks, order = coarse_ref.shape[0], coarse_ref.shape[1]
    width = order // CORNER_DOF
    columns = []
    for block in range(blocks):
        lanes = slice(block * width, (block + 1) * width)
        row = jnp.concatenate([total[j : j + 1, lanes] for j in range(CORNER_DOF)], axis=1)
        parts = pieces_of(row) + [jnp.zeros((ROWS - 3, order), F32)]
        stacked = jnp.concatenate(parts, axis=0).astype(BF16)
        product = lax.dot_general(stacked, coarse_ref[block], NT, preferred_element_type=F32)
        result = product[0:1] + product[1:2] + product[2:3]
        rows = [result[:, j * width : (j + 1) * width] for j in range(CORNER_DOF)]
        columns.append(jnp.concatenate(rows, axis=0))
    solved = jnp.concatenate(columns, axis=1)
    solved_ref[...] = jnp.concatenate(
        [solved, jnp.zeros((ROWS - CORNER_DOF, solved.shape[1]), F32)], axis=0
    )


def lift_kernel(ranks, place_ref, local_ref, operators_ref, table_ref, selector_ref, dots_ref, other_ref, *rest):
    pieces, (near_ref, far_ref, dots_out, values_ref) = rest[:ranks], rest[ranks:]
    cells = local_ref.shape[1]
    owned = values_ref.shape[1] // ranks
    dots_out[...] = dots_ref[...] + other_ref[...]
    for distance in range(ranks):
        rank = place_ref[1] ^ distance
        values_ref[:, pl.ds(pl.multiple_of(rank * owned, 128), owned)] = pieces[distance][...]
    picked = exact_dot(values_ref[...], table_ref[...], NN)
    lifted = local_ref[...]
    for corner in range(CORNERS_SUB):
        lanes = slice(corner * cells, (corner + 1) * cells)
        for dof in range(CORNER_DOF):
            operator = operators_ref[corner * CORNER_DOF + dof].astype(F32)
            lifted = lifted + operator * picked[dof : dof + 1, lanes]
    collect_to(place_ref[0] % 2 == 1, lifted, selector_ref[...], near_ref, far_ref)


def final_kernel(dots_ref, scalars_ref, x_ref, r_ref, u_ref, w_ref, p_ref, s_ref, x_out, r_out):
    totals = jnp.sum(dots_ref[...], axis=0)
    alpha, beta, _, _ = step_sizes(totals, scalars_ref[...])
    x_out[...] = x_ref[...] + alpha * (u_ref[...] + beta * p_ref[...])
    r_out[...] = r_ref[...] - alpha * (w_ref[0] + beta * s_ref[...])


def shifted(block, distance):
    count = lax.axis_size("sub")
    route = [(i, i + distance) for i in range(count) if 0 <= i + distance < count]
    return lax.ppermute(block, "sub", route)


def swapped(block, bit):
    return lax.ppermute(block, "sub", [(i, i ^ bit) for i in range(lax.axis_size("sub"))])


def swapped_far(block):
    inner = range(1, lax.axis_size("sub") - 1)
    return lax.ppermute(block, "sub", [(i, i + 1 if i % 2 else i - 1) for i in inner])


def exchanged(block, distance):
    return lax.ppermute(block, "grp", [(i, i ^ distance) for i in range(lax.axis_size("grp"))])


def shape(*dims, dtype=F32):
    return jax.ShapeDtypeStruct(dims, dtype)


def call(kernel, out_shape, in_smem=(), count=0, scratch=(), flops=0, moved=0, name=None):
    specs = [
        pl.BlockSpec(memory_space=pltpu.SMEM if i in in_smem else pltpu.VMEM) for i in range(count)
    ]
    out_specs = jax.tree.map(lambda _: pl.BlockSpec(memory_space=pltpu.VMEM), out_shape)
    return pl.pallas_call(
        kernel,
        out_shape=out_shape,
        in_specs=specs,
        out_specs=out_specs,
        scratch_shapes=list(scratch),
        compiler_params=pltpu.CompilerParams(vmem_limit_bytes=24 * 1024 * 1024),
        cost_estimate=pl.CostEstimate(flops=flops, bytes_accessed=moved, transcendentals=0),
        name=name,
    )


def on_device(
    gap_data,
    local_inverse,
    stiffness,
    stiff_column,
    neighbour,
    corner_ops,
    corner_index,
    coarse_inverse,
):
    iface, _, cells = gap_data.shape
    ranks = lax.axis_size("grp")
    sub_count = lax.axis_size("sub")
    start = lax.axis_index("sub") * cells
    place = jnp.stack([lax.axis_index("sub"), lax.axis_index("grp")]).astype(jnp.int32)
    right_side = gap_data[:, 0, :]
    inverse = local_inverse[:, :, 0, :]
    stiff = stiffness[:, :, :, 0, :]
    operators = corner_ops[:, :, 0, :]
    blocks_own, order = coarse_inverse.shape[:2]
    owned = blocks_own * (order // CORNER_DOF)
    group = owned * ranks
    slots = jnp.where(neighbour < 0, -1, neighbour - (start - cells))
    column = stiff_column - start
    corners = corner_index.reshape(1, CORNERS_SUB * cells)

    selector, swap, table = call(
        table_kernel,
        (
            shape(2 * cells, cells, dtype=BF16),
            shape(cells, cells, dtype=BF16),
            shape(group, CORNERS_SUB * cells, dtype=BF16),
        ),
        count=3,
        name="tables",
    )(slots, column, corners)

    field = shape(iface, cells)
    pair = shape(2, iface, cells)
    message = shape(iface + ROWS, cells)
    rows = shape(ROWS, cells)
    piece = shape(ROWS, owned)
    stiff_scratch = [pltpu.VMEM((iface, cells), F32)]
    stiff_cost = dict(flops=4 * iface * iface * cells, moved=4 * iface * iface * cells)

    def apply_operator(near, far):
        from_far, from_near = swapped_far(far), swapped(near, 1)
        m, gap, *parts = call(
            lambda *refs: corner_kernel(ranks, *refs),
            (field, field) + (piece,) * ranks,
            in_smem=(0,),
            count=8,
            scratch=[pltpu.VMEM((ROWS, group), F32)],
            flops=2 * 24 * iface * cells,
            moved=2 * 24 * iface * cells + group * CORNERS_SUB * cells * 2,
            name="corners",
        )(place, near, far, from_near, from_far, selector, operators, table)
        arrivals = [parts[0]] + [exchanged(parts[d], d) for d in range(1, ranks)]
        local = call(
            local_kernel,
            field,
            count=2,
            flops=2 * iface * iface * cells,
            moved=2 * iface * iface * cells,
            name="local",
        )(gap, inverse)
        solved, dots = call(
            lambda *refs: coarse_kernel(ranks, *refs),
            (piece, rows),
            in_smem=(0,),
            count=2 + ranks,
            scratch=[pltpu.VMEM((ranks, ROWS, owned), F32)],
            flops=2 * blocks_own * order * order,
            moved=2 * blocks_own * order * order,
            name="coarse",
        )(place, coarse_inverse, *arrivals)
        values = [solved] + [exchanged(solved, d) for d in range(1, ranks)]
        other = swapped(dots, 2)
        near, far, dots = call(
            lambda *refs: lift_kernel(ranks, *refs),
            (field, field, rows),
            in_smem=(0,),
            count=7 + ranks,
            scratch=[pltpu.VMEM((ROWS, group), F32)],
            flops=2 * 24 * iface * cells,
            moved=2 * 24 * iface * cells + group * CORNERS_SUB * cells * 2,
            name="lift",
        )(place, local, operators, table, selector, dots, other, *values)
        return m, near, far, dots

    previous = shifted(right_side, 1)
    near, far = call(
        first_kernel, (message, field), in_smem=(0,), count=6, scratch=stiff_scratch, name="first", **stiff_cost
    )(place, right_side, previous, selector, swap, stiff)
    u, near, far, dots = apply_operator(near, far)
    r = right_side
    from_far, from_near = swapped_far(far), swapped(near, 1)
    near, far, w = call(
        second_kernel,
        (message, field, pair),
        in_smem=(0,),
        count=10,
        scratch=stiff_scratch,
        name="second",
        **stiff_cost,
    )(place, near, far, from_near, from_far, r, u, selector, swap, stiff)

    scalars, x, p, s, q, z = [jnp.zeros((ROWS, cells), F32)] + [r] * 4 + [w]
    for step in range(ITERS - 1):
        first, last = step == 0, step == ITERS - 2
        m, near, far, dots = apply_operator(near, far)
        from_far, from_near, other = swapped_far(far), swapped(near, 1), swapped(dots, 4)
        bit = 8
        while bit < sub_count:
            dots = dots + other
            other = swapped(dots, bit)
            bit *= 2
        outs = (rows, field, field, field, pair, field, field, field, pair)
        if last:
            count = sub_count * ranks
            outs += (shape(count, ROWS, cells),)
        else:
            outs += (message, field)
        result = call(
            lambda *refs, first=first, last=last: middle_kernel(first, last, *refs),
            outs,
            in_smem=(0,),
            count=20,
            scratch=() if last else stiff_scratch,
            name="last" if last else "middle",
            **({} if last else stiff_cost),
        )(
            place, near, far, from_near, from_far, dots, other, m, selector, swap, stiff,
            scalars, x, r, u, w, p, s, q, z,
        )
        scalars, x, r, u, w, p, s, q, z = result[:9]
        if not last:
            near, far = result[9:]
    everyone = lax.all_to_all(result[9], ("sub", "grp"), 0, 0, tiled=True)
    x, r = call(final_kernel, (field, field), count=8, name="final")(
        everyone, scalars, x, r, u, w, p, s
    )
    return (x[:, None, :], r[:, None, :])


def solution(mesh):
    in_specs = (
        P(None, "grp", "sub"),
        P(None, None, "grp", "sub"),
        P(None, None, None, "grp", "sub"),
        P("grp", "sub"),
        P("grp", "sub"),
        P(None, None, "grp", "sub"),
        P(None, "grp", "sub"),
        P("grp", None, "sub"),
    )
    out_specs = (P(None, "grp", "sub"), P(None, "grp", "sub"))
    return jax.shard_map(
        on_device, mesh=mesh, in_specs=in_specs, out_specs=out_specs, check_vma=False
    )
```

```python
import jax
import jax.numpy as jnp
from jax import lax
from jax.experimental import pallas as pl
from jax.experimental.pallas import tpu as pltpu
from jax.sharding import PartitionSpec as P

CORNER_DOF = 6
CORNERS_SUB = 4
ITERS = 5
ROWS = 8
LANES = 128
NN = (((1,), (0,)), ((), ()))
NT = (((1,), (1,)), ((), ()))
F32 = jnp.float32
BF16 = jnp.bfloat16


def pieces_of(value):
    high = value.astype(BF16).astype(F32)
    rest = value - high
    middle = rest.astype(BF16).astype(F32)
    return [high, middle, rest - middle]


def exact_dot(value, table, dims):
    rows = value.shape[0]
    stacked = jnp.concatenate(pieces_of(value), axis=0).astype(BF16)
    product = lax.dot_general(stacked, table, dims, preferred_element_type=F32)
    return product[:rows] + product[rows : 2 * rows] + product[2 * rows :]


def dot_lanes(*pairs):
    lane = lax.broadcasted_iota(jnp.int32, (1, LANES), 1)
    row = jnp.zeros((1, LANES), F32)
    for place, (first, second) in enumerate(pairs):
        total = jnp.sum(jnp.sum(first * second, axis=0, keepdims=True), axis=1, keepdims=True)
        row = jnp.where(lane == place, total, row)
    return row


def fill_lanes(out_ref, row):
    block = jnp.broadcast_to(row, (ROWS, LANES))
    for start in range(0, out_ref.shape[1], LANES):
        out_ref[:, start : start + LANES] = block


def step_sizes(sums, before):
    norm, curvature = sums[:, 0:1], sums[:, 1:2]
    if before is None:
        beta = None
    else:
        beta = norm / before[0:1, 0:1]
        curvature = curvature + beta * (sums[:, 2:3] + sums[:, 3:4]) + beta * beta * before[1:2, 0:1]
    return norm / curvature, beta, norm, curvature


def collect_to(odd, vector, selector, near_ref, far_ref):
    iface, cells = vector.shape
    moved = exact_dot(vector, selector, NT)
    low = moved[:, :cells]
    high = vector - moved[:, cells:]
    near_ref[...] = jnp.where(odd, low, high)
    far_ref[...] = jnp.where(odd, high, low)


def spread_of(own, previous, selector):
    return own - exact_dot(jnp.concatenate([previous, own], axis=1), selector, NN)


def apply_blocks(blocks, vectors, out_ref):
    def step(index, carry):
        at = pl.ds(index * ROWS, ROWS)
        total = None
        for block, vector in zip(blocks, vectors):
            term = block[at].astype(F32) * vector[None]
            total = term if total is None else total + term
        out_ref[pl.ds(pl.multiple_of(index * ROWS, ROWS), ROWS)] = jnp.sum(total, axis=1)
        return carry

    lax.fori_loop(0, out_ref.shape[0] // ROWS, step, 0)


def table_kernel(slots_ref, column_ref, corner_ref, selector_ref, swap_ref, table_ref):
    def one_hot(row, count):
        places = lax.broadcasted_iota(jnp.int32, (count, row.shape[1]), 0)
        return jnp.where(places == row, 1.0, 0.0).astype(BF16)

    selector_ref[...] = one_hot(slots_ref[...], selector_ref.shape[0])
    swap_ref[...] = one_hot(column_ref[...], swap_ref.shape[0])
    chunk = 128

    def step(index, carry):
        row = corner_ref[...] - index * chunk
        table_ref[pl.ds(pl.multiple_of(index * chunk, chunk), chunk)] = one_hot(row, chunk)
        return carry

    lax.fori_loop(0, table_ref.shape[0] // chunk, step, 0)


def stiffen(odd, own, previous, selector_ref, swap_ref, stiffness_ref, stiff_ref, near_ref, far_ref):
    gap = spread_of(own, previous, selector_ref[...])
    taken = exact_dot(gap, swap_ref[...], NN)
    apply_blocks([stiffness_ref.at[0], stiffness_ref.at[1]], [gap, taken], stiff_ref)
    collect_to(odd, stiff_ref[...], selector_ref[...], near_ref, far_ref)


def first_kernel(
    own_ref, previous_ref, selector_ref, swap_ref, stiffness_ref, near_ref, far_ref, stiff_ref
):
    odd = lax.axis_index("sub") % 2 == 1
    stiffen(
        odd, own_ref[...], previous_ref[...], selector_ref, swap_ref, stiffness_ref, stiff_ref, near_ref, far_ref
    )


def arrived(odd, near_ref, far_ref, from_near_ref, from_far_ref):
    near, far = near_ref[...], far_ref[...]
    from_near, from_far = from_near_ref[...], from_far_ref[...]
    own = jnp.where(odd, far - from_far, near - from_near)
    previous = jnp.where(odd, from_near - near, from_far - far)
    return own, previous


def second_kernel(
    near_ref, far_ref, from_near_ref, from_far_ref, r_ref, u_ref, selector_ref, swap_ref, stiffness_ref,
    w_out, dots_out, near_out, far_out, stiff_ref,
):
    odd = lax.axis_index("sub") % 2 == 1
    w, w_previous = arrived(odd, near_ref, far_ref, from_near_ref, from_far_ref)
    w_out[0] = w
    w_out[1] = w_previous
    r, u = r_ref[...], u_ref[...]
    fill_lanes(dots_out, dot_lanes((r, u), (u, w)))
    stiffen(odd, w, w_previous, selector_ref, swap_ref, stiffness_ref, stiff_ref, near_out, far_out)


def update(first, last, refs, m, n, n_previous, totals):
    scalars_in, x_in, r_in, u_in, w_in, p_in, s_in, q_in, z_in = refs[:9]
    scalars_out, x_out, r_out, u_out, w_out, p_out, s_out, q_out, z_out = refs[9:]
    alpha, beta, norm, curvature = step_sizes(totals, None if first else scalars_in[...])
    cells = m.shape[1]
    scalars_out[...] = jnp.concatenate(
        [
            jnp.broadcast_to(norm, (1, cells)),
            jnp.broadcast_to(curvature, (1, cells)),
            jnp.zeros((ROWS - 2, cells), F32),
        ],
        axis=0,
    )

    def turned(fresh, kept):
        return fresh if first else fresh + beta * kept[...]

    u, w = u_in[...], w_in[0]
    p = turned(u, p_in)
    s = turned(w, s_in)
    q = turned(m, q_in)
    z = turned(n, None if first else z_in.at[0])
    p_out[...] = p
    s_out[...] = s
    x_out[...] = alpha * p if first else x_in[...] + alpha * p
    r = r_in[...] - alpha * s
    u = u - alpha * q
    w = w - alpha * z
    r_out[...] = r
    u_out[...] = u
    w_out[0] = w
    previous = None
    if not last:
        z_previous = turned(n_previous, None if first else z_in.at[1])
        previous = w_in[1] - alpha * z_previous
        q_out[...] = q
        z_out[0] = z
        z_out[1] = z_previous
        w_out[1] = previous
    return dot_lanes((r, u), (u, w), (u, s), (p, w)), w, previous


def middle_kernel(first, last, *refs):
    (near_ref, far_ref, from_near_ref, from_far_ref, dots_ref, m_ref) = refs[:6]
    (selector_ref, swap_ref, stiffness_ref) = refs[6:9]
    ins = list(refs[9:18])
    outs = list(refs[18:27])
    m = m_ref[...]
    odd = lax.axis_index("sub") % 2 == 1
    n, n_previous = arrived(odd, near_ref, far_ref, from_near_ref, from_far_ref)
    dots, w, previous = update(
        first, last, ins + outs, m, n, n_previous, dots_ref[0:1]
    )
    dots_out = refs[27]
    if last:
        dots_out[...] = jnp.broadcast_to(dots, dots_out.shape)
    else:
        fill_lanes(dots_out, dots)
    if not last:
        near_out, far_out, stiff_ref = refs[28:31]
        stiffen(odd, w, previous, selector_ref, swap_ref, stiffness_ref, stiff_ref, near_out, far_out)


def corner_kernel(
    ranks, near_ref, far_ref, from_near_ref, from_far_ref, selector_ref, operators_ref, table_ref,
    m_out, gap_out, *rest,
):
    outs, sums_ref = rest[:ranks], rest[ranks]
    iface, cells = m_out.shape
    odd = lax.axis_index("sub") % 2 == 1
    own, previous = arrived(odd, near_ref, far_ref, from_near_ref, from_far_ref)
    m_out[...] = own
    gap = spread_of(own, previous, selector_ref[...])
    gap_out[...] = gap
    parts = []
    for corner in range(CORNERS_SUB):
        at = slice(corner * CORNER_DOF, (corner + 1) * CORNER_DOF)
        part = jnp.sum(operators_ref[at].astype(F32) * gap[None], axis=1)
        parts.append(jnp.concatenate([part, jnp.zeros((ROWS - CORNER_DOF, cells), F32)], axis=0))
    sums_ref[...] = exact_dot(jnp.concatenate(parts, axis=1), table_ref[...], NT)
    owned = sums_ref.shape[1] // ranks
    for distance in range(ranks):
        rank = lax.axis_index("grp") ^ distance
        outs[distance][...] = sums_ref[:, pl.ds(pl.multiple_of(rank * owned, LANES), owned)]


def local_kernel(gap_ref, inverse_ref, local_ref):
    apply_blocks([inverse_ref], [gap_ref[...]], local_ref)


def coarse_kernel(ranks, coarse_ref, *rest):
    pieces, (solved_ref, sums_ref) = rest[:ranks], rest[ranks:]
    for distance in range(ranks):
        rank = lax.axis_index("grp") ^ distance
        sums_ref[rank] = pieces[distance][...]
    total = sums_ref[0]
    for rank in range(1, ranks):
        total = total + sums_ref[rank]
    blocks, order = coarse_ref.shape[0], coarse_ref.shape[1]
    width = order // CORNER_DOF
    columns = []
    for block in range(blocks):
        lanes = slice(block * width, (block + 1) * width)
        row = jnp.concatenate([total[j : j + 1, lanes] for j in range(CORNER_DOF)], axis=1)
        parts = pieces_of(row) + [jnp.zeros((ROWS - 3, order), F32)]
        stacked = jnp.concatenate(parts, axis=0).astype(BF16)
        product = lax.dot_general(stacked, coarse_ref[block], NT, preferred_element_type=F32)
        result = product[0:1] + product[1:2] + product[2:3]
        rows = [result[:, j * width : (j + 1) * width] for j in range(CORNER_DOF)]
        columns.append(jnp.concatenate(rows, axis=0))
    solved = jnp.concatenate(columns, axis=1)
    solved_ref[...] = jnp.concatenate(
        [solved, jnp.zeros((ROWS - CORNER_DOF, solved.shape[1]), F32)], axis=0
    )


def lift_kernel(ranks, local_ref, operators_ref, table_ref, selector_ref, *rest):
    pieces, (near_ref, far_ref, values_ref) = rest[:ranks], rest[ranks:]
    cells = local_ref.shape[1]
    owned = values_ref.shape[1] // ranks
    for distance in range(ranks):
        rank = lax.axis_index("grp") ^ distance
        values_ref[:, pl.ds(pl.multiple_of(rank * owned, LANES), owned)] = pieces[distance][...]
    picked = exact_dot(values_ref[...], table_ref[...], NN)
    lifted = local_ref[...]
    for corner in range(CORNERS_SUB):
        lanes = slice(corner * cells, (corner + 1) * cells)
        for dof in range(CORNER_DOF):
            operator = operators_ref[corner * CORNER_DOF + dof].astype(F32)
            lifted = lifted + operator * picked[dof : dof + 1, lanes]
    collect_to(lax.axis_index("sub") % 2 == 1, lifted, selector_ref[...], near_ref, far_ref)


def final_kernel(dots_ref, scalars_ref, x_ref, r_ref, u_ref, w_ref, p_ref, s_ref, x_out, r_out):
    alpha, beta, _, _ = step_sizes(jnp.sum(dots_ref[...], axis=0), scalars_ref[...])
    x_out[...] = x_ref[...] + alpha * (u_ref[...] + beta * p_ref[...])
    r_out[...] = r_ref[...] - alpha * (w_ref[0] + beta * s_ref[...])


def shifted(block, distance):
    count = lax.axis_size("sub")
    route = [(i, i + distance) for i in range(count) if 0 <= i + distance < count]
    return lax.ppermute(block, "sub", route)


def swapped(block, bit):
    return lax.ppermute(block, "sub", [(i, i ^ bit) for i in range(lax.axis_size("sub"))])


def swapped_far(block):
    inner = range(1, lax.axis_size("sub") - 1)
    return lax.ppermute(block, "sub", [(i, i + 1 if i % 2 else i - 1) for i in inner])


def exchanged(block, distance):
    return lax.ppermute(block, "grp", [(i, i ^ distance) for i in range(lax.axis_size("grp"))])


def shape(*dims, dtype=F32):
    return jax.ShapeDtypeStruct(dims, dtype)


def call(kernel, out_shape, in_smem=(), count=0, scratch=(), flops=0, moved=0, name=None):
    specs = [
        pl.BlockSpec(memory_space=pltpu.SMEM if i in in_smem else pltpu.VMEM) for i in range(count)
    ]
    out_specs = jax.tree.map(lambda _: pl.BlockSpec(memory_space=pltpu.VMEM), out_shape)
    return pl.pallas_call(
        kernel,
        out_shape=out_shape,
        in_specs=specs,
        out_specs=out_specs,
        scratch_shapes=list(scratch),
        compiler_params=pltpu.CompilerParams(vmem_limit_bytes=24 * 1024 * 1024),
        cost_estimate=pl.CostEstimate(flops=flops, bytes_accessed=moved, transcendentals=0),
        name=name,
    )


def on_device(
    gap_data,
    local_inverse,
    stiffness,
    stiff_column,
    neighbour,
    corner_ops,
    corner_index,
    coarse_inverse,
):
    iface, _, cells = gap_data.shape
    ranks = lax.axis_size("grp")
    sub_count = lax.axis_size("sub")
    start = lax.axis_index("sub") * cells
    right_side = gap_data[:, 0, :]
    inverse = local_inverse[:, :, 0, :]
    stiff = stiffness[:, :, :, 0, :]
    operators = corner_ops[:, :, 0, :]
    blocks_own, order = coarse_inverse.shape[:2]
    owned = blocks_own * (order // CORNER_DOF)
    group = owned * ranks
    slots = jnp.where(neighbour < 0, -1, neighbour - (start - cells))
    column = stiff_column - start
    corners = corner_index.reshape(1, CORNERS_SUB * cells)

    selector, swap, table = call(
        table_kernel,
        (
            shape(2 * cells, cells, dtype=BF16),
            shape(cells, cells, dtype=BF16),
            shape(group, CORNERS_SUB * cells, dtype=BF16),
        ),
        count=3,
        name="tables",
    )(slots, column, corners)

    field = shape(iface, cells)
    pair = shape(2, iface, cells)
    rows = shape(ROWS, cells)
    parts = shape(ROWS, sub_count * ranks * LANES)
    last_parts = shape(sub_count * ranks, 1, LANES)
    piece = shape(ROWS, owned)
    stiff_scratch = [pltpu.VMEM((iface, cells), F32)]
    stiff_cost = dict(flops=4 * iface * iface * cells, moved=4 * iface * iface * cells)

    def apply_operator(near, far):
        from_far, from_near = swapped_far(far), swapped(near, 1)
        m, gap, *parts = call(
            lambda *refs: corner_kernel(ranks, *refs),
            (field, field) + (piece,) * ranks,
            count=7,
            scratch=[pltpu.VMEM((ROWS, group), F32)],
            flops=2 * 24 * iface * cells,
            moved=2 * 24 * iface * cells + group * CORNERS_SUB * cells * 2,
            name="corners",
        )(near, far, from_near, from_far, selector, operators, table)
        arrivals = [parts[0]] + [exchanged(parts[d], d) for d in range(1, ranks)]
        local = call(
            local_kernel,
            field,
            count=2,
            flops=2 * iface * iface * cells,
            moved=2 * iface * iface * cells,
            name="local",
        )(gap, inverse)
        solved = call(
            lambda *refs: coarse_kernel(ranks, *refs),
            piece,
            count=1 + ranks,
            scratch=[pltpu.VMEM((ranks, ROWS, owned), F32)],
            flops=2 * blocks_own * order * order,
            moved=2 * blocks_own * order * order,
            name="coarse",
        )(coarse_inverse, *arrivals)
        values = [solved] + [exchanged(solved, d) for d in range(1, ranks)]
        near, far = call(
            lambda *refs: lift_kernel(ranks, *refs),
            (field, field),
            count=4 + ranks,
            scratch=[pltpu.VMEM((ROWS, group), F32)],
            flops=2 * 24 * iface * cells,
            moved=2 * 24 * iface * cells + group * CORNERS_SUB * cells * 2,
            name="lift",
        )(local, operators, table, selector, *values)
        return m, near, far

    previous = shifted(right_side, 1)
    near, far = call(
        first_kernel, (field, field), count=5, scratch=stiff_scratch, name="first", **stiff_cost
    )(right_side, previous, selector, swap, stiff)
    u, near, far = apply_operator(near, far)
    r = right_side
    from_far, from_near = swapped_far(far), swapped(near, 1)
    w, dots, near, far = call(
        second_kernel,
        (pair, parts, field, field),
        count=9,
        scratch=stiff_scratch,
        name="second",
        **stiff_cost,
    )(near, far, from_near, from_far, r, u, selector, swap, stiff)

    scalars, x, p, s, q, z = [jnp.zeros((ROWS, cells), F32)] + [r] * 4 + [w]
    for step in range(ITERS - 1):
        first, last = step == 0, step == ITERS - 2
        sums = lax.psum_scatter(dots, ("sub", "grp"), scatter_dimension=1, tiled=True)
        m, near, far = apply_operator(near, far)
        from_far, from_near = swapped_far(far), swapped(near, 1)
        outs = (rows, field, field, field, pair, field, field, field, pair)
        outs += (last_parts if last else parts,)
        if not last:
            outs += (field, field)
        result = call(
            lambda *refs, first=first, last=last: middle_kernel(first, last, *refs),
            outs,
            count=18,
            scratch=() if last else stiff_scratch,
            name="last" if last else "middle",
            **({} if last else stiff_cost),
        )(
            near, far, from_near, from_far, sums, m, selector, swap, stiff,
            scalars, x, r, u, w, p, s, q, z,
        )
        scalars, x, r, u, w, p, s, q, z, dots = result[:10]
        if not last:
            near, far = result[10:]
    everyone = lax.all_to_all(dots, ("sub", "grp"), 0, 0, tiled=True)
    x, r = call(final_kernel, (field, field), count=8, name="final")(
        everyone, scalars, x, r, u, w, p, s
    )
    return (x[:, None, :], r[:, None, :])


def solution(mesh):
    in_specs = (
        P(None, "grp", "sub"),
        P(None, None, "grp", "sub"),
        P(None, None, None, "grp", "sub"),
        P("grp", "sub"),
        P("grp", "sub"),
        P(None, None, "grp", "sub"),
        P(None, "grp", "sub"),
        P("grp", None, "sub"),
    )
    out_specs = (P(None, "grp", "sub"), P(None, "grp", "sub"))
    return jax.shard_map(
        on_device, mesh=mesh, in_specs=in_specs, out_specs=out_specs, check_vma=False
    )
```

```python
import jax
import jax.numpy as jnp
from jax import lax
from jax.experimental import pallas as pl
from jax.experimental.pallas import tpu as pltpu
from jax.sharding import PartitionSpec as P

CORNER_DOF = 6
CORNERS_SUB = 4
ITERS = 5
ROWS = 8
NN = (((1,), (0,)), ((), ()))
NT = (((1,), (1,)), ((), ()))
F32 = jnp.float32
BF16 = jnp.bfloat16


def pieces_of(value):
    high = value.astype(BF16).astype(F32)
    rest = value - high
    middle = rest.astype(BF16).astype(F32)
    return [high, middle, rest - middle]


def exact_dot(value, table, dims):
    rows = value.shape[0]
    stacked = jnp.concatenate(pieces_of(value), axis=0).astype(BF16)
    product = lax.dot_general(stacked, table, dims, preferred_element_type=F32)
    return product[:rows] + product[rows : 2 * rows] + product[2 * rows :]


def lane_total(rows):
    return jnp.sum(rows, axis=1, keepdims=True)


def dot_rows(r, u, w, s=None, p=None):
    rows = [jnp.sum(r * u, axis=0, keepdims=True), jnp.sum(u * w, axis=0, keepdims=True)]
    if s is None:
        rows.append(jnp.zeros((ROWS - 2, r.shape[1]), F32))
    else:
        rows.append(jnp.sum(u * s, axis=0, keepdims=True))
        rows.append(jnp.sum(p * w, axis=0, keepdims=True))
        rows.append(jnp.zeros((ROWS - 4, r.shape[1]), F32))
    return jnp.concatenate(rows, axis=0)


def packed(rows):
    totals = jnp.broadcast_to(lane_total(rows), rows.shape)
    row = lax.broadcasted_iota(jnp.int32, rows.shape, 0)
    lane = lax.broadcasted_iota(jnp.int32, rows.shape, 1)
    return jnp.sum(jnp.where(row == lane, totals, 0.0), axis=0, keepdims=True)


def step_sizes(sums, before):
    norm, curvature, crossed, other = sums
    if before is None:
        beta = None
    else:
        beta = norm / before[0:1, 0:1]
        curvature = curvature + beta * (crossed + other) + beta * beta * before[1:2, 0:1]
    return norm / curvature, beta, norm, curvature


def collect_to(odd, vector, selector, near_ref, far_ref):
    iface, cells = vector.shape
    moved = exact_dot(vector, selector, NT)
    low = moved[:, :cells]
    high = vector - moved[:, cells:]
    near_ref[:iface] = jnp.where(odd, low, high)
    far_ref[:iface] = jnp.where(odd, high, low)


def spread_of(own, previous, selector):
    return own - exact_dot(jnp.concatenate([previous, own], axis=1), selector, NN)


def apply_blocks(blocks, vectors, out_ref):
    def step(index, carry):
        at = pl.ds(index * ROWS, ROWS)
        total = None
        for block, vector in zip(blocks, vectors):
            term = block[at].astype(F32) * vector[None]
            total = term if total is None else total + term
        out_ref[pl.ds(pl.multiple_of(index * ROWS, ROWS), ROWS)] = jnp.sum(total, axis=1)
        return carry

    lax.fori_loop(0, out_ref.shape[0] // ROWS, step, 0)


def table_kernel(slots_ref, column_ref, corner_ref, selector_ref, swap_ref, table_ref):
    def one_hot(row, count):
        places = lax.broadcasted_iota(jnp.int32, (count, row.shape[1]), 0)
        return jnp.where(places == row, 1.0, 0.0).astype(BF16)

    selector_ref[...] = one_hot(slots_ref[...], selector_ref.shape[0])
    swap_ref[...] = one_hot(column_ref[...], swap_ref.shape[0])
    chunk = 128

    def step(index, carry):
        row = corner_ref[...] - index * chunk
        table_ref[pl.ds(pl.multiple_of(index * chunk, chunk), chunk)] = one_hot(row, chunk)
        return carry

    lax.fori_loop(0, table_ref.shape[0] // chunk, step, 0)


def stiffen(odd, own, previous, selector_ref, swap_ref, stiffness_ref, stiff_ref, near_ref, far_ref):
    gap = spread_of(own, previous, selector_ref[...])
    taken = exact_dot(gap, swap_ref[...], NN)
    apply_blocks([stiffness_ref.at[0], stiffness_ref.at[1]], [gap, taken], stiff_ref)
    collect_to(odd, stiff_ref[...], selector_ref[...], near_ref, far_ref)


def first_kernel(
    own_ref, previous_ref, selector_ref, swap_ref, stiffness_ref, far_ref, near_ref, stiff_ref
):
    iface, cells = own_ref.shape
    odd = lax.axis_index("sub") % 2 == 1
    stiffen(
        odd, own_ref[...], previous_ref[...], selector_ref, swap_ref, stiffness_ref, stiff_ref, near_ref, far_ref
    )
    near_ref[iface:] = jnp.zeros((ROWS, cells), F32)


def arrived(odd, near_ref, far_ref, from_far_ref, from_near_ref, iface):
    near, far = near_ref[:iface], far_ref[...]
    from_near, from_far = from_near_ref[:iface], from_far_ref[...]
    own = jnp.where(odd, far - from_far, near - from_near)
    previous = jnp.where(odd, from_near - near, from_far - far)
    return own, previous


def second_kernel(
    near_ref, far_ref, from_far_ref, from_near_ref, r_ref, u_ref, selector_ref, swap_ref, stiffness_ref,
    far_out, near_out, w_out, stiff_ref,
):
    iface = r_ref.shape[0]
    odd = lax.axis_index("sub") % 2 == 1
    w, w_previous = arrived(odd, near_ref, far_ref, from_far_ref, from_near_ref, iface)
    w_out[0] = w
    w_out[1] = w_previous
    dots = dot_rows(r_ref[...], u_ref[...], w)
    near_out[iface:] = dots
    stiffen(odd, w, w_previous, selector_ref, swap_ref, stiffness_ref, stiff_ref, near_out, far_out)


def update(first, last, refs, m, n, n_previous, totals):
    scalars_in, x_in, r_in, u_in, w_in, p_in, s_in, q_in, z_in = refs[:9]
    scalars_out, x_out, r_out, u_out, w_out, p_out, s_out, q_out, z_out = refs[9:]
    sums = lane_total(totals)
    sums = [sums[k : k + 1] for k in range(4)]
    alpha, beta, norm, curvature = step_sizes(sums, None if first else scalars_in[...])
    cells = m.shape[1]
    scalars_out[...] = jnp.concatenate(
        [
            jnp.broadcast_to(norm, (1, cells)),
            jnp.broadcast_to(curvature, (1, cells)),
            jnp.zeros((ROWS - 2, cells), F32),
        ],
        axis=0,
    )

    def turned(fresh, kept):
        return fresh if first else fresh + beta * kept[...]

    u, w = u_in[...], w_in[0]
    p = turned(u, p_in)
    s = turned(w, s_in)
    q = turned(m, q_in)
    z = turned(n, None if first else z_in.at[0])
    p_out[...] = p
    s_out[...] = s
    x_out[...] = alpha * p if first else x_in[...] + alpha * p
    r = r_in[...] - alpha * s
    u = u - alpha * q
    w = w - alpha * z
    r_out[...] = r
    u_out[...] = u
    w_out[0] = w
    previous = None
    if not last:
        z_previous = turned(n_previous, None if first else z_in.at[1])
        previous = w_in[1] - alpha * z_previous
        q_out[...] = q
        z_out[0] = z
        z_out[1] = z_previous
        w_out[1] = previous
    return dot_rows(r, u, w, s, p), w, previous


def middle_kernel(first, last, *refs):
    (near_ref, far_ref, from_far_ref, from_near_ref, dots_ref, dots_other_ref, m_ref) = refs[:7]
    (selector_ref, swap_ref, stiffness_ref) = refs[7:10]
    ins = list(refs[10:19])
    outs = list(refs[19:28])
    m = m_ref[...]
    iface = m.shape[0]
    odd = lax.axis_index("sub") % 2 == 1
    n, n_previous = arrived(odd, near_ref, far_ref, from_far_ref, from_near_ref, iface)
    dots, w, previous = update(
        first, last, ins + outs, m, n, n_previous, dots_ref[...] + dots_other_ref[...]
    )
    if last:
        dots_out = refs[28]
        dots_out[...] = jnp.broadcast_to(packed(dots)[None], dots_out.shape)
    else:
        far_out, near_out, stiff_ref = refs[28:31]
        near_out[iface:] = dots
        stiffen(odd, w, previous, selector_ref, swap_ref, stiffness_ref, stiff_ref, near_out, far_out)


def corner_kernel(
    ranks, near_ref, far_ref, from_far_ref, from_near_ref, selector_ref, operators_ref, table_ref,
    m_out, gap_out, *rest,
):
    outs, sums_ref = rest[:ranks], rest[ranks]
    iface, cells = m_out.shape
    odd = lax.axis_index("sub") % 2 == 1
    own, previous = arrived(odd, near_ref, far_ref, from_far_ref, from_near_ref, iface)
    m_out[...] = own
    dots = near_ref[iface:] + from_near_ref[iface:]
    gap = spread_of(own, previous, selector_ref[...])
    gap_out[...] = gap
    parts = []
    for corner in range(CORNERS_SUB):
        at = slice(corner * CORNER_DOF, (corner + 1) * CORNER_DOF)
        part = jnp.sum(operators_ref[at].astype(F32) * gap[None], axis=1)
        parts.append(jnp.concatenate([part, jnp.zeros((ROWS - CORNER_DOF, cells), F32)], axis=0))
    sums_ref[...] = exact_dot(jnp.concatenate(parts, axis=1), table_ref[...], NT)
    owned = sums_ref.shape[1] // ranks
    pad = jnp.zeros((1, owned - 2 * cells), F32) if owned > 2 * cells else None
    tail = []
    for row in range(0, ROWS - CORNER_DOF):
        lanes = [dots[2 * row : 2 * row + 1], dots[2 * row + 1 : 2 * row + 2]]
        if pad is not None:
            lanes.append(pad)
        tail.append(jnp.concatenate(lanes, axis=1))
    tail = jnp.concatenate(tail, axis=0)
    for distance in range(ranks):
        rank = lax.axis_index("grp") ^ distance
        piece = sums_ref[:, pl.ds(pl.multiple_of(rank * owned, 128), owned)]
        outs[distance][...] = jnp.concatenate([piece[:CORNER_DOF], tail], axis=0)


def local_kernel(gap_ref, inverse_ref, local_ref):
    apply_blocks([inverse_ref], [gap_ref[...]], local_ref)


def coarse_kernel(ranks, coarse_ref, *rest):
    pieces, (solved_ref, dots_ref, sums_ref) = rest[:ranks], rest[ranks:]
    cells = dots_ref.shape[1]
    for distance in range(ranks):
        rank = lax.axis_index("grp") ^ distance
        sums_ref[rank] = pieces[distance][...]
    total = sums_ref[0]
    for rank in range(1, ranks):
        total = total + sums_ref[rank]
    tail = total[CORNER_DOF:]
    dots_ref[...] = jnp.concatenate(
        [
            tail[0:1, :cells],
            tail[0:1, cells : 2 * cells],
            tail[1:2, :cells],
            tail[1:2, cells : 2 * cells],
            jnp.zeros((ROWS - 4, cells), F32),
        ],
        axis=0,
    )
    blocks, order = coarse_ref.shape[0], coarse_ref.shape[1]
    width = order // CORNER_DOF
    columns = []
    for block in range(blocks):
        lanes = slice(block * width, (block + 1) * width)
        row = jnp.concatenate([total[j : j + 1, lanes] for j in range(CORNER_DOF)], axis=1)
        parts = pieces_of(row) + [jnp.zeros((ROWS - 3, order), F32)]
        stacked = jnp.concatenate(parts, axis=0).astype(BF16)
        product = lax.dot_general(stacked, coarse_ref[block], NT, preferred_element_type=F32)
        result = product[0:1] + product[1:2] + product[2:3]
        rows = [result[:, j * width : (j + 1) * width] for j in range(CORNER_DOF)]
        columns.append(jnp.concatenate(rows, axis=0))
    solved = jnp.concatenate(columns, axis=1)
    solved_ref[...] = jnp.concatenate(
        [solved, jnp.zeros((ROWS - CORNER_DOF, solved.shape[1]), F32)], axis=0
    )


def lift_kernel(ranks, local_ref, operators_ref, table_ref, selector_ref, dots_ref, other_ref, *rest):
    pieces, (far_ref, near_ref, dots_out, values_ref) = rest[:ranks], rest[ranks:]
    cells = local_ref.shape[1]
    owned = values_ref.shape[1] // ranks
    dots_out[...] = dots_ref[...] + other_ref[...]
    for distance in range(ranks):
        rank = lax.axis_index("grp") ^ distance
        values_ref[:, pl.ds(pl.multiple_of(rank * owned, 128), owned)] = pieces[distance][...]
    picked = exact_dot(values_ref[...], table_ref[...], NN)
    lifted = local_ref[...]
    for corner in range(CORNERS_SUB):
        lanes = slice(corner * cells, (corner + 1) * cells)
        for dof in range(CORNER_DOF):
            operator = operators_ref[corner * CORNER_DOF + dof].astype(F32)
            lifted = lifted + operator * picked[dof : dof + 1, lanes]
    collect_to(lax.axis_index("sub") % 2 == 1, lifted, selector_ref[...], near_ref, far_ref)


def final_kernel(dots_ref, scalars_ref, x_ref, r_ref, u_ref, w_ref, p_ref, s_ref, x_out, r_out):
    totals = jnp.sum(dots_ref[...], axis=0)
    sums = [totals[:, k : k + 1] for k in range(4)]
    alpha, beta, _, _ = step_sizes(sums, scalars_ref[...])
    x_out[...] = x_ref[...] + alpha * (u_ref[...] + beta * p_ref[...])
    r_out[...] = r_ref[...] - alpha * (w_ref[0] + beta * s_ref[...])


def shifted(block, distance):
    count = lax.axis_size("sub")
    route = [(i, i + distance) for i in range(count) if 0 <= i + distance < count]
    return lax.ppermute(block, "sub", route)


def swapped(block, bit):
    return lax.ppermute(block, "sub", [(i, i ^ bit) for i in range(lax.axis_size("sub"))])


def swapped_far(block):
    inner = range(1, lax.axis_size("sub") - 1)
    return lax.ppermute(block, "sub", [(i, i + 1 if i % 2 else i - 1) for i in inner])


def exchanged(block, distance):
    return lax.ppermute(block, "grp", [(i, i ^ distance) for i in range(lax.axis_size("grp"))])


def shape(*dims, dtype=F32):
    return jax.ShapeDtypeStruct(dims, dtype)


def call(kernel, out_shape, count=0, scratch=(), flops=0, moved=0, name=None):
    specs = [pl.BlockSpec(memory_space=pltpu.VMEM)] * count
    out_specs = jax.tree.map(lambda _: pl.BlockSpec(memory_space=pltpu.VMEM), out_shape)
    return pl.pallas_call(
        kernel,
        out_shape=out_shape,
        in_specs=specs,
        out_specs=out_specs,
        scratch_shapes=list(scratch),
        compiler_params=pltpu.CompilerParams(vmem_limit_bytes=24 * 1024 * 1024),
        cost_estimate=pl.CostEstimate(flops=flops, bytes_accessed=moved, transcendentals=0),
        name=name,
    )


def on_device(
    gap_data,
    local_inverse,
    stiffness,
    stiff_column,
    neighbour,
    corner_ops,
    corner_index,
    coarse_inverse,
):
    iface, _, cells = gap_data.shape
    ranks = lax.axis_size("grp")
    sub_count = lax.axis_size("sub")
    start = lax.axis_index("sub") * cells
    right_side = gap_data[:, 0, :]
    inverse = local_inverse[:, :, 0, :]
    stiff = stiffness[:, :, :, 0, :]
    operators = corner_ops[:, :, 0, :]
    blocks_own, order = coarse_inverse.shape[:2]
    owned = blocks_own * (order // CORNER_DOF)
    group = owned * ranks
    slots = jnp.where(neighbour < 0, -1, neighbour - (start - cells))
    column = stiff_column - start
    corners = corner_index.reshape(1, CORNERS_SUB * cells)

    selector, swap, table = call(
        table_kernel,
        (
            shape(2 * cells, cells, dtype=BF16),
            shape(cells, cells, dtype=BF16),
            shape(group, CORNERS_SUB * cells, dtype=BF16),
        ),
        count=3,
        name="tables",
    )(slots, column, corners)

    field = shape(iface, cells)
    pair = shape(2, iface, cells)
    message = shape(iface + ROWS, cells)
    rows = shape(ROWS, cells)
    piece = shape(ROWS, owned)
    stiff_scratch = [pltpu.VMEM((iface, cells), F32)]
    stiff_cost = dict(flops=4 * iface * iface * cells, moved=4 * iface * iface * cells)

    def apply_operator(near, far):
        from_far, from_near = swapped_far(far), swapped(near, 1)
        m, gap, *parts = call(
            lambda *refs: corner_kernel(ranks, *refs),
            (field, field) + (piece,) * ranks,
            count=7,
            scratch=[pltpu.VMEM((ROWS, group), F32)],
            flops=2 * 24 * iface * cells,
            moved=2 * 24 * iface * cells + group * CORNERS_SUB * cells * 2,
            name="corners",
        )(near, far, from_far, from_near, selector, operators, table)
        arrivals = [parts[0]] + [exchanged(parts[d], d) for d in range(1, ranks)]
        local = call(
            local_kernel,
            field,
            count=2,
            flops=2 * iface * iface * cells,
            moved=2 * iface * iface * cells,
            name="local",
        )(gap, inverse)
        solved, dots = call(
            lambda *refs: coarse_kernel(ranks, *refs),
            (piece, rows),
            count=1 + ranks,
            scratch=[pltpu.VMEM((ranks, ROWS, owned), F32)],
            flops=2 * blocks_own * order * order,
            moved=2 * blocks_own * order * order,
            name="coarse",
        )(coarse_inverse, *arrivals)
        values = [solved] + [exchanged(solved, d) for d in range(1, ranks)]
        other = swapped(dots, 2)
        far, near, dots = call(
            lambda *refs: lift_kernel(ranks, *refs),
            (field, field, rows),
            count=6 + ranks,
            scratch=[pltpu.VMEM((ROWS, group), F32)],
            flops=2 * 24 * iface * cells,
            moved=2 * 24 * iface * cells + group * CORNERS_SUB * cells * 2,
            name="lift",
        )(local, operators, table, selector, dots, other, *values)
        return m, near, far, dots

    previous = shifted(right_side, 1)
    far, near = call(
        first_kernel, (field, message), count=5, scratch=stiff_scratch, name="first", **stiff_cost
    )(right_side, previous, selector, swap, stiff)
    u, near, far, dots = apply_operator(near, far)
    r = right_side
    from_far, from_near = swapped_far(far), swapped(near, 1)
    far, near, w = call(
        second_kernel,
        (field, message, pair),
        count=9,
        scratch=stiff_scratch,
        name="second",
        **stiff_cost,
    )(near, far, from_far, from_near, r, u, selector, swap, stiff)

    scalars, x, p, s, q, z = [jnp.zeros((ROWS, cells), F32)] + [r] * 4 + [w]
    for step in range(ITERS - 1):
        first, last = step == 0, step == ITERS - 2
        m, near, far, dots = apply_operator(near, far)
        from_far, from_near, other = swapped_far(far), swapped(near, 1), swapped(dots, 4)
        bit = 8
        while bit < sub_count:
            dots = dots + other
            other = swapped(dots, bit)
            bit *= 2
        outs = (rows, field, field, field, pair, field, field, field, pair)
        if last:
            count = sub_count * ranks
            outs += (shape(count, 1, cells),)
        else:
            outs += (field, message)
        result = call(
            lambda *refs, first=first, last=last: middle_kernel(first, last, *refs),
            outs,
            count=19,
            scratch=() if last else stiff_scratch,
            name="last" if last else "middle",
            **({} if last else stiff_cost),
        )(
            near, far, from_far, from_near, dots, other, m, selector, swap, stiff,
            scalars, x, r, u, w, p, s, q, z,
        )
        scalars, x, r, u, w, p, s, q, z = result[:9]
        if not last:
            far, near = result[9:]
    everyone = lax.all_to_all(result[9], ("sub", "grp"), 0, 0, tiled=True)
    x, r = call(final_kernel, (field, field), count=8, name="final")(
        everyone, scalars, x, r, u, w, p, s
    )
    return (x[:, None, :], r[:, None, :])


def solution(mesh):
    in_specs = (
        P(None, "grp", "sub"),
        P(None, None, "grp", "sub"),
        P(None, None, None, "grp", "sub"),
        P("grp", "sub"),
        P("grp", "sub"),
        P(None, None, "grp", "sub"),
        P(None, "grp", "sub"),
        P("grp", None, "sub"),
    )
    out_specs = (P(None, "grp", "sub"), P(None, "grp", "sub"))
    return jax.shard_map(
        on_device, mesh=mesh, in_specs=in_specs, out_specs=out_specs, check_vma=False
    )
```

```python
import jax
import jax.numpy as jnp
from jax import lax
from jax.experimental import pallas as pl
from jax.experimental.pallas import tpu as pltpu
from jax.sharding import PartitionSpec as P

CORNER_DOF = 6
CORNERS_SUB = 4
ITERS = 5
ROWS = 8
NN = (((1,), (0,)), ((), ()))
NT = (((1,), (1,)), ((), ()))
F32 = jnp.float32
BF16 = jnp.bfloat16


def pieces_of(value):
    high = value.astype(BF16).astype(F32)
    rest = value - high
    middle = rest.astype(BF16).astype(F32)
    return [high, middle, rest - middle]


def exact_dot(value, table, dims):
    rows = value.shape[0]
    stacked = jnp.concatenate(pieces_of(value), axis=0).astype(BF16)
    product = lax.dot_general(stacked, table, dims, preferred_element_type=F32)
    return product[:rows] + product[rows : 2 * rows] + product[2 * rows :]


def lane_total(rows):
    return jnp.sum(rows, axis=1, keepdims=True)


def dot_rows(r, u, w, s=None, p=None):
    rows = [jnp.sum(r * u, axis=0, keepdims=True), jnp.sum(u * w, axis=0, keepdims=True)]
    if s is None:
        rows.append(jnp.zeros((ROWS - 2, r.shape[1]), F32))
    else:
        rows.append(jnp.sum(u * s, axis=0, keepdims=True))
        rows.append(jnp.sum(p * w, axis=0, keepdims=True))
        rows.append(jnp.zeros((ROWS - 4, r.shape[1]), F32))
    return jnp.concatenate(rows, axis=0)


def packed(rows):
    totals = jnp.broadcast_to(lane_total(rows), rows.shape)
    row = lax.broadcasted_iota(jnp.int32, rows.shape, 0)
    lane = lax.broadcasted_iota(jnp.int32, rows.shape, 1)
    return jnp.sum(jnp.where(row == lane, totals, 0.0), axis=0, keepdims=True)


def step_sizes(sums, before):
    norm, curvature, crossed, other = sums
    if before is None:
        beta = None
    else:
        beta = norm / before[0:1, 0:1]
        curvature = curvature + beta * (crossed + other) + beta * beta * before[1:2, 0:1]
    return norm / curvature, beta, norm, curvature


def collect_to(odd, vector, selector, near_ref, far_ref):
    iface, cells = vector.shape
    moved = exact_dot(vector, selector, NT)
    low = moved[:, :cells]
    high = vector - moved[:, cells:]
    near_ref[:iface] = jnp.where(odd, low, high)
    far_ref[:iface] = jnp.where(odd, high, low)


def spread_of(own, previous, selector):
    return own - exact_dot(jnp.concatenate([previous, own], axis=1), selector, NN)


def apply_blocks(blocks, vectors, out_ref):
    def step(index, carry):
        at = pl.ds(index * ROWS, ROWS)
        total = None
        for block, vector in zip(blocks, vectors):
            term = block[at].astype(F32) * vector[None]
            total = term if total is None else total + term
        out_ref[pl.ds(pl.multiple_of(index * ROWS, ROWS), ROWS)] = jnp.sum(total, axis=1)
        return carry

    lax.fori_loop(0, out_ref.shape[0] // ROWS, step, 0, unroll=True)


def table_kernel(neighbour_ref, column_ref, corner_ref, selector_ref, swap_ref, table_ref):
    cells = swap_ref.shape[0]
    start = lax.axis_index("sub") * cells
    def one_hot(row, count):
        places = lax.broadcasted_iota(jnp.int32, (count, row.shape[1]), 0)
        return jnp.where(places == row, 1.0, 0.0).astype(BF16)

    neighbour = neighbour_ref[...]
    slots = jnp.where(neighbour < 0, -1, neighbour - (start - cells))
    selector_ref[...] = one_hot(slots, selector_ref.shape[0])
    swap_ref[...] = one_hot(column_ref[...] - start, swap_ref.shape[0])
    chunk = 128

    def step(index, carry):
        row = corner_ref[...] - index * chunk
        table_ref[pl.ds(pl.multiple_of(index * chunk, chunk), chunk)] = one_hot(row, chunk)
        return carry

    lax.fori_loop(0, table_ref.shape[0] // chunk, step, 0)


def stiffen(odd, own, previous, selector_ref, swap_ref, stiffness_ref, stiff_ref, near_ref, far_ref):
    gap = spread_of(own, previous, selector_ref[...])
    taken = exact_dot(gap, swap_ref[...], NN)
    apply_blocks([stiffness_ref.at[0], stiffness_ref.at[1]], [gap, taken], stiff_ref)
    collect_to(odd, stiff_ref[...], selector_ref[...], near_ref, far_ref)


def first_kernel(
    own_ref, previous_ref, selector_ref, swap_ref, stiffness_ref, far_ref, near_ref, stiff_ref
):
    iface, cells = own_ref.shape
    odd = lax.axis_index("sub") % 2 == 1
    stiffen(
        odd, own_ref[...], previous_ref[...], selector_ref, swap_ref, stiffness_ref, stiff_ref, near_ref, far_ref
    )
    near_ref[iface:] = jnp.zeros((ROWS, cells), F32)
    far_ref[iface:] = jnp.zeros((ROWS, cells), F32)


def arrived(odd, far_ref, near_ref, from_far_ref, from_near_ref, iface):
    near, far = near_ref[:iface], far_ref[:iface]
    from_near, from_far = from_near_ref[:iface], from_far_ref[:iface]
    own = jnp.where(odd, far - from_far, near - from_near)
    previous = jnp.where(odd, from_near - near, from_far - far)
    return own, previous


def second_kernel(
    far_ref, near_ref, from_far_ref, from_near_ref, r_ref, u_ref, selector_ref, swap_ref, stiffness_ref,
    far_out, near_out, w_out, stiff_ref,
):
    iface = r_ref.shape[0]
    odd = lax.axis_index("sub") % 2 == 1
    w, w_previous = arrived(odd, far_ref, near_ref, from_far_ref, from_near_ref, iface)
    w_out[0] = w
    w_out[1] = w_previous
    dots = dot_rows(r_ref[...], u_ref[...], w)
    near_out[iface:] = dots
    far_out[iface:] = dots
    stiffen(odd, w, w_previous, selector_ref, swap_ref, stiffness_ref, stiff_ref, near_out, far_out)


def update(first, last, refs, m, n, n_previous, totals):
    scalars_in, x_in, r_in, u_in, w_in, p_in, s_in, q_in, z_in = refs[:9]
    scalars_out, x_out, r_out, u_out, w_out, p_out, s_out, q_out, z_out = refs[9:]
    sums = lane_total(totals)
    sums = [sums[k : k + 1] for k in range(4)]
    alpha, beta, norm, curvature = step_sizes(sums, None if first else scalars_in[...])
    cells = m.shape[1]
    scalars_out[...] = jnp.concatenate(
        [
            jnp.broadcast_to(norm, (1, cells)),
            jnp.broadcast_to(curvature, (1, cells)),
            jnp.zeros((ROWS - 2, cells), F32),
        ],
        axis=0,
    )

    def turned(fresh, kept):
        return fresh if first else fresh + beta * kept[...]

    u, w = u_in[...], w_in[0]
    p = turned(u, p_in)
    s = turned(w, s_in)
    q = turned(m, q_in)
    z = turned(n, None if first else z_in.at[0])
    p_out[...] = p
    s_out[...] = s
    x_out[...] = alpha * p if first else x_in[...] + alpha * p
    r = r_in[...] - alpha * s
    u = u - alpha * q
    w = w - alpha * z
    r_out[...] = r
    u_out[...] = u
    w_out[0] = w
    previous = None
    if not last:
        z_previous = turned(n_previous, None if first else z_in.at[1])
        previous = w_in[1] - alpha * z_previous
        q_out[...] = q
        z_out[0] = z
        z_out[1] = z_previous
        w_out[1] = previous
    return dot_rows(r, u, w, s, p), w, previous


def middle_kernel(first, last, *refs):
    (far_ref, near_ref, from_far_ref, from_near_ref, dots_ref, dots_other_ref, m_ref) = refs[:7]
    (selector_ref, swap_ref, stiffness_ref) = refs[7:10]
    ins = list(refs[10:19])
    outs = list(refs[19:28])
    m = m_ref[...]
    iface = m.shape[0]
    odd = lax.axis_index("sub") % 2 == 1
    n, n_previous = arrived(odd, far_ref, near_ref, from_far_ref, from_near_ref, iface)
    dots, w, previous = update(
        first, last, ins + outs, m, n, n_previous, dots_ref[...] + dots_other_ref[...]
    )
    if last:
        dots_out = refs[28]
        dots_out[...] = jnp.broadcast_to(packed(dots)[None], dots_out.shape)
    else:
        far_out, near_out, stiff_ref = refs[28:31]
        near_out[iface:] = dots
        far_out[iface:] = dots
        stiffen(odd, w, previous, selector_ref, swap_ref, stiffness_ref, stiff_ref, near_out, far_out)


def corner_kernel(
    ranks, far_ref, near_ref, from_far_ref, from_near_ref, selector_ref, operators_ref, table_ref,
    m_out, gap_out, *rest,
):
    outs, (dots_out, sums_ref) = rest[:ranks], rest[ranks:]
    iface, cells = m_out.shape
    odd = lax.axis_index("sub") % 2 == 1
    own, previous = arrived(odd, far_ref, near_ref, from_far_ref, from_near_ref, iface)
    m_out[...] = own
    dots_out[...] = near_ref[iface:] + from_near_ref[iface:]
    gap = spread_of(own, previous, selector_ref[...])
    gap_out[...] = gap
    parts = []
    for corner in range(CORNERS_SUB):
        at = slice(corner * CORNER_DOF, (corner + 1) * CORNER_DOF)
        part = jnp.sum(operators_ref[at].astype(F32) * gap[None], axis=1)
        parts.append(jnp.concatenate([part, jnp.zeros((ROWS - CORNER_DOF, cells), F32)], axis=0))
    sums_ref[...] = exact_dot(jnp.concatenate(parts, axis=1), table_ref[...], NT)
    owned = sums_ref.shape[1] // ranks
    for distance in range(ranks):
        rank = lax.axis_index("grp") ^ (ranks - 1 - distance)
        outs[distance][...] = sums_ref[:, pl.ds(pl.multiple_of(rank * owned, 128), owned)]


def local_kernel(gap_ref, inverse_ref, local_ref):
    apply_blocks([inverse_ref], [gap_ref[...]], local_ref)


def coarse_kernel(ranks, coarse_ref, dots_ref, other_ref, *rest):
    pieces, (solved_ref, sums_ref) = rest[:ranks], rest[ranks:]
    cells = dots_ref.shape[1]
    for distance in range(ranks):
        rank = lax.axis_index("grp") ^ distance
        sums_ref[rank] = pieces[ranks - 1 - distance][...]
    total = sums_ref[0]
    for rank in range(1, ranks):
        total = total + sums_ref[rank]
    blocks, order = coarse_ref.shape[0], coarse_ref.shape[1]
    width = order // CORNER_DOF
    columns = []
    for block in range(blocks):
        lanes = slice(block * width, (block + 1) * width)
        row = jnp.concatenate([total[j : j + 1, lanes] for j in range(CORNER_DOF)], axis=1)
        parts = pieces_of(row) + [jnp.zeros((ROWS - 3, order), F32)]
        stacked = jnp.concatenate(parts, axis=0).astype(BF16)
        product = lax.dot_general(stacked, coarse_ref[block], NT, preferred_element_type=F32)
        result = product[0:1] + product[1:2] + product[2:3]
        rows = [result[:, j * width : (j + 1) * width] for j in range(CORNER_DOF)]
        columns.append(jnp.concatenate(rows, axis=0))
    solved = jnp.concatenate(columns, axis=1)
    dots = dots_ref[...] + other_ref[...]
    rows = [solved]
    for first in (0, 2):
        lanes = [dots[first : first + 1], dots[first + 1 : first + 2]]
        if solved.shape[1] > 2 * cells:
            lanes.append(jnp.zeros((1, solved.shape[1] - 2 * cells), F32))
        rows.append(jnp.concatenate(lanes, axis=1))
    solved_ref[...] = jnp.concatenate(rows, axis=0)


def lift_kernel(ranks, local_ref, operators_ref, table_ref, selector_ref, *rest):
    pieces, (far_ref, near_ref, dots_out, values_ref) = rest[:ranks], rest[ranks:]
    cells = local_ref.shape[1]
    owned = values_ref.shape[1] // ranks
    for distance in range(ranks):
        rank = lax.axis_index("grp") ^ distance
        values_ref[:, pl.ds(pl.multiple_of(rank * owned, 128), owned)] = pieces[distance][...]
    values = values_ref[...]
    tail = values[CORNER_DOF:, :owned]
    for rank in range(1, ranks):
        tail = tail + values[CORNER_DOF:, rank * owned : (rank + 1) * owned]
    dots_out[...] = jnp.concatenate(
        [
            tail[0:1, :cells],
            tail[0:1, cells : 2 * cells],
            tail[1:2, :cells],
            tail[1:2, cells : 2 * cells],
            jnp.zeros((ROWS - 4, cells), F32),
        ],
        axis=0,
    )
    picked = exact_dot(values, table_ref[...], NN)
    lifted = local_ref[...]
    for corner in range(CORNERS_SUB):
        lanes = slice(corner * cells, (corner + 1) * cells)
        for dof in range(CORNER_DOF):
            operator = operators_ref[corner * CORNER_DOF + dof].astype(F32)
            lifted = lifted + operator * picked[dof : dof + 1, lanes]
    collect_to(lax.axis_index("sub") % 2 == 1, lifted, selector_ref[...], near_ref, far_ref)


def final_kernel(dots_ref, scalars_ref, x_ref, r_ref, u_ref, w_ref, p_ref, s_ref, x_out, r_out):
    totals = jnp.sum(dots_ref[...], axis=0)
    sums = [totals[:, k : k + 1] for k in range(4)]
    alpha, beta, _, _ = step_sizes(sums, scalars_ref[...])
    x_out[...] = x_ref[...] + alpha * (u_ref[...] + beta * p_ref[...])
    r_out[...] = r_ref[...] - alpha * (w_ref[0] + beta * s_ref[...])


def shifted(block, distance):
    count = lax.axis_size("sub")
    route = [(i, i + distance) for i in range(count) if 0 <= i + distance < count]
    return lax.ppermute(block, "sub", route)


def swapped(block, bit):
    return lax.ppermute(block, "sub", [(i, i ^ bit) for i in range(lax.axis_size("sub"))])


def swapped_far(block):
    inner = range(1, lax.axis_size("sub") - 1)
    return lax.ppermute(block, "sub", [(i, i + 1 if i % 2 else i - 1) for i in inner])


def exchanged(block, distance):
    return lax.ppermute(block, "grp", [(i, i ^ distance) for i in range(lax.axis_size("grp"))])


def shape(*dims, dtype=F32):
    return jax.ShapeDtypeStruct(dims, dtype)


def call(kernel, out_shape, count=0, scratch=(), flops=0, moved=0, name=None):
    specs = [pl.BlockSpec(memory_space=pltpu.VMEM)] * count
    out_specs = jax.tree.map(lambda _: pl.BlockSpec(memory_space=pltpu.VMEM), out_shape)
    return pl.pallas_call(
        kernel,
        out_shape=out_shape,
        in_specs=specs,
        out_specs=out_specs,
        scratch_shapes=list(scratch),
        compiler_params=pltpu.CompilerParams(vmem_limit_bytes=24 * 1024 * 1024),
        cost_estimate=pl.CostEstimate(flops=flops, bytes_accessed=moved, transcendentals=0),
        name=name,
    )


def on_device(
    gap_data,
    local_inverse,
    stiffness,
    stiff_column,
    neighbour,
    corner_ops,
    corner_index,
    coarse_inverse,
):
    iface, _, cells = gap_data.shape
    ranks = lax.axis_size("grp")
    sub_count = lax.axis_size("sub")
    right_side = gap_data[:, 0, :]
    inverse = local_inverse[:, :, 0, :]
    stiff = stiffness[:, :, :, 0, :]
    operators = corner_ops[:, :, 0, :]
    blocks_own, order = coarse_inverse.shape[:2]
    owned = blocks_own * (order // CORNER_DOF)
    group = owned * ranks
    corners = corner_index.reshape(1, CORNERS_SUB * cells)

    selector, swap, table = call(
        table_kernel,
        (
            shape(2 * cells, cells, dtype=BF16),
            shape(cells, cells, dtype=BF16),
            shape(group, CORNERS_SUB * cells, dtype=BF16),
        ),
        count=3,
        name="tables",
    )(neighbour, stiff_column, corners)

    field = shape(iface, cells)
    pair = shape(2, iface, cells)
    message = shape(iface + ROWS, cells)
    rows = shape(ROWS, cells)
    piece = shape(ROWS, owned)
    stiff_scratch = [pltpu.VMEM((iface, cells), F32)]
    stiff_cost = dict(flops=4 * iface * iface * cells, moved=4 * iface * iface * cells)

    def apply_operator(near, far):
        from_far, from_near = swapped_far(far), swapped(near, 1)
        m, gap, *parts, dots = call(
            lambda *refs: corner_kernel(ranks, *refs),
            (field, field) + (piece,) * ranks + (rows,),
            count=7,
            scratch=[pltpu.VMEM((ROWS, group), F32)],
            flops=2 * 24 * iface * cells,
            moved=2 * 24 * iface * cells + group * CORNERS_SUB * cells * 2,
            name="corners",
        )(far, near, from_far, from_near, selector, operators, table)
        arrivals = [exchanged(parts[ranks - 1 - d], d) for d in range(ranks - 1, 0, -1)] + [parts[ranks - 1]]
        local = call(
            local_kernel,
            field,
            count=2,
            flops=2 * iface * iface * cells,
            moved=2 * iface * iface * cells,
            name="local",
        )(gap, inverse)
        other = swapped(dots, 2)
        solved = call(
            lambda *refs: coarse_kernel(ranks, *refs),
            piece,
            count=3 + ranks,
            scratch=[pltpu.VMEM((ranks, ROWS, owned), F32)],
            flops=2 * blocks_own * order * order,
            moved=2 * blocks_own * order * order,
            name="coarse",
        )(coarse_inverse, dots, other, *arrivals)
        values = [solved] + [exchanged(solved, d) for d in range(1, ranks)]
        far, near, dots = call(
            lambda *refs: lift_kernel(ranks, *refs),
            (field, field, rows),
            count=4 + ranks,
            scratch=[pltpu.VMEM((ROWS, group), F32)],
            flops=2 * 24 * iface * cells,
            moved=2 * 24 * iface * cells + group * CORNERS_SUB * cells * 2,
            name="lift",
        )(local, operators, table, selector, *values)
        return m, near, far, dots

    previous = shifted(right_side, 1)
    far, near = call(
        first_kernel, (message, message), count=5, scratch=stiff_scratch, name="first", **stiff_cost
    )(right_side, previous, selector, swap, stiff)
    u, near, far, dots = apply_operator(near, far)
    r = right_side
    from_far, from_near = swapped_far(far), swapped(near, 1)
    far, near, w = call(
        second_kernel,
        (message, message, pair),
        count=9,
        scratch=stiff_scratch,
        name="second",
        **stiff_cost,
    )(far, near, from_far, from_near, r, u, selector, swap, stiff)

    scalars, x, p, s, q, z = [jnp.zeros((ROWS, cells), F32)] + [r] * 4 + [w]
    for step in range(ITERS - 1):
        first, last = step == 0, step == ITERS - 2
        m, near, far, dots = apply_operator(near, far)
        from_far, from_near, other = swapped_far(far), swapped(near, 1), swapped(dots, 4)
        bit = 8
        while bit < sub_count:
            dots = dots + other
            other = swapped(dots, bit)
            bit *= 2
        outs = (rows, field, field, field, pair, field, field, field, pair)
        if last:
            count = sub_count * ranks
            outs += (shape(count, 1, cells),)
        else:
            outs += (message, message)
        result = call(
            lambda *refs, first=first, last=last: middle_kernel(first, last, *refs),
            outs,
            count=19,
            scratch=() if last else stiff_scratch,
            name="last" if last else "middle",
            **({} if last else stiff_cost),
        )(
            far, near, from_far, from_near, dots, other, m, selector, swap, stiff,
            scalars, x, r, u, w, p, s, q, z,
        )
        scalars, x, r, u, w, p, s, q, z = result[:9]
        if not last:
            far, near = result[9:]
    everyone = lax.all_to_all(result[9], ("sub", "grp"), 0, 0, tiled=True)
    x, r = call(final_kernel, (field, field), count=8, name="final")(
        everyone, scalars, x, r, u, w, p, s
    )
    return (x[:, None, :], r[:, None, :])


def solution(mesh):
    in_specs = (
        P(None, "grp", "sub"),
        P(None, None, "grp", "sub"),
        P(None, None, None, "grp", "sub"),
        P("grp", "sub"),
        P("grp", "sub"),
        P(None, None, "grp", "sub"),
        P(None, "grp", "sub"),
        P("grp", None, "sub"),
    )
    out_specs = (P(None, "grp", "sub"), P(None, "grp", "sub"))
    return jax.shard_map(
        on_device, mesh=mesh, in_specs=in_specs, out_specs=out_specs, check_vma=False
    )
```

```python
import jax
import jax.numpy as jnp
from jax import lax
from jax.experimental import pallas as pl
from jax.experimental.pallas import tpu as pltpu
from jax.sharding import PartitionSpec as P

CORNER_DOF = 6
CORNERS_SUB = 4
ITERS = 5
ROWS = 8
NN = (((1,), (0,)), ((), ()))
NT = (((1,), (1,)), ((), ()))
F32 = jnp.float32
BF16 = jnp.bfloat16


def pieces_of(value):
    high = value.astype(BF16).astype(F32)
    rest = value - high
    middle = rest.astype(BF16).astype(F32)
    return [high, middle, rest - middle]


def exact_dot(value, table, dims):
    rows = value.shape[0]
    stacked = jnp.concatenate(pieces_of(value), axis=0).astype(BF16)
    product = lax.dot_general(stacked, table, dims, preferred_element_type=F32)
    return product[:rows] + product[rows : 2 * rows] + product[2 * rows :]


def lane_total(rows):
    return jnp.sum(rows, axis=1, keepdims=True)


def dot_rows(r, u, w, s=None, p=None):
    rows = [jnp.sum(r * u, axis=0, keepdims=True), jnp.sum(u * w, axis=0, keepdims=True)]
    if s is None:
        rows.append(jnp.zeros((ROWS - 2, r.shape[1]), F32))
    else:
        rows.append(jnp.sum(u * s, axis=0, keepdims=True))
        rows.append(jnp.sum(p * w, axis=0, keepdims=True))
        rows.append(jnp.zeros((ROWS - 4, r.shape[1]), F32))
    return jnp.concatenate(rows, axis=0)


def packed(rows):
    totals = jnp.broadcast_to(lane_total(rows), rows.shape)
    row = lax.broadcasted_iota(jnp.int32, rows.shape, 0)
    lane = lax.broadcasted_iota(jnp.int32, rows.shape, 1)
    return jnp.sum(jnp.where(row == lane, totals, 0.0), axis=0, keepdims=True)


def step_sizes(sums, before):
    norm, curvature, crossed, other = sums
    if before is None:
        beta = None
    else:
        beta = norm / before[0:1, 0:1]
        curvature = curvature + beta * (crossed + other) + beta * beta * before[1:2, 0:1]
    return norm / curvature, beta, norm, curvature


def collect_to(odd, vector, selector, near_ref, far_ref):
    iface, cells = vector.shape
    moved = exact_dot(vector, selector, NT)
    low = moved[:, :cells]
    high = vector - moved[:, cells:]
    near_ref[:iface] = jnp.where(odd, low, high)
    far_ref[:iface] = jnp.where(odd, high, low)


def spread_of(own, previous, selector):
    return own - exact_dot(jnp.concatenate([previous, own], axis=1), selector, NN)


def apply_blocks(blocks, vectors, out_ref):
    def step(index, carry):
        at = pl.ds(index * ROWS, ROWS)
        total = None
        for block, vector in zip(blocks, vectors):
            term = block[at].astype(F32) * vector[None]
            total = term if total is None else total + term
        out_ref[pl.ds(pl.multiple_of(index * ROWS, ROWS), ROWS)] = jnp.sum(total, axis=1)
        return carry

    lax.fori_loop(0, out_ref.shape[0] // ROWS, step, 0, unroll=True)


def table_kernel(neighbour_ref, column_ref, corner_ref, *refs):
    selector_ref, swap_ref, table_ref = refs[-3:]
    cells = swap_ref.shape[0]
    start = lax.axis_index("sub") * cells
    def one_hot(row, count):
        places = lax.broadcasted_iota(jnp.int32, (count, row.shape[1]), 0)
        return jnp.where(places == row, 1.0, 0.0).astype(BF16)

    neighbour = neighbour_ref[...]
    slots = jnp.where(neighbour < 0, -1, neighbour - (start - cells))
    selector_ref[...] = one_hot(slots, selector_ref.shape[0])
    swap_ref[...] = one_hot(column_ref[...] - start, swap_ref.shape[0])
    chunk = 128

    def step(index, carry):
        row = corner_ref[...] - index * chunk
        table_ref[pl.ds(pl.multiple_of(index * chunk, chunk), chunk)] = one_hot(row, chunk)
        return carry

    lax.fori_loop(0, table_ref.shape[0] // chunk, step, 0)


def stiffen(odd, own, previous, selector_ref, swap_ref, stiffness_ref, stiff_ref, near_ref, far_ref):
    gap = spread_of(own, previous, selector_ref[...])
    taken = exact_dot(gap, swap_ref[...], NN)
    apply_blocks([stiffness_ref.at[0], stiffness_ref.at[1]], [gap, taken], stiff_ref)
    collect_to(odd, stiff_ref[...], selector_ref[...], near_ref, far_ref)


def first_kernel(
    own_ref, previous_ref, selector_ref, swap_ref, stiffness_ref, far_ref, near_ref, stiff_ref
):
    iface, cells = own_ref.shape
    odd = lax.axis_index("sub") % 2 == 1
    stiffen(
        odd, own_ref[...], previous_ref[...], selector_ref, swap_ref, stiffness_ref, stiff_ref, near_ref, far_ref
    )
    near_ref[iface:] = jnp.zeros((ROWS, cells), F32)
    far_ref[iface:] = jnp.zeros((ROWS, cells), F32)


def arrived(odd, far_ref, near_ref, from_far_ref, from_near_ref, iface):
    near, far = near_ref[:iface], far_ref[:iface]
    from_near, from_far = from_near_ref[:iface], from_far_ref[:iface]
    own = jnp.where(odd, far - from_far, near - from_near)
    previous = jnp.where(odd, from_near - near, from_far - far)
    return own, previous


def second_kernel(
    far_ref, near_ref, from_far_ref, from_near_ref, r_ref, u_ref, selector_ref, swap_ref, stiffness_ref,
    far_out, near_out, w_out, stiff_ref,
):
    iface = r_ref.shape[0]
    odd = lax.axis_index("sub") % 2 == 1
    w, w_previous = arrived(odd, far_ref, near_ref, from_far_ref, from_near_ref, iface)
    w_out[0] = w
    w_out[1] = w_previous
    dots = dot_rows(r_ref[...], u_ref[...], w)
    near_out[iface:] = dots
    far_out[iface:] = dots
    stiffen(odd, w, w_previous, selector_ref, swap_ref, stiffness_ref, stiff_ref, near_out, far_out)


def update(first, last, refs, m, n, n_previous, totals):
    scalars_in, x_in, r_in, u_in, w_in, p_in, s_in, q_in, z_in = refs[:9]
    scalars_out, x_out, r_out, u_out, w_out, p_out, s_out, q_out, z_out = refs[9:]
    sums = lane_total(totals)
    sums = [sums[k : k + 1] for k in range(4)]
    alpha, beta, norm, curvature = step_sizes(sums, None if first else scalars_in[...])
    cells = m.shape[1]
    scalars_out[...] = jnp.concatenate(
        [
            jnp.broadcast_to(norm, (1, cells)),
            jnp.broadcast_to(curvature, (1, cells)),
            jnp.zeros((ROWS - 2, cells), F32),
        ],
        axis=0,
    )

    def turned(fresh, kept):
        return fresh if first else fresh + beta * kept[...]

    u, w = u_in[...], w_in[0]
    p = turned(u, p_in)
    s = turned(w, s_in)
    q = turned(m, q_in)
    z = turned(n, None if first else z_in.at[0])
    p_out[...] = p
    s_out[...] = s
    x_out[...] = alpha * p if first else x_in[...] + alpha * p
    r = r_in[...] - alpha * s
    u = u - alpha * q
    w = w - alpha * z
    r_out[...] = r
    u_out[...] = u
    w_out[0] = w
    previous = None
    if not last:
        z_previous = turned(n_previous, None if first else z_in.at[1])
        previous = w_in[1] - alpha * z_previous
        q_out[...] = q
        z_out[0] = z
        z_out[1] = z_previous
        w_out[1] = previous
    return dot_rows(r, u, w, s, p), w, previous


def middle_kernel(first, last, *refs):
    (far_ref, near_ref, from_far_ref, from_near_ref, dots_ref, dots_other_ref, m_ref) = refs[:7]
    (selector_ref, swap_ref, stiffness_ref) = refs[7:10]
    ins = list(refs[10:19])
    outs = list(refs[19:28])
    m = m_ref[...]
    iface = m.shape[0]
    odd = lax.axis_index("sub") % 2 == 1
    n, n_previous = arrived(odd, far_ref, near_ref, from_far_ref, from_near_ref, iface)
    dots, w, previous = update(
        first, last, ins + outs, m, n, n_previous, dots_ref[...] + dots_other_ref[...]
    )
    if last:
        dots_out = refs[28]
        dots_out[...] = jnp.broadcast_to(packed(dots)[None], dots_out.shape)
    else:
        far_out, near_out, stiff_ref = refs[28:31]
        near_out[iface:] = dots
        far_out[iface:] = dots
        stiffen(odd, w, previous, selector_ref, swap_ref, stiffness_ref, stiff_ref, near_out, far_out)


def corner_kernel(
    ranks, far_ref, near_ref, from_far_ref, from_near_ref, selector_ref, operators_ref, table_ref,
    m_out, gap_out, *rest,
):
    dots_sent, outs, (dots_out, sums_ref) = rest[0], rest[1 : ranks + 1], rest[ranks + 1 :]
    iface, cells = m_out.shape
    odd = lax.axis_index("sub") % 2 == 1
    own, previous = arrived(odd, far_ref, near_ref, from_far_ref, from_near_ref, iface)
    m_out[...] = own
    dots_sent[...] = jnp.zeros_like(dots_sent)
    dots = near_ref[iface:] + from_near_ref[iface:]
    dots_out[...] = dots
    dots_sent[:, :cells] = dots
    gap = spread_of(own, previous, selector_ref[...])
    gap_out[...] = gap
    parts = []
    for corner in range(CORNERS_SUB):
        at = slice(corner * CORNER_DOF, (corner + 1) * CORNER_DOF)
        part = jnp.sum(operators_ref[at].astype(F32) * gap[None], axis=1)
        parts.append(jnp.concatenate([part, jnp.zeros((ROWS - CORNER_DOF, cells), F32)], axis=0))
    sums_ref[...] = exact_dot(jnp.concatenate(parts, axis=1), table_ref[...], NT)
    owned = sums_ref.shape[1] // ranks
    for distance in range(ranks):
        rank = lax.axis_index("grp") ^ (ranks - 1 - distance)
        outs[distance][...] = sums_ref[:, pl.ds(pl.multiple_of(rank * owned, 128), owned)]


def local_kernel(gap_ref, inverse_ref, local_ref):
    apply_blocks([inverse_ref], [gap_ref[...]], local_ref)


def coarse_kernel(ranks, coarse_ref, dots_ref, other_ref, *rest):
    pieces, (solved_ref, sums_ref) = rest[:ranks], rest[ranks:]
    cells = dots_ref.shape[1]
    for distance in range(ranks):
        rank = lax.axis_index("grp") ^ distance
        sums_ref[rank] = pieces[ranks - 1 - distance][...]
    total = sums_ref[0]
    for rank in range(1, ranks):
        total = total + sums_ref[rank]
    blocks, order = coarse_ref.shape[0], coarse_ref.shape[1]
    width = order // CORNER_DOF
    columns = []
    for block in range(blocks):
        lanes = slice(block * width, (block + 1) * width)
        row = jnp.concatenate([total[j : j + 1, lanes] for j in range(CORNER_DOF)], axis=1)
        parts = pieces_of(row) + [jnp.zeros((ROWS - 3, order), F32)]
        stacked = jnp.concatenate(parts, axis=0).astype(BF16)
        product = lax.dot_general(stacked, coarse_ref[block], NT, preferred_element_type=F32)
        result = product[0:1] + product[1:2] + product[2:3]
        rows = [result[:, j * width : (j + 1) * width] for j in range(CORNER_DOF)]
        columns.append(jnp.concatenate(rows, axis=0))
    solved = jnp.concatenate(columns, axis=1)
    dots = dots_ref[...] + other_ref[:, :cells]
    rows = [solved]
    for first in (0, 2):
        lanes = [dots[first : first + 1], dots[first + 1 : first + 2]]
        if solved.shape[1] > 2 * cells:
            lanes.append(jnp.zeros((1, solved.shape[1] - 2 * cells), F32))
        rows.append(jnp.concatenate(lanes, axis=1))
    solved_ref[...] = jnp.concatenate(rows, axis=0)


def lift_kernel(ranks, local_ref, operators_ref, table_ref, selector_ref, *rest):
    pieces, (far_ref, near_ref, dots_out, values_ref) = rest[:ranks], rest[ranks:]
    cells = local_ref.shape[1]
    owned = values_ref.shape[1] // ranks
    for distance in range(ranks):
        rank = lax.axis_index("grp") ^ distance
        values_ref[:, pl.ds(pl.multiple_of(rank * owned, 128), owned)] = pieces[distance][...]
    values = values_ref[...]
    tail = values[CORNER_DOF:, :owned]
    for rank in range(1, ranks):
        tail = tail + values[CORNER_DOF:, rank * owned : (rank + 1) * owned]
    dots_out[...] = jnp.concatenate(
        [
            tail[0:1, :cells],
            tail[0:1, cells : 2 * cells],
            tail[1:2, :cells],
            tail[1:2, cells : 2 * cells],
            jnp.zeros((ROWS - 4, cells), F32),
        ],
        axis=0,
    )
    picked = exact_dot(values, table_ref[...], NN)
    lifted = local_ref[...]
    for corner in range(CORNERS_SUB):
        lanes = slice(corner * cells, (corner + 1) * cells)
        for dof in range(CORNER_DOF):
            operator = operators_ref[corner * CORNER_DOF + dof].astype(F32)
            lifted = lifted + operator * picked[dof : dof + 1, lanes]
    collect_to(lax.axis_index("sub") % 2 == 1, lifted, selector_ref[...], near_ref, far_ref)


def final_kernel(dots_ref, scalars_ref, x_ref, r_ref, u_ref, w_ref, p_ref, s_ref, x_out, r_out):
    totals = jnp.sum(dots_ref[...], axis=0)
    sums = [totals[:, k : k + 1] for k in range(4)]
    alpha, beta, _, _ = step_sizes(sums, scalars_ref[...])
    x_out[...] = x_ref[...] + alpha * (u_ref[...] + beta * p_ref[...])
    r_out[...] = r_ref[...] - alpha * (w_ref[0] + beta * s_ref[...])


def shifted(block, distance):
    count = lax.axis_size("sub")
    route = [(i, i + distance) for i in range(count) if 0 <= i + distance < count]
    return lax.ppermute(block, "sub", route)


def swapped(block, bit):
    return lax.ppermute(block, "sub", [(i, i ^ bit) for i in range(lax.axis_size("sub"))])


def swapped_far(block):
    inner = range(1, lax.axis_size("sub") - 1)
    return lax.ppermute(block, "sub", [(i, i + 1 if i % 2 else i - 1) for i in inner])


def exchanged(block, distance):
    return lax.ppermute(block, "grp", [(i, i ^ distance) for i in range(lax.axis_size("grp"))])


def shape(*dims, dtype=F32):
    return jax.ShapeDtypeStruct(dims, dtype)


def call(kernel, out_shape, count=0, scratch=(), flops=0, moved=0, name=None):
    specs = [pl.BlockSpec(memory_space=pltpu.VMEM)] * count
    out_specs = jax.tree.map(lambda _: pl.BlockSpec(memory_space=pltpu.VMEM), out_shape)
    return pl.pallas_call(
        kernel,
        out_shape=out_shape,
        in_specs=specs,
        out_specs=out_specs,
        scratch_shapes=list(scratch),
        compiler_params=pltpu.CompilerParams(vmem_limit_bytes=24 * 1024 * 1024),
        cost_estimate=pl.CostEstimate(flops=flops, bytes_accessed=moved, transcendentals=0),
        name=name,
    )


def on_device(
    gap_data,
    local_inverse,
    stiffness,
    stiff_column,
    neighbour,
    corner_ops,
    corner_index,
    coarse_inverse,
):
    iface, _, cells = gap_data.shape
    ranks = lax.axis_size("grp")
    sub_count = lax.axis_size("sub")
    right_side = gap_data[:, 0, :]
    inverse = local_inverse[:, :, 0, :]
    stiff = stiffness[:, :, :, 0, :]
    operators = corner_ops[:, :, 0, :]
    blocks_own, order = coarse_inverse.shape[:2]
    owned = blocks_own * (order // CORNER_DOF)
    group = owned * ranks
    corners = corner_index.reshape(1, CORNERS_SUB * cells)

    selector, swap, table = call(
        table_kernel,
        (
            shape(2 * cells, cells, dtype=BF16),
            shape(cells, cells, dtype=BF16),
            shape(group, CORNERS_SUB * cells, dtype=BF16),
        ),
        count=6,
        name="tables",
    )(neighbour, stiff_column, corners, stiff, operators, right_side)

    field = shape(iface, cells)
    pair = shape(2, iface, cells)
    message = shape(iface + ROWS, cells)
    rows = shape(ROWS, cells)
    piece = shape(ROWS, owned)
    stiff_scratch = [pltpu.VMEM((iface, cells), F32)]
    stiff_cost = dict(flops=4 * iface * iface * cells, moved=4 * iface * iface * cells)

    def apply_operator(near, far):
        from_far, from_near = swapped_far(far), swapped(near, 1)
        m, gap, sent, *parts, dots = call(
            lambda *refs: corner_kernel(ranks, *refs),
            (field, field) + (piece,) * (ranks + 1) + (rows,),
            count=7,
            scratch=[pltpu.VMEM((ROWS, group), F32)],
            flops=2 * 24 * iface * cells,
            moved=2 * 24 * iface * cells + group * CORNERS_SUB * cells * 2,
            name="corners",
        )(far, near, from_far, from_near, selector, operators, table)
        arrivals = [exchanged(parts[ranks - 1 - d], d) for d in range(ranks - 1, 0, -1)] + [parts[ranks - 1]]
        local = call(
            local_kernel,
            field,
            count=2,
            flops=2 * iface * iface * cells,
            moved=2 * iface * iface * cells,
            name="local",
        )(gap, inverse)
        other = swapped(sent, 2)
        solved = call(
            lambda *refs: coarse_kernel(ranks, *refs),
            piece,
            count=3 + ranks,
            scratch=[pltpu.VMEM((ranks, ROWS, owned), F32)],
            flops=2 * blocks_own * order * order,
            moved=2 * blocks_own * order * order,
            name="coarse",
        )(coarse_inverse, dots, other, *arrivals)
        values = [solved] + [exchanged(solved, d) for d in range(1, ranks)]
        far, near, dots = call(
            lambda *refs: lift_kernel(ranks, *refs),
            (field, field, rows),
            count=4 + ranks,
            scratch=[pltpu.VMEM((ROWS, group), F32)],
            flops=2 * 24 * iface * cells,
            moved=2 * 24 * iface * cells + group * CORNERS_SUB * cells * 2,
            name="lift",
        )(local, operators, table, selector, *values)
        return m, near, far, dots

    previous = shifted(right_side, 1)
    far, near = call(
        first_kernel, (message, message), count=5, scratch=stiff_scratch, name="first", **stiff_cost
    )(right_side, previous, selector, swap, stiff)
    u, near, far, dots = apply_operator(near, far)
    r = right_side
    from_far, from_near = swapped_far(far), swapped(near, 1)
    far, near, w = call(
        second_kernel,
        (message, message, pair),
        count=9,
        scratch=stiff_scratch,
        name="second",
        **stiff_cost,
    )(far, near, from_far, from_near, r, u, selector, swap, stiff)

    scalars, x, p, s, q, z = [jnp.zeros((ROWS, cells), F32)] + [r] * 4 + [w]
    for step in range(ITERS - 1):
        first, last = step == 0, step == ITERS - 2
        m, near, far, dots = apply_operator(near, far)
        from_far, from_near, other = swapped_far(far), swapped(near, 1), swapped(dots, 4)
        bit = 8
        while bit < sub_count:
            dots = dots + other
            other = swapped(dots, bit)
            bit *= 2
        outs = (rows, field, field, field, pair, field, field, field, pair)
        if last:
            count = sub_count * ranks
            outs += (shape(count, 1, cells),)
        else:
            outs += (message, message)
        result = call(
            lambda *refs, first=first, last=last: middle_kernel(first, last, *refs),
            outs,
            count=19,
            scratch=() if last else stiff_scratch,
            name="last" if last else "middle",
            **({} if last else stiff_cost),
        )(
            far, near, from_far, from_near, dots, other, m, selector, swap, stiff,
            scalars, x, r, u, w, p, s, q, z,
        )
        scalars, x, r, u, w, p, s, q, z = result[:9]
        if not last:
            far, near = result[9:]
    everyone = lax.all_to_all(result[9], ("sub", "grp"), 0, 0, tiled=True)
    x, r = call(final_kernel, (field, field), count=8, name="final")(
        everyone, scalars, x, r, u, w, p, s
    )
    return (x[:, None, :], r[:, None, :])


def solution(mesh):
    in_specs = (
        P(None, "grp", "sub"),
        P(None, None, "grp", "sub"),
        P(None, None, None, "grp", "sub"),
        P("grp", "sub"),
        P("grp", "sub"),
        P(None, None, "grp", "sub"),
        P(None, "grp", "sub"),
        P("grp", None, "sub"),
    )
    out_specs = (P(None, "grp", "sub"), P(None, "grp", "sub"))
    return jax.shard_map(
        on_device, mesh=mesh, in_specs=in_specs, out_specs=out_specs, check_vma=False
    )
```

```python
import jax
import jax.numpy as jnp
from jax import lax
from jax.experimental import pallas as pl
from jax.experimental.pallas import tpu as pltpu
from jax.sharding import PartitionSpec as P

CORNER_DOF = 6
CORNERS_SUB = 4
ITERS = 5
ROWS = 8
STATES = 12
NN = (((1,), (0,)), ((), ()))
NT = (((1,), (1,)), ((), ()))
F32 = jnp.float32
BF16 = jnp.bfloat16


def pieces_of(value):
    high = value.astype(BF16).astype(F32)
    rest = value - high
    middle = rest.astype(BF16).astype(F32)
    return [high, middle, rest - middle]


def exact_dot(value, table, dims):
    rows = value.shape[0]
    stacked = jnp.concatenate(pieces_of(value), axis=0).astype(BF16)
    product = lax.dot_general(stacked, table, dims, preferred_element_type=F32)
    return product[:rows] + product[rows : 2 * rows] + product[2 * rows :]


def lane_total(rows):
    return jnp.sum(rows, axis=1, keepdims=True)


def dot_rows(r, u, w, s=None, p=None):
    rows = [jnp.sum(r * u, axis=0, keepdims=True), jnp.sum(u * w, axis=0, keepdims=True)]
    if s is None:
        rows.append(jnp.zeros((ROWS - 2, r.shape[1]), F32))
    else:
        rows.append(jnp.sum(u * s, axis=0, keepdims=True))
        rows.append(jnp.sum(p * w, axis=0, keepdims=True))
        rows.append(jnp.zeros((ROWS - 4, r.shape[1]), F32))
    return jnp.concatenate(rows, axis=0)


def packed(rows):
    row = lax.broadcasted_iota(jnp.int32, rows.shape, 0)
    lane = lax.broadcasted_iota(jnp.int32, rows.shape, 1)
    return jnp.sum(jnp.where(row == lane, lane_total(rows), 0.0), axis=0, keepdims=True)


def step_sizes(sums, before):
    norm, curvature, crossed, other = sums
    if before is None:
        beta = None
    else:
        beta = norm / before[0:1, 0:1]
        curvature = curvature + beta * (crossed + other) + beta * beta * before[1:2, 0:1]
    return norm / curvature, beta, norm, curvature


def collect_to(odd, vector, selector, near_ref, far_ref):
    iface, cells = vector.shape
    moved = exact_dot(vector, selector, NT)
    low = moved[:, :cells]
    high = vector - moved[:, cells:]
    near_ref[:iface] = jnp.where(odd, low, high)
    far_ref[:iface] = jnp.where(odd, high, low)


def spread_of(own, previous, selector):
    return own - exact_dot(jnp.concatenate([previous, own], axis=1), selector, NN)


def apply_blocks(blocks, vectors, out_ref):
    def step(index, carry):
        at = pl.ds(index * ROWS, ROWS)
        total = None
        for block, vector in zip(blocks, vectors):
            term = block[at].astype(F32) * vector[None]
            total = term if total is None else total + term
        out_ref[pl.ds(pl.multiple_of(index * ROWS, ROWS), ROWS)] = jnp.sum(total, axis=1)
        return carry

    lax.fori_loop(0, out_ref.shape[0] // ROWS, step, 0, unroll=True)


def table_kernel(neighbour_ref, column_ref, corner_ref, *refs):
    selector_ref, swap_ref, table_ref = refs[-3:]
    cells = swap_ref.shape[0]
    start = lax.axis_index("sub") * cells
    def one_hot(row, count):
        places = lax.broadcasted_iota(jnp.int32, (count, row.shape[1]), 0)
        return jnp.where(places == row, 1.0, 0.0).astype(BF16)

    neighbour = neighbour_ref[...]
    slots = jnp.where(neighbour < 0, -1, neighbour - (start - cells))
    selector_ref[...] = one_hot(slots, selector_ref.shape[0])
    swap_ref[...] = one_hot(column_ref[...] - start, swap_ref.shape[0])
    chunk = 128

    def step(index, carry):
        row = corner_ref[...] - index * chunk
        table_ref[pl.ds(pl.multiple_of(index * chunk, chunk), chunk)] = one_hot(row, chunk)
        return carry

    lax.fori_loop(0, table_ref.shape[0] // chunk, step, 0)


def stiffen(odd, own, previous, selector_ref, swap_ref, stiffness_ref, stiff_ref, near_ref, far_ref):
    gap = spread_of(own, previous, selector_ref[...])
    taken = exact_dot(gap, swap_ref[...], NN)
    apply_blocks([stiffness_ref.at[0], stiffness_ref.at[1]], [gap, taken], stiff_ref)
    collect_to(odd, stiff_ref[...], selector_ref[...], near_ref, far_ref)


def first_kernel(
    own_ref, previous_ref, selector_ref, swap_ref, stiffness_ref, far_ref, near_ref, stiff_ref
):
    iface, cells = own_ref.shape
    odd = lax.axis_index("sub") % 2 == 1
    stiffen(
        odd, own_ref[...], previous_ref[...], selector_ref, swap_ref, stiffness_ref, stiff_ref, near_ref, far_ref
    )
    near_ref[iface:] = jnp.zeros((ROWS, cells), F32)
    far_ref[iface:] = jnp.zeros((ROWS, cells), F32)


def arrived(odd, far_ref, near_ref, from_far_ref, from_near_ref, iface):
    near, far = near_ref[:iface], far_ref[:iface]
    from_near, from_far = from_near_ref[:iface], from_far_ref[:iface]
    own = jnp.where(odd, far - from_far, near - from_near)
    previous = jnp.where(odd, from_near - near, from_far - far)
    return own, previous


def second_kernel(
    far_ref, near_ref, from_far_ref, from_near_ref, r_ref, u_ref, selector_ref, swap_ref, stiffness_ref,
    far_out, near_out, w_out, stiff_ref,
):
    iface = r_ref.shape[0]
    odd = lax.axis_index("sub") % 2 == 1
    w, w_previous = arrived(odd, far_ref, near_ref, from_far_ref, from_near_ref, iface)
    w_out[0] = w
    w_out[1] = w_previous
    dots = dot_rows(r_ref[...], u_ref[...], w)
    near_out[iface:] = dots
    far_out[iface:] = dots
    stiffen(odd, w, w_previous, selector_ref, swap_ref, stiffness_ref, stiff_ref, near_out, far_out)


def update(first, refs, m, gap, n, n_previous, totals):
    scalars_in, x_in, r_in, u_in, w_in, p_in, s_in, q_in, z_in, gap_u_in, gap_p_in, gap_q_in = refs[:STATES]
    scalars_out, x_out, r_out, u_out, w_out, p_out, s_out, q_out, z_out, gap_u_out, gap_p_out, gap_q_out = refs[STATES:]
    sums = lane_total(totals)
    sums = [sums[k : k + 1] for k in range(4)]
    alpha, beta, norm, curvature = step_sizes(sums, None if first else scalars_in[...])
    cells = m.shape[1]
    scalars_out[...] = jnp.concatenate(
        [
            jnp.broadcast_to(norm, (1, cells)),
            jnp.broadcast_to(curvature, (1, cells)),
            jnp.zeros((ROWS - 2, cells), F32),
        ],
        axis=0,
    )

    def turned(fresh, kept):
        return fresh if first else fresh + beta * kept[...]

    u, w = u_in[...], w_in[0]
    p = turned(u, p_in)
    s = turned(w, s_in)
    q = turned(m, q_in)
    z = turned(n, None if first else z_in.at[0])
    p_out[...] = p
    s_out[...] = s
    x_out[...] = alpha * p if first else x_in[...] + alpha * p
    r = r_in[...] - alpha * s
    u = u - alpha * q
    w = w - alpha * z
    r_out[...] = r
    u_out[...] = u
    w_out[0] = w
    z_previous = turned(n_previous, None if first else z_in.at[1])
    previous = w_in[1] - alpha * z_previous
    q_out[...] = q
    z_out[0] = z
    z_out[1] = z_previous
    w_out[1] = previous
    gap_u = gap_u_in[...]
    gap_q = turned(gap, gap_q_in)
    gap_p_out[...] = turned(gap_u, gap_p_in)
    gap_q_out[...] = gap_q
    gap_u_out[...] = gap_u - alpha * gap_q
    return dot_rows(r, u, w, s, p), w, previous


def middle_kernel(first, *refs):
    (far_ref, near_ref, from_far_ref, from_near_ref, dots_ref, dots_other_ref, m_ref, gap_ref) = refs[:8]
    (selector_ref, swap_ref, stiffness_ref) = refs[8:11]
    states = list(refs[11 : 11 + 2 * STATES])
    far_out, near_out, stiff_ref = refs[11 + 2 * STATES :]
    m = m_ref[...]
    iface = m.shape[0]
    odd = lax.axis_index("sub") % 2 == 1
    n, n_previous = arrived(odd, far_ref, near_ref, from_far_ref, from_near_ref, iface)
    dots, w, previous = update(
        first, states, m, gap_ref[...], n, n_previous, dots_ref[...] + dots_other_ref[...]
    )
    near_out[iface:] = dots
    far_out[iface:] = dots
    stiffen(odd, w, previous, selector_ref, swap_ref, stiffness_ref, stiff_ref, near_out, far_out)


def corner_kernel(
    ranks, far_ref, near_ref, from_far_ref, from_near_ref, selector_ref, operators_ref, table_ref,
    m_out, gap_out, *rest,
):
    dots_sent, outs, (dots_out, sums_ref) = rest[0], rest[1 : ranks + 1], rest[ranks + 1 :]
    iface, cells = m_out.shape
    odd = lax.axis_index("sub") % 2 == 1
    own, previous = arrived(odd, far_ref, near_ref, from_far_ref, from_near_ref, iface)
    m_out[...] = own
    dots_sent[...] = jnp.zeros_like(dots_sent)
    dots = near_ref[iface:] + from_near_ref[iface:]
    dots_out[...] = dots
    dots_sent[:, :cells] = dots
    gap = spread_of(own, previous, selector_ref[...])
    gap_out[...] = gap
    parts = []
    for corner in range(CORNERS_SUB):
        at = slice(corner * CORNER_DOF, (corner + 1) * CORNER_DOF)
        part = jnp.sum(operators_ref[at].astype(F32) * gap[None], axis=1)
        parts.append(jnp.concatenate([part, jnp.zeros((ROWS - CORNER_DOF, cells), F32)], axis=0))
    sums_ref[...] = exact_dot(jnp.concatenate(parts, axis=1), table_ref[...], NT)
    owned = sums_ref.shape[1] // ranks
    for distance in range(ranks):
        rank = lax.axis_index("grp") ^ (ranks - 1 - distance)
        outs[distance][...] = sums_ref[:, pl.ds(pl.multiple_of(rank * owned, 128), owned)]


def local_kernel(gap_ref, inverse_ref, local_ref):
    apply_blocks([inverse_ref], [gap_ref[...]], local_ref)


def coarse_kernel(ranks, coarse_ref, dots_ref, other_ref, *rest):
    pieces, (solved_ref, sums_ref) = rest[:ranks], rest[ranks:]
    cells = dots_ref.shape[1]
    for distance in range(ranks):
        rank = lax.axis_index("grp") ^ distance
        sums_ref[rank] = pieces[ranks - 1 - distance][...]
    total = sums_ref[0]
    for rank in range(1, ranks):
        total = total + sums_ref[rank]
    blocks, order = coarse_ref.shape[0], coarse_ref.shape[1]
    width = order // CORNER_DOF
    columns = []
    for block in range(blocks):
        lanes = slice(block * width, (block + 1) * width)
        row = jnp.concatenate([total[j : j + 1, lanes] for j in range(CORNER_DOF)], axis=1)
        parts = pieces_of(row) + [jnp.zeros((ROWS - 3, order), F32)]
        stacked = jnp.concatenate(parts, axis=0).astype(BF16)
        product = lax.dot_general(stacked, coarse_ref[block], NT, preferred_element_type=F32)
        result = product[0:1] + product[1:2] + product[2:3]
        rows = [result[:, j * width : (j + 1) * width] for j in range(CORNER_DOF)]
        columns.append(jnp.concatenate(rows, axis=0))
    solved = jnp.concatenate(columns, axis=1)
    dots = dots_ref[...] + other_ref[:, :cells]
    rows = [solved]
    for first in (0, 2):
        lanes = [dots[first : first + 1], dots[first + 1 : first + 2]]
        if solved.shape[1] > 2 * cells:
            lanes.append(jnp.zeros((1, solved.shape[1] - 2 * cells), F32))
        rows.append(jnp.concatenate(lanes, axis=1))
    solved_ref[...] = jnp.concatenate(rows, axis=0)


def lift_kernel(ranks, local_ref, operators_ref, table_ref, selector_ref, *rest):
    pieces, (far_ref, near_ref, dots_out, lifted_ref, values_ref) = rest[:ranks], rest[ranks:]
    cells = local_ref.shape[1]
    owned = values_ref.shape[1] // ranks
    for distance in range(ranks):
        rank = lax.axis_index("grp") ^ distance
        values_ref[:, pl.ds(pl.multiple_of(rank * owned, 128), owned)] = pieces[distance][...]
    values = values_ref[...]
    tail = values[CORNER_DOF:, :owned]
    for rank in range(1, ranks):
        tail = tail + values[CORNER_DOF:, rank * owned : (rank + 1) * owned]
    dots_out[...] = jnp.concatenate(
        [
            tail[0:1, :cells],
            tail[0:1, cells : 2 * cells],
            tail[1:2, :cells],
            tail[1:2, cells : 2 * cells],
            jnp.zeros((ROWS - 4, cells), F32),
        ],
        axis=0,
    )
    picked = exact_dot(values, table_ref[...], NN)
    lifted = local_ref[...]
    for corner in range(CORNERS_SUB):
        lanes = slice(corner * cells, (corner + 1) * cells)
        for dof in range(CORNER_DOF):
            operator = operators_ref[corner * CORNER_DOF + dof].astype(F32)
            lifted = lifted + operator * picked[dof : dof + 1, lanes]
    lifted_ref[...] = lifted
    collect_to(lax.axis_index("sub") % 2 == 1, lifted, selector_ref[...], near_ref, far_ref)


def gram_kernel(
    r_ref, u_ref, w_ref, p_ref, s_ref, q_ref, z_ref, m_ref, gap_u_ref, gap_p_ref, gap_q_ref, gap_ref, lifted_ref, out_ref
):
    left = [u_ref[...], m_ref[...], q_ref[...], p_ref[...]]
    gaps = [gap_u_ref[...], gap_ref[...], gap_q_ref[...], gap_p_ref[...]]
    w, z, s = w_ref[0], z_ref[0], s_ref[...]
    r, lifted = r_ref[...], lifted_ref[...]
    products = []
    for v, gap in zip(left, gaps):
        products += [v * w, gap * lifted, v * z, v * s]
    products += [r * v for v in left[:3]]
    rows = [jnp.sum(product, axis=0, keepdims=True) for product in products]
    rows.append(jnp.zeros((-len(rows) % ROWS, r.shape[1]), F32))
    out_ref[...] = jnp.broadcast_to(packed(jnp.concatenate(rows, axis=0))[None], out_ref.shape)


def final_kernel(
    dots_ref, scalars_ref, x_ref, r_ref, u_ref, w_ref, p_ref, s_ref, q_ref, z_ref, m_ref,
    far_ref, near_ref, from_far_ref, from_near_ref, x_out, r_out,
):
    totals = jnp.sum(dots_ref[...], axis=0)
    gram = [[totals[:, 4 * i + k : 4 * i + k + 1] for k in range(4)] for i in range(4)]
    with_r = [totals[:, 16 + i : 17 + i] for i in range(3)]

    def form(first, second):
        total = None
        for i, left in first.items():
            row = None
            for k, right in second.items():
                term = gram[i][k] * right
                row = term if row is None else row + term
            total = left * row if total is None else total + left * row
        return total

    norm = with_r[0]
    beta = norm / scalars_ref[0:1, 0:1]
    one = jnp.ones_like(norm)
    turned = {0: one, 3: beta}
    alpha = norm / form(turned, turned)
    stepped = {0: one, 1: -alpha, 2: -alpha * beta}
    norm_next = with_r[0] + stepped[1] * with_r[1] + stepped[2] * with_r[2] - alpha * form(stepped, turned)
    beta_next = norm_next / norm
    turned_next = {0: one + beta_next, 1: stepped[1], 2: stepped[2], 3: beta_next * beta}
    alpha_next = norm_next / form(turned_next, turned_next)

    odd = lax.axis_index("sub") % 2 == 1
    n, _ = arrived(odd, far_ref, near_ref, from_far_ref, from_near_ref, r_ref.shape[0])
    p = u_ref[...] + beta * p_ref[...]
    s = w_ref[0] + beta * s_ref[...]
    u = u_ref[...] - alpha * (m_ref[...] + beta * q_ref[...])
    w = w_ref[0] - alpha * (n + beta * z_ref[0])
    x_out[...] = x_ref[...] + alpha * p + alpha_next * (u + beta_next * p)
    r_out[...] = r_ref[...] - alpha * s - alpha_next * (w + beta_next * s)


def shifted(block, distance):
    count = lax.axis_size("sub")
    route = [(i, i + distance) for i in range(count) if 0 <= i + distance < count]
    return lax.ppermute(block, "sub", route)


def swapped(block, bit):
    return lax.ppermute(block, "sub", [(i, i ^ bit) for i in range(lax.axis_size("sub"))])


def swapped_far(block):
    inner = range(1, lax.axis_size("sub") - 1)
    return lax.ppermute(block, "sub", [(i, i + 1 if i % 2 else i - 1) for i in inner])


def exchanged(block, distance):
    return lax.ppermute(block, "grp", [(i, i ^ distance) for i in range(lax.axis_size("grp"))])


def shape(*dims, dtype=F32):
    return jax.ShapeDtypeStruct(dims, dtype)


def call(kernel, out_shape, count=0, scratch=(), flops=0, moved=0, name=None):
    specs = [pl.BlockSpec(memory_space=pltpu.VMEM)] * count
    out_specs = jax.tree.map(lambda _: pl.BlockSpec(memory_space=pltpu.VMEM), out_shape)
    return pl.pallas_call(
        kernel,
        out_shape=out_shape,
        in_specs=specs,
        out_specs=out_specs,
        scratch_shapes=list(scratch),
        compiler_params=pltpu.CompilerParams(vmem_limit_bytes=24 * 1024 * 1024),
        cost_estimate=pl.CostEstimate(flops=flops, bytes_accessed=moved, transcendentals=0),
        name=name,
    )


def on_device(
    gap_data,
    local_inverse,
    stiffness,
    stiff_column,
    neighbour,
    corner_ops,
    corner_index,
    coarse_inverse,
):
    iface, _, cells = gap_data.shape
    ranks = lax.axis_size("grp")
    sub_count = lax.axis_size("sub")
    right_side = gap_data[:, 0, :]
    inverse = local_inverse[:, :, 0, :]
    stiff = stiffness[:, :, :, 0, :]
    operators = corner_ops[:, :, 0, :]
    blocks_own, order = coarse_inverse.shape[:2]
    owned = blocks_own * (order // CORNER_DOF)
    group = owned * ranks
    corners = corner_index.reshape(1, CORNERS_SUB * cells)

    selector, swap, table = call(
        table_kernel,
        (
            shape(2 * cells, cells, dtype=BF16),
            shape(cells, cells, dtype=BF16),
            shape(group, CORNERS_SUB * cells, dtype=BF16),
        ),
        count=6,
        name="tables",
    )(neighbour, stiff_column, corners, stiff, operators, right_side)

    field = shape(iface, cells)
    pair = shape(2, iface, cells)
    message = shape(iface + ROWS, cells)
    rows = shape(ROWS, cells)
    piece = shape(ROWS, owned)
    stiff_scratch = [pltpu.VMEM((iface, cells), F32)]
    stiff_cost = dict(flops=4 * iface * iface * cells, moved=4 * iface * iface * cells)

    def apply_operator(near, far, reduce=True):
        from_far, from_near = swapped_far(far), swapped(near, 1)
        m, gap, sent, *parts, dots = call(
            lambda *refs: corner_kernel(ranks, *refs),
            (field, field) + (piece,) * (ranks + 1) + (rows,),
            count=7,
            scratch=[pltpu.VMEM((ROWS, group), F32)],
            flops=2 * 24 * iface * cells,
            moved=2 * 24 * iface * cells + group * CORNERS_SUB * cells * 2,
            name="corners",
        )(far, near, from_far, from_near, selector, operators, table)
        arrivals = [exchanged(parts[ranks - 1 - d], d) for d in range(ranks - 1, 0, -1)] + [parts[ranks - 1]]
        local = call(
            local_kernel,
            field,
            count=2,
            flops=2 * iface * iface * cells,
            moved=2 * iface * iface * cells,
            name="local",
        )(gap, inverse)
        other = swapped(sent, 2) if reduce else sent
        solved = call(
            lambda *refs: coarse_kernel(ranks, *refs),
            piece,
            count=3 + ranks,
            scratch=[pltpu.VMEM((ranks, ROWS, owned), F32)],
            flops=2 * blocks_own * order * order,
            moved=2 * blocks_own * order * order,
            name="coarse",
        )(coarse_inverse, dots, other, *arrivals)
        values = [solved] + [exchanged(solved, d) for d in range(1, ranks)]
        far, near, dots, lifted = call(
            lambda *refs: lift_kernel(ranks, *refs),
            (field, field, rows, field),
            count=4 + ranks,
            scratch=[pltpu.VMEM((ROWS, group), F32)],
            flops=2 * 24 * iface * cells,
            moved=2 * 24 * iface * cells + group * CORNERS_SUB * cells * 2,
            name="lift",
        )(local, operators, table, selector, *values)
        return m, gap, near, far, dots, lifted

    previous = shifted(right_side, 1)
    far, near = call(
        first_kernel, (message, message), count=5, scratch=stiff_scratch, name="first", **stiff_cost
    )(right_side, previous, selector, swap, stiff)
    u, gap_u, near, far, _, _ = apply_operator(near, far)
    r = right_side
    from_far, from_near = swapped_far(far), swapped(near, 1)
    far, near, w = call(
        second_kernel,
        (message, message, pair),
        count=9,
        scratch=stiff_scratch,
        name="second",
        **stiff_cost,
    )(far, near, from_far, from_near, r, u, selector, swap, stiff)

    states = (jnp.zeros((ROWS, cells), F32), r, r, u, w, r, r, r, w, gap_u, r, r)
    outs = (rows, field, field, field, pair, field, field, field, pair, field, field, field, message, message)
    for step in range(ITERS - 2):
        m, gap, near, far, dots, _ = apply_operator(near, far)
        from_far, from_near, other = swapped_far(far), swapped(near, 1), swapped(dots, 4)
        bit = 8
        while bit < sub_count:
            dots = dots + other
            other = swapped(dots, bit)
            bit *= 2
        *states, far, near = call(
            lambda *refs, first=step == 0: middle_kernel(first, *refs),
            outs,
            count=11 + STATES,
            scratch=stiff_scratch,
            name="middle",
            **stiff_cost,
        )(far, near, from_far, from_near, dots, other, m, gap, selector, swap, stiff, *states)
    scalars, x, r, u, w, p, s, q, z, gap_u, gap_p, gap_q = states
    m, gap, near, far, _, lifted = apply_operator(near, far, reduce=False)
    from_far, from_near = swapped_far(far), swapped(near, 1)
    parts = call(gram_kernel, shape(sub_count * ranks, 1, cells), count=13, name="gram")(
        r, u, w, p, s, q, z, m, gap_u, gap_p, gap_q, gap, lifted
    )
    everyone = lax.all_to_all(parts, ("sub", "grp"), 0, 0, tiled=True)
    x, r = call(final_kernel, (field, field), count=15, name="final")(
        everyone, scalars, x, r, u, w, p, s, q, z, m, far, near, from_far, from_near
    )
    return (x[:, None, :], r[:, None, :])


def solution(mesh):
    in_specs = (
        P(None, "grp", "sub"),
        P(None, None, "grp", "sub"),
        P(None, None, None, "grp", "sub"),
        P("grp", "sub"),
        P("grp", "sub"),
        P(None, None, "grp", "sub"),
        P(None, "grp", "sub"),
        P("grp", None, "sub"),
    )
    out_specs = (P(None, "grp", "sub"), P(None, "grp", "sub"))
    return jax.shard_map(
        on_device, mesh=mesh, in_specs=in_specs, out_specs=out_specs, check_vma=False
    )
```

```python
import jax
import jax.numpy as jnp
from jax import lax
from jax.experimental import pallas as pl
from jax.experimental.pallas import tpu as pltpu
from jax.sharding import PartitionSpec as P

CORNER_DOF = 6
CORNERS_SUB = 4
ITERS = 5
ROWS = 8
STATES = 12
LOADED = 3
NN = (((1,), (0,)), ((), ()))
NT = (((1,), (1,)), ((), ()))
F32 = jnp.float32
BF16 = jnp.bfloat16


def pieces_of(value):
    high = value.astype(BF16).astype(F32)
    rest = value - high
    middle = rest.astype(BF16).astype(F32)
    return [high, middle, rest - middle]


def exact_dot(value, table, dims):
    rows = value.shape[0]
    stacked = jnp.concatenate(pieces_of(value), axis=0).astype(BF16)
    product = lax.dot_general(stacked, table, dims, preferred_element_type=F32)
    return product[:rows] + product[rows : 2 * rows] + product[2 * rows :]


def lane_total(rows):
    return jnp.sum(rows, axis=1, keepdims=True)


def dot_rows(r, u, w, s=None, p=None):
    rows = [jnp.sum(r * u, axis=0, keepdims=True), jnp.sum(u * w, axis=0, keepdims=True)]
    if s is None:
        rows.append(jnp.zeros((ROWS - 2, r.shape[1]), F32))
    else:
        rows.append(jnp.sum(u * s, axis=0, keepdims=True))
        rows.append(jnp.sum(p * w, axis=0, keepdims=True))
        rows.append(jnp.zeros((ROWS - 4, r.shape[1]), F32))
    return jnp.concatenate(rows, axis=0)


def packed(rows):
    row = lax.broadcasted_iota(jnp.int32, rows.shape, 0)
    lane = lax.broadcasted_iota(jnp.int32, rows.shape, 1)
    return jnp.sum(jnp.where(row == lane, lane_total(rows), 0.0), axis=0, keepdims=True)


def step_sizes(sums, before):
    norm, curvature, crossed, other = sums
    if before is None:
        beta = None
    else:
        beta = norm / before[0:1, 0:1]
        curvature = curvature + beta * (crossed + other) + beta * beta * before[1:2, 0:1]
    return norm / curvature, beta, norm, curvature


def collect_to(odd, vector, selector, near_ref, far_ref):
    iface, cells = vector.shape
    moved = exact_dot(vector, selector, NT)
    low = moved[:, :cells]
    high = vector - moved[:, cells:]
    near_ref[:iface] = jnp.where(odd, low, high)
    far_ref[:iface] = jnp.where(odd, high, low)


def spread_of(own, previous, selector):
    return own - exact_dot(jnp.concatenate([previous, own], axis=1), selector, NN)


def apply_blocks(blocks, vectors, out_ref):
    def step(index, carry):
        at = pl.ds(index * ROWS, ROWS)
        total = None
        for block, vector in zip(blocks, vectors):
            term = block[at].astype(F32) * vector[None]
            total = term if total is None else total + term
        out_ref[pl.ds(pl.multiple_of(index * ROWS, ROWS), ROWS)] = jnp.sum(total, axis=1)
        return carry

    lax.fori_loop(0, out_ref.shape[0] // ROWS, step, 0, unroll=True)


def table_kernel(neighbour_ref, column_ref, corner_ref, *refs):
    sources, sems = refs[:LOADED], refs[-1]
    (selector_ref, swap_ref, table_ref), targets = refs[LOADED : LOADED + 3], refs[LOADED + 3 : -1]
    copies = [pltpu.make_async_copy(sources[k], targets[k], sems.at[k]) for k in range(LOADED)]
    for copy in copies:
        copy.start()
    cells = swap_ref.shape[0]
    start = lax.axis_index("sub") * cells

    def one_hot(row, count):
        places = lax.broadcasted_iota(jnp.int32, (count, row.shape[1]), 0)
        return jnp.where(places == row, 1.0, 0.0).astype(BF16)

    neighbour = neighbour_ref[...]
    slots = jnp.where(neighbour < 0, -1, neighbour - (start - cells))
    selector_ref[...] = one_hot(slots, selector_ref.shape[0])
    swap_ref[...] = one_hot(column_ref[...] - start, swap_ref.shape[0])
    chunk = 128

    def step(index, carry):
        row = corner_ref[...] - index * chunk
        table_ref[pl.ds(pl.multiple_of(index * chunk, chunk), chunk)] = one_hot(row, chunk)
        return carry

    lax.fori_loop(0, table_ref.shape[0] // chunk, step, 0)
    for copy in copies:
        copy.wait()


def stiffen(odd, own, previous, selector_ref, swap_ref, stiffness_ref, stiff_ref, near_ref, far_ref):
    gap = spread_of(own, previous, selector_ref[...])
    taken = exact_dot(gap, swap_ref[...], NN)
    apply_blocks([stiffness_ref.at[0], stiffness_ref.at[1]], [gap, taken], stiff_ref)
    collect_to(odd, stiff_ref[...], selector_ref[...], near_ref, far_ref)


def first_kernel(
    own_ref, previous_ref, selector_ref, swap_ref, stiffness_ref, far_ref, near_ref, stiff_ref
):
    iface, cells = own_ref.shape
    odd = lax.axis_index("sub") % 2 == 1
    stiffen(
        odd, own_ref[...], previous_ref[...], selector_ref, swap_ref, stiffness_ref, stiff_ref, near_ref, far_ref
    )
    near_ref[iface:] = jnp.zeros((ROWS, cells), F32)
    far_ref[iface:] = jnp.zeros((ROWS, cells), F32)


def arrived(odd, far_ref, near_ref, from_far_ref, from_near_ref, iface):
    near, far = near_ref[:iface], far_ref[:iface]
    from_near, from_far = from_near_ref[:iface], from_far_ref[:iface]
    own = jnp.where(odd, far - from_far, near - from_near)
    previous = jnp.where(odd, from_near - near, from_far - far)
    return own, previous


def second_kernel(
    far_ref, near_ref, from_far_ref, from_near_ref, r_ref, u_ref, selector_ref, swap_ref, stiffness_ref,
    far_out, near_out, w_out, stiff_ref,
):
    iface = r_ref.shape[0]
    odd = lax.axis_index("sub") % 2 == 1
    w, w_previous = arrived(odd, far_ref, near_ref, from_far_ref, from_near_ref, iface)
    w_out[0] = w
    w_out[1] = w_previous
    dots = dot_rows(r_ref[...], u_ref[...], w)
    near_out[iface:] = dots
    far_out[iface:] = dots
    stiffen(odd, w, w_previous, selector_ref, swap_ref, stiffness_ref, stiff_ref, near_out, far_out)


def update(first, refs, m, gap, n, n_previous, totals):
    scalars_in, x_in, r_in, u_in, w_in, p_in, s_in, q_in, z_in, gap_u_in, gap_p_in, gap_q_in = refs[:STATES]
    scalars_out, x_out, r_out, u_out, w_out, p_out, s_out, q_out, z_out, gap_u_out, gap_p_out, gap_q_out = refs[STATES:]
    sums = lane_total(totals)
    sums = [sums[k : k + 1] for k in range(4)]
    alpha, beta, norm, curvature = step_sizes(sums, None if first else scalars_in[...])
    cells = m.shape[1]
    scalars_out[...] = jnp.concatenate(
        [
            jnp.broadcast_to(norm, (1, cells)),
            jnp.broadcast_to(curvature, (1, cells)),
            jnp.zeros((ROWS - 2, cells), F32),
        ],
        axis=0,
    )

    def turned(fresh, kept):
        return fresh if first else fresh + beta * kept[...]

    u, w = u_in[...], w_in[0]
    p = turned(u, p_in)
    s = turned(w, s_in)
    q = turned(m, q_in)
    z = turned(n, None if first else z_in.at[0])
    p_out[...] = p
    s_out[...] = s
    x_out[...] = alpha * p if first else x_in[...] + alpha * p
    r = r_in[...] - alpha * s
    u = u - alpha * q
    w = w - alpha * z
    r_out[...] = r
    u_out[...] = u
    w_out[0] = w
    z_previous = turned(n_previous, None if first else z_in.at[1])
    previous = w_in[1] - alpha * z_previous
    q_out[...] = q
    z_out[0] = z
    z_out[1] = z_previous
    w_out[1] = previous
    gap_u = gap_u_in[...]
    gap_q = turned(gap, gap_q_in)
    gap_p_out[...] = turned(gap_u, gap_p_in)
    gap_q_out[...] = gap_q
    gap_u_out[...] = gap_u - alpha * gap_q
    return dot_rows(r, u, w, s, p), w, previous


def middle_kernel(first, *refs):
    (far_ref, near_ref, from_far_ref, from_near_ref, dots_ref, dots_other_ref, m_ref, gap_ref) = refs[:8]
    (selector_ref, swap_ref, stiffness_ref) = refs[8:11]
    states = list(refs[11 : 11 + 2 * STATES])
    far_out, near_out, stiff_ref = refs[11 + 2 * STATES :]
    m = m_ref[...]
    iface = m.shape[0]
    odd = lax.axis_index("sub") % 2 == 1
    n, n_previous = arrived(odd, far_ref, near_ref, from_far_ref, from_near_ref, iface)
    dots, w, previous = update(
        first, states, m, gap_ref[...], n, n_previous, dots_ref[...] + dots_other_ref[...]
    )
    near_out[iface:] = dots
    far_out[iface:] = dots
    stiffen(odd, w, previous, selector_ref, swap_ref, stiffness_ref, stiff_ref, near_out, far_out)


def corner_kernel(
    ranks, far_ref, near_ref, from_far_ref, from_near_ref, selector_ref, operators_ref, table_ref,
    m_out, gap_out, *rest,
):
    dots_sent, outs, (dots_out, sums_ref) = rest[0], rest[1 : ranks + 1], rest[ranks + 1 :]
    iface, cells = m_out.shape
    odd = lax.axis_index("sub") % 2 == 1
    own, previous = arrived(odd, far_ref, near_ref, from_far_ref, from_near_ref, iface)
    m_out[...] = own
    dots_sent[...] = jnp.zeros_like(dots_sent)
    dots = near_ref[iface:] + from_near_ref[iface:]
    dots_out[...] = dots
    dots_sent[:, :cells] = dots
    gap = spread_of(own, previous, selector_ref[...])
    gap_out[...] = gap
    parts = []
    for corner in range(CORNERS_SUB):
        at = slice(corner * CORNER_DOF, (corner + 1) * CORNER_DOF)
        part = jnp.sum(operators_ref[at].astype(F32) * gap[None], axis=1)
        parts.append(jnp.concatenate([part, jnp.zeros((ROWS - CORNER_DOF, cells), F32)], axis=0))
    sums_ref[...] = exact_dot(jnp.concatenate(parts, axis=1), table_ref[...], NT)
    owned = sums_ref.shape[1] // ranks
    for distance in range(ranks):
        rank = lax.axis_index("grp") ^ (ranks - 1 - distance)
        outs[distance][...] = sums_ref[:, pl.ds(pl.multiple_of(rank * owned, 128), owned)]


def local_kernel(gap_ref, inverse_ref, local_ref):
    apply_blocks([inverse_ref], [gap_ref[...]], local_ref)


def coarse_kernel(ranks, coarse_ref, dots_ref, other_ref, *rest):
    pieces, (solved_ref, sums_ref) = rest[:ranks], rest[ranks:]
    cells = dots_ref.shape[1]
    for distance in range(ranks):
        rank = lax.axis_index("grp") ^ distance
        sums_ref[rank] = pieces[ranks - 1 - distance][...]
    total = sums_ref[0]
    for rank in range(1, ranks):
        total = total + sums_ref[rank]
    blocks, order = coarse_ref.shape[0], coarse_ref.shape[1]
    width = order // CORNER_DOF
    columns = []
    for block in range(blocks):
        lanes = slice(block * width, (block + 1) * width)
        row = jnp.concatenate([total[j : j + 1, lanes] for j in range(CORNER_DOF)], axis=1)
        parts = pieces_of(row) + [jnp.zeros((ROWS - 3, order), F32)]
        stacked = jnp.concatenate(parts, axis=0).astype(BF16)
        product = lax.dot_general(stacked, coarse_ref[block], NT, preferred_element_type=F32)
        result = product[0:1] + product[1:2] + product[2:3]
        rows = [result[:, j * width : (j + 1) * width] for j in range(CORNER_DOF)]
        columns.append(jnp.concatenate(rows, axis=0))
    solved = jnp.concatenate(columns, axis=1)
    dots = dots_ref[...] + other_ref[:, :cells]
    rows = [solved]
    for first in (0, 2):
        lanes = [dots[first : first + 1], dots[first + 1 : first + 2]]
        if solved.shape[1] > 2 * cells:
            lanes.append(jnp.zeros((1, solved.shape[1] - 2 * cells), F32))
        rows.append(jnp.concatenate(lanes, axis=1))
    solved_ref[...] = jnp.concatenate(rows, axis=0)


def lift_kernel(ranks, last, local_ref, operators_ref, table_ref, selector_ref, *rest):
    pieces, (far_ref, near_ref, extra_out, values_ref) = rest[:ranks], rest[ranks:]
    cells = local_ref.shape[1]
    owned = values_ref.shape[1] // ranks
    for distance in range(ranks):
        rank = lax.axis_index("grp") ^ distance
        values_ref[:, pl.ds(pl.multiple_of(rank * owned, 128), owned)] = pieces[distance][...]
    values = values_ref[...]
    if not last:
        tail = values[CORNER_DOF:, :owned]
        for rank in range(1, ranks):
            tail = tail + values[CORNER_DOF:, rank * owned : (rank + 1) * owned]
        extra_out[...] = jnp.concatenate(
            [
                tail[0:1, :cells],
                tail[0:1, cells : 2 * cells],
                tail[1:2, :cells],
                tail[1:2, cells : 2 * cells],
                jnp.zeros((ROWS - 4, cells), F32),
            ],
            axis=0,
        )
    picked = exact_dot(values, table_ref[...], NN)
    lifted = local_ref[...]
    for corner in range(CORNERS_SUB):
        lanes = slice(corner * cells, (corner + 1) * cells)
        for dof in range(CORNER_DOF):
            operator = operators_ref[corner * CORNER_DOF + dof].astype(F32)
            lifted = lifted + operator * picked[dof : dof + 1, lanes]
    if last:
        extra_out[...] = lifted
    collect_to(lax.axis_index("sub") % 2 == 1, lifted, selector_ref[...], near_ref, far_ref)


def gram_kernel(
    r_ref, u_ref, w_ref, p_ref, s_ref, q_ref, z_ref, m_ref, gap_u_ref, gap_p_ref, gap_q_ref, gap_ref, lifted_ref, out_ref
):
    left = [u_ref[...], m_ref[...], q_ref[...], p_ref[...]]
    gaps = [gap_u_ref[...], gap_ref[...], gap_q_ref[...], gap_p_ref[...]]
    w, z, s = w_ref[0], z_ref[0], s_ref[...]
    r, lifted = r_ref[...], lifted_ref[...]
    products = []
    for v, gap in zip(left, gaps):
        products += [v * w, gap * lifted, v * z, v * s]
    products += [r * v for v in left[:3]]
    rows = [jnp.sum(product, axis=0, keepdims=True) for product in products]
    rows.append(jnp.zeros((-len(rows) % ROWS, r.shape[1]), F32))
    out_ref[...] = jnp.broadcast_to(packed(jnp.concatenate(rows, axis=0))[None], out_ref.shape)


def final_kernel(
    dots_ref, scalars_ref, x_ref, r_ref, u_ref, w_ref, p_ref, s_ref, q_ref, z_ref, m_ref,
    far_ref, near_ref, from_far_ref, from_near_ref, x_out, r_out,
):
    totals = jnp.sum(dots_ref[...], axis=0)
    gram = [[totals[:, 4 * i + k : 4 * i + k + 1] for k in range(4)] for i in range(4)]
    with_r = [totals[:, 16 + i : 17 + i] for i in range(3)]

    def form(first, second):
        total = None
        for i, left in first.items():
            row = None
            for k, right in second.items():
                term = gram[i][k] * right
                row = term if row is None else row + term
            total = left * row if total is None else total + left * row
        return total

    norm = with_r[0]
    beta = norm / scalars_ref[0:1, 0:1]
    one = jnp.ones_like(norm)
    turned = {0: one, 3: beta}
    alpha = norm / form(turned, turned)
    stepped = {0: one, 1: -alpha, 2: -alpha * beta}
    norm_next = with_r[0] + stepped[1] * with_r[1] + stepped[2] * with_r[2] - alpha * form(stepped, turned)
    beta_next = norm_next / norm
    turned_next = {0: one + beta_next, 1: stepped[1], 2: stepped[2], 3: beta_next * beta}
    alpha_next = norm_next / form(turned_next, turned_next)

    odd = lax.axis_index("sub") % 2 == 1
    n, _ = arrived(odd, far_ref, near_ref, from_far_ref, from_near_ref, r_ref.shape[0])
    p = u_ref[...] + beta * p_ref[...]
    s = w_ref[0] + beta * s_ref[...]
    u = u_ref[...] - alpha * (m_ref[...] + beta * q_ref[...])
    w = w_ref[0] - alpha * (n + beta * z_ref[0])
    x_out[...] = x_ref[...] + alpha * p + alpha_next * (u + beta_next * p)
    r_out[...] = r_ref[...] - alpha * s - alpha_next * (w + beta_next * s)


def shifted(block, distance):
    count = lax.axis_size("sub")
    route = [(i, i + distance) for i in range(count) if 0 <= i + distance < count]
    return lax.ppermute(block, "sub", route)


def swapped(block, bit):
    return lax.ppermute(block, "sub", [(i, i ^ bit) for i in range(lax.axis_size("sub"))])


def swapped_far(block):
    inner = range(1, lax.axis_size("sub") - 1)
    return lax.ppermute(block, "sub", [(i, i + 1 if i % 2 else i - 1) for i in inner])


def exchanged(block, distance):
    return lax.ppermute(block, "grp", [(i, i ^ distance) for i in range(lax.axis_size("grp"))])


def shape(*dims, dtype=F32):
    return jax.ShapeDtypeStruct(dims, dtype)


def call(kernel, out_shape, count=0, kept=0, scratch=(), flops=0, moved=0, name=None):
    specs = [pl.BlockSpec(memory_space=pltpu.VMEM)] * count + [pl.BlockSpec(memory_space=pltpu.HBM)] * kept
    out_specs = jax.tree.map(lambda _: pl.BlockSpec(memory_space=pltpu.VMEM), out_shape)
    return pl.pallas_call(
        kernel,
        out_shape=out_shape,
        in_specs=specs,
        out_specs=out_specs,
        scratch_shapes=list(scratch),
        compiler_params=pltpu.CompilerParams(vmem_limit_bytes=24 * 1024 * 1024),
        cost_estimate=pl.CostEstimate(flops=flops, bytes_accessed=moved, transcendentals=0),
        name=name,
    )


def on_device(
    gap_data,
    local_inverse,
    stiffness,
    stiff_column,
    neighbour,
    corner_ops,
    corner_index,
    coarse_inverse,
):
    iface, _, cells = gap_data.shape
    ranks = lax.axis_size("grp")
    sub_count = lax.axis_size("sub")
    right_side = gap_data[:, 0, :]
    inverse = local_inverse[:, :, 0, :]
    stiff = stiffness[:, :, :, 0, :]
    operators = corner_ops[:, :, 0, :]
    blocks_own, order = coarse_inverse.shape[:2]
    owned = blocks_own * (order // CORNER_DOF)
    group = owned * ranks
    corners = corner_index.reshape(1, CORNERS_SUB * cells)

    previous = shifted(right_side, 1)
    large = (stiff, operators, right_side)
    selector, swap, table, stiff, operators, right_side = call(
        table_kernel,
        (
            shape(2 * cells, cells, dtype=BF16),
            shape(cells, cells, dtype=BF16),
            shape(group, CORNERS_SUB * cells, dtype=BF16),
        )
        + tuple(jax.ShapeDtypeStruct(array.shape, array.dtype) for array in large),
        count=3,
        kept=LOADED,
        scratch=[pltpu.SemaphoreType.DMA((LOADED,))],
        moved=4 * iface * iface * cells,
        name="tables",
    )(neighbour, stiff_column, corners, *(pltpu.with_memory_space_constraint(array, pltpu.HBM) for array in large))

    field = shape(iface, cells)
    pair = shape(2, iface, cells)
    message = shape(iface + ROWS, cells)
    rows = shape(ROWS, cells)
    piece = shape(ROWS, owned)
    stiff_scratch = [pltpu.VMEM((iface, cells), F32)]
    stiff_cost = dict(flops=4 * iface * iface * cells, moved=4 * iface * iface * cells)

    def apply_operator(near, far, reduce=True):
        from_far, from_near = swapped_far(far), swapped(near, 1)
        m, gap, sent, *parts, dots = call(
            lambda *refs: corner_kernel(ranks, *refs),
            (field, field) + (piece,) * (ranks + 1) + (rows,),
            count=7,
            scratch=[pltpu.VMEM((ROWS, group), F32)],
            flops=2 * 24 * iface * cells,
            moved=2 * 24 * iface * cells + group * CORNERS_SUB * cells * 2,
            name="corners",
        )(far, near, from_far, from_near, selector, operators, table)
        arrivals = [exchanged(parts[ranks - 1 - d], d) for d in range(ranks - 1, 0, -1)] + [parts[ranks - 1]]
        local = call(
            local_kernel,
            field,
            count=2,
            flops=2 * iface * iface * cells,
            moved=2 * iface * iface * cells,
            name="local",
        )(gap, inverse)
        other = swapped(sent, 2) if reduce else sent
        solved = call(
            lambda *refs: coarse_kernel(ranks, *refs),
            piece,
            count=3 + ranks,
            scratch=[pltpu.VMEM((ranks, ROWS, owned), F32)],
            flops=2 * blocks_own * order * order,
            moved=2 * blocks_own * order * order,
            name="coarse",
        )(coarse_inverse, dots, other, *arrivals)
        values = [solved] + [exchanged(solved, d) for d in range(1, ranks)]
        far, near, extra = call(
            lambda *refs: lift_kernel(ranks, not reduce, *refs),
            (field, field, rows if reduce else field),
            count=4 + ranks,
            scratch=[pltpu.VMEM((ROWS, group), F32)],
            flops=2 * 24 * iface * cells,
            moved=2 * 24 * iface * cells + group * CORNERS_SUB * cells * 2,
            name="lift",
        )(local, operators, table, selector, *values)
        return m, gap, near, far, extra

    far, near = call(
        first_kernel, (message, message), count=5, scratch=stiff_scratch, name="first", **stiff_cost
    )(right_side, previous, selector, swap, stiff)
    u, gap_u, near, far, _ = apply_operator(near, far)
    r = right_side
    from_far, from_near = swapped_far(far), swapped(near, 1)
    far, near, w = call(
        second_kernel,
        (message, message, pair),
        count=9,
        scratch=stiff_scratch,
        name="second",
        **stiff_cost,
    )(far, near, from_far, from_near, r, u, selector, swap, stiff)

    states = (jnp.zeros((ROWS, cells), F32), r, r, u, w, r, r, r, w, gap_u, r, r)
    outs = (rows, field, field, field, pair, field, field, field, pair, field, field, field, message, message)
    for step in range(ITERS - 2):
        m, gap, near, far, dots = apply_operator(near, far)
        from_far, from_near, other = swapped_far(far), swapped(near, 1), swapped(dots, 4)
        bit = 8
        while bit < sub_count:
            dots = dots + other
            other = swapped(dots, bit)
            bit *= 2
        *states, far, near = call(
            lambda *refs, first=step == 0: middle_kernel(first, *refs),
            outs,
            count=11 + STATES,
            scratch=stiff_scratch,
            name="middle",
            **stiff_cost,
        )(far, near, from_far, from_near, dots, other, m, gap, selector, swap, stiff, *states)
    scalars, x, r, u, w, p, s, q, z, gap_u, gap_p, gap_q = states
    m, gap, near, far, lifted = apply_operator(near, far, reduce=False)
    from_far, from_near = swapped_far(far), swapped(near, 1)
    parts = call(gram_kernel, shape(sub_count * ranks, 1, cells), count=13, name="gram")(
        r, u, w, p, s, q, z, m, gap_u, gap_p, gap_q, gap, lifted
    )
    everyone = lax.all_to_all(parts, ("sub", "grp"), 0, 0, tiled=True)
    x, r = call(final_kernel, (field, field), count=15, name="final")(
        everyone, scalars, x, r, u, w, p, s, q, z, m, far, near, from_far, from_near
    )
    return (x[:, None, :], r[:, None, :])


def solution(mesh):
    in_specs = (
        P(None, "grp", "sub"),
        P(None, None, "grp", "sub"),
        P(None, None, None, "grp", "sub"),
        P("grp", "sub"),
        P("grp", "sub"),
        P(None, None, "grp", "sub"),
        P(None, "grp", "sub"),
        P("grp", None, "sub"),
    )
    out_specs = (P(None, "grp", "sub"), P(None, "grp", "sub"))
    return jax.shard_map(
        on_device, mesh=mesh, in_specs=in_specs, out_specs=out_specs, check_vma=False
    )
```

```python
import jax
import jax.numpy as jnp
from jax import lax
from jax.experimental import pallas as pl
from jax.experimental.pallas import tpu as pltpu
from jax.sharding import PartitionSpec as P

CORNER_DOF = 6
CORNERS_SUB = 4
ITERS = 5
ROWS = 8
STATES = 12
LOADED = 3
NN = (((1,), (0,)), ((), ()))
NT = (((1,), (1,)), ((), ()))
F32 = jnp.float32
BF16 = jnp.bfloat16


def pieces_of(value):
    high = value.astype(BF16).astype(F32)
    rest = value - high
    middle = rest.astype(BF16).astype(F32)
    return [high, middle, rest - middle]


def exact_dot(value, table, dims):
    rows = value.shape[0]
    stacked = jnp.concatenate(pieces_of(value), axis=0).astype(BF16)
    product = lax.dot_general(stacked, table, dims, preferred_element_type=F32)
    return product[:rows] + product[rows : 2 * rows] + product[2 * rows :]


def lane_total(rows):
    return jnp.sum(rows, axis=1, keepdims=True)


def dot_rows(r, u, w, s=None, p=None):
    rows = [jnp.sum(r * u, axis=0, keepdims=True), jnp.sum(u * w, axis=0, keepdims=True)]
    if s is None:
        rows.append(jnp.zeros((ROWS - 2, r.shape[1]), F32))
    else:
        rows.append(jnp.sum(u * s, axis=0, keepdims=True))
        rows.append(jnp.sum(p * w, axis=0, keepdims=True))
        rows.append(jnp.zeros((ROWS - 4, r.shape[1]), F32))
    return jnp.concatenate(rows, axis=0)


def packed(rows):
    row = lax.broadcasted_iota(jnp.int32, rows.shape, 0)
    lane = lax.broadcasted_iota(jnp.int32, rows.shape, 1)
    return jnp.sum(jnp.where(row == lane, lane_total(rows), 0.0), axis=0, keepdims=True)


def step_sizes(sums, before):
    norm, curvature, crossed, other = sums
    if before is None:
        beta = None
    else:
        beta = norm / before[0:1, 0:1]
        curvature = curvature + beta * (crossed + other) + beta * beta * before[1:2, 0:1]
    return norm / curvature, beta, norm, curvature


def collect_to(odd, vector, selector, near_ref, far_ref):
    iface, cells = vector.shape
    moved = exact_dot(vector, selector, NT)
    low = moved[:, :cells]
    high = vector - moved[:, cells:]
    near_ref[:iface] = jnp.where(odd, low, high)
    far_ref[:iface] = jnp.where(odd, high, low)


def spread_of(own, previous, selector):
    return own - exact_dot(jnp.concatenate([previous, own], axis=1), selector, NN)


def apply_blocks(blocks, vectors, out_ref):
    def step(index, carry):
        at = pl.ds(index * ROWS, ROWS)
        total = None
        for block, vector in zip(blocks, vectors):
            term = block[at].astype(F32) * vector[None]
            total = term if total is None else total + term
        out_ref[pl.ds(pl.multiple_of(index * ROWS, ROWS), ROWS)] = jnp.sum(total, axis=1)
        return carry

    lax.fori_loop(0, out_ref.shape[0] // ROWS, step, 0, unroll=True)


def table_kernel(*refs):
    sources, (selector_ref, swap_ref, table_ref), sems = refs[: LOADED + 3], refs[LOADED + 3 : LOADED + 6], refs[-1]
    neighbour_ref, column_ref, corner_ref = refs[-4:-1]
    targets = refs[-4:-1] + refs[LOADED + 6 : -4]
    copies = [pltpu.make_async_copy(sources[k], targets[k], sems.at[k]) for k in range(LOADED + 3)]
    for copy in copies:
        copy.start()
    for copy in copies[:3]:
        copy.wait()
    cells = swap_ref.shape[0]
    start = lax.axis_index("sub") * cells

    def one_hot(row, count):
        places = lax.broadcasted_iota(jnp.int32, (count, row.shape[1]), 0)
        return jnp.where(places == row, 1.0, 0.0).astype(BF16)

    neighbour = neighbour_ref[...]
    slots = jnp.where(neighbour < 0, -1, neighbour - (start - cells))
    selector_ref[...] = one_hot(slots, selector_ref.shape[0])
    swap_ref[...] = one_hot(column_ref[...] - start, swap_ref.shape[0])
    chunk = 128

    def step(index, carry):
        row = corner_ref[...] - index * chunk
        table_ref[pl.ds(pl.multiple_of(index * chunk, chunk), chunk)] = one_hot(row, chunk)
        return carry

    lax.fori_loop(0, table_ref.shape[0] // chunk, step, 0)
    for copy in copies[3:]:
        copy.wait()


def stiffen(odd, own, previous, selector_ref, swap_ref, stiffness_ref, stiff_ref, near_ref, far_ref):
    gap = spread_of(own, previous, selector_ref[...])
    taken = exact_dot(gap, swap_ref[...], NN)
    apply_blocks([stiffness_ref.at[0], stiffness_ref.at[1]], [gap, taken], stiff_ref)
    collect_to(odd, stiff_ref[...], selector_ref[...], near_ref, far_ref)


def first_kernel(
    own_ref, previous_ref, selector_ref, swap_ref, stiffness_ref, far_ref, near_ref, stiff_ref
):
    iface, cells = own_ref.shape
    odd = lax.axis_index("sub") % 2 == 1
    stiffen(
        odd, own_ref[...], previous_ref[...], selector_ref, swap_ref, stiffness_ref, stiff_ref, near_ref, far_ref
    )
    near_ref[iface:] = jnp.zeros((ROWS, cells), F32)
    far_ref[iface:] = jnp.zeros((ROWS, cells), F32)


def arrived(odd, far_ref, near_ref, from_far_ref, from_near_ref, iface):
    near, far = near_ref[:iface], far_ref[:iface]
    from_near, from_far = from_near_ref[:iface], from_far_ref[:iface]
    own = jnp.where(odd, far - from_far, near - from_near)
    previous = jnp.where(odd, from_near - near, from_far - far)
    return own, previous


def second_kernel(
    far_ref, near_ref, from_far_ref, from_near_ref, r_ref, u_ref, selector_ref, swap_ref, stiffness_ref,
    far_out, near_out, w_out, stiff_ref,
):
    iface = r_ref.shape[0]
    odd = lax.axis_index("sub") % 2 == 1
    w, w_previous = arrived(odd, far_ref, near_ref, from_far_ref, from_near_ref, iface)
    w_out[0] = w
    w_out[1] = w_previous
    dots = dot_rows(r_ref[...], u_ref[...], w)
    near_out[iface:] = dots
    far_out[iface:] = dots
    stiffen(odd, w, w_previous, selector_ref, swap_ref, stiffness_ref, stiff_ref, near_out, far_out)


def update(first, refs, m, gap, n, n_previous, totals):
    scalars_in, x_in, r_in, u_in, w_in, p_in, s_in, q_in, z_in, gap_u_in, gap_p_in, gap_q_in = refs[:STATES]
    scalars_out, x_out, r_out, u_out, w_out, p_out, s_out, q_out, z_out, gap_u_out, gap_p_out, gap_q_out = refs[STATES:]
    sums = lane_total(totals)
    sums = [sums[k : k + 1] for k in range(4)]
    alpha, beta, norm, curvature = step_sizes(sums, None if first else scalars_in[...])
    cells = m.shape[1]
    scalars_out[...] = jnp.concatenate(
        [
            jnp.broadcast_to(norm, (1, cells)),
            jnp.broadcast_to(curvature, (1, cells)),
            jnp.zeros((ROWS - 2, cells), F32),
        ],
        axis=0,
    )

    def turned(fresh, kept):
        return fresh if first else fresh + beta * kept[...]

    u, w = u_in[...], w_in[0]
    p = turned(u, p_in)
    s = turned(w, s_in)
    q = turned(m, q_in)
    z = turned(n, None if first else z_in.at[0])
    p_out[...] = p
    s_out[...] = s
    x_out[...] = alpha * p if first else x_in[...] + alpha * p
    r = r_in[...] - alpha * s
    u = u - alpha * q
    w = w - alpha * z
    r_out[...] = r
    u_out[...] = u
    w_out[0] = w
    z_previous = turned(n_previous, None if first else z_in.at[1])
    previous = w_in[1] - alpha * z_previous
    q_out[...] = q
    z_out[0] = z
    z_out[1] = z_previous
    w_out[1] = previous
    gap_u = gap_u_in[...]
    gap_q = turned(gap, gap_q_in)
    gap_p_out[...] = turned(gap_u, gap_p_in)
    gap_q_out[...] = gap_q
    gap_u_out[...] = gap_u - alpha * gap_q
    return dot_rows(r, u, w, s, p), w, previous


def middle_kernel(first, *refs):
    (far_ref, near_ref, from_far_ref, from_near_ref, dots_ref, dots_other_ref, m_ref, gap_ref) = refs[:8]
    (selector_ref, swap_ref, stiffness_ref) = refs[8:11]
    states = list(refs[11 : 11 + 2 * STATES])
    far_out, near_out, stiff_ref = refs[11 + 2 * STATES :]
    m = m_ref[...]
    iface = m.shape[0]
    odd = lax.axis_index("sub") % 2 == 1
    n, n_previous = arrived(odd, far_ref, near_ref, from_far_ref, from_near_ref, iface)
    dots, w, previous = update(
        first, states, m, gap_ref[...], n, n_previous, dots_ref[...] + dots_other_ref[...]
    )
    near_out[iface:] = dots
    far_out[iface:] = dots
    stiffen(odd, w, previous, selector_ref, swap_ref, stiffness_ref, stiff_ref, near_out, far_out)


def corner_kernel(
    ranks, far_ref, near_ref, from_far_ref, from_near_ref, selector_ref, operators_ref, table_ref,
    m_out, gap_out, *rest,
):
    dots_sent, outs, (dots_out, sums_ref) = rest[0], rest[1 : ranks + 1], rest[ranks + 1 :]
    iface, cells = m_out.shape
    odd = lax.axis_index("sub") % 2 == 1
    own, previous = arrived(odd, far_ref, near_ref, from_far_ref, from_near_ref, iface)
    m_out[...] = own
    dots_sent[...] = jnp.zeros_like(dots_sent)
    dots = near_ref[iface:] + from_near_ref[iface:]
    dots_out[...] = dots
    dots_sent[:, :cells] = dots
    gap = spread_of(own, previous, selector_ref[...])
    gap_out[...] = gap
    parts = []
    for corner in range(CORNERS_SUB):
        at = slice(corner * CORNER_DOF, (corner + 1) * CORNER_DOF)
        part = jnp.sum(operators_ref[at].astype(F32) * gap[None], axis=1)
        parts.append(jnp.concatenate([part, jnp.zeros((ROWS - CORNER_DOF, cells), F32)], axis=0))
    sums_ref[...] = exact_dot(jnp.concatenate(parts, axis=1), table_ref[...], NT)
    owned = sums_ref.shape[1] // ranks
    for distance in range(ranks):
        rank = lax.axis_index("grp") ^ (ranks - 1 - distance)
        outs[distance][...] = sums_ref[:, pl.ds(pl.multiple_of(rank * owned, 128), owned)]


def local_kernel(gap_ref, inverse_ref, local_ref):
    apply_blocks([inverse_ref], [gap_ref[...]], local_ref)


def coarse_kernel(ranks, coarse_ref, dots_ref, other_ref, *rest):
    pieces, (solved_ref, sums_ref) = rest[:ranks], rest[ranks:]
    cells = dots_ref.shape[1]
    for distance in range(ranks):
        rank = lax.axis_index("grp") ^ distance
        sums_ref[rank] = pieces[ranks - 1 - distance][...]
    total = sums_ref[0]
    for rank in range(1, ranks):
        total = total + sums_ref[rank]
    blocks, order = coarse_ref.shape[0], coarse_ref.shape[1]
    width = order // CORNER_DOF
    columns = []
    for block in range(blocks):
        lanes = slice(block * width, (block + 1) * width)
        row = jnp.concatenate([total[j : j + 1, lanes] for j in range(CORNER_DOF)], axis=1)
        parts = pieces_of(row) + [jnp.zeros((ROWS - 3, order), F32)]
        stacked = jnp.concatenate(parts, axis=0).astype(BF16)
        product = lax.dot_general(stacked, coarse_ref[block], NT, preferred_element_type=F32)
        result = product[0:1] + product[1:2] + product[2:3]
        rows = [result[:, j * width : (j + 1) * width] for j in range(CORNER_DOF)]
        columns.append(jnp.concatenate(rows, axis=0))
    solved = jnp.concatenate(columns, axis=1)
    dots = dots_ref[...] + other_ref[:, :cells]
    rows = [solved]
    for first in (0, 2):
        lanes = [dots[first : first + 1], dots[first + 1 : first + 2]]
        if solved.shape[1] > 2 * cells:
            lanes.append(jnp.zeros((1, solved.shape[1] - 2 * cells), F32))
        rows.append(jnp.concatenate(lanes, axis=1))
    solved_ref[...] = jnp.concatenate(rows, axis=0)


def lift_kernel(ranks, extra, local_ref, operators_ref, table_ref, selector_ref, *rest):
    pieces, (far_ref, near_ref), (*extra_out, values_ref) = rest[:ranks], rest[ranks : ranks + 2], rest[ranks + 2 :]
    cells = local_ref.shape[1]
    owned = values_ref.shape[1] // ranks
    for distance in range(ranks):
        rank = lax.axis_index("grp") ^ distance
        values_ref[:, pl.ds(pl.multiple_of(rank * owned, 128), owned)] = pieces[distance][...]
    values = values_ref[...]
    if extra == "dots":
        tail = values[CORNER_DOF:, :owned]
        for rank in range(1, ranks):
            tail = tail + values[CORNER_DOF:, rank * owned : (rank + 1) * owned]
        extra_out[0][...] = jnp.concatenate(
            [
                tail[0:1, :cells],
                tail[0:1, cells : 2 * cells],
                tail[1:2, :cells],
                tail[1:2, cells : 2 * cells],
                jnp.zeros((ROWS - 4, cells), F32),
            ],
            axis=0,
        )
    picked = exact_dot(values, table_ref[...], NN)
    lifted = local_ref[...]
    for corner in range(CORNERS_SUB):
        lanes = slice(corner * cells, (corner + 1) * cells)
        for dof in range(CORNER_DOF):
            operator = operators_ref[corner * CORNER_DOF + dof].astype(F32)
            lifted = lifted + operator * picked[dof : dof + 1, lanes]
    if extra == "lifted":
        extra_out[0][...] = lifted
    collect_to(lax.axis_index("sub") % 2 == 1, lifted, selector_ref[...], near_ref, far_ref)


def gram_kernel(
    r_ref, u_ref, w_ref, p_ref, s_ref, q_ref, z_ref, m_ref, gap_u_ref, gap_p_ref, gap_q_ref, gap_ref, lifted_ref, out_ref
):
    left = [u_ref[...], m_ref[...], q_ref[...], p_ref[...]]
    gaps = [gap_u_ref[...], gap_ref[...], gap_q_ref[...], gap_p_ref[...]]
    w, z, s = w_ref[0], z_ref[0], s_ref[...]
    r, lifted = r_ref[...], lifted_ref[...]
    products = []
    for v, gap in zip(left, gaps):
        products += [v * w, gap * lifted, v * z, v * s]
    products += [r * v for v in left[:3]]
    rows = [jnp.sum(product, axis=0, keepdims=True) for product in products]
    rows.append(jnp.zeros((-len(rows) % ROWS, r.shape[1]), F32))
    out_ref[...] = jnp.broadcast_to(packed(jnp.concatenate(rows, axis=0))[None], out_ref.shape)


def final_kernel(
    dots_ref, scalars_ref, x_ref, r_ref, u_ref, w_ref, p_ref, s_ref, q_ref, z_ref, m_ref,
    far_ref, near_ref, from_far_ref, from_near_ref, x_out, r_out,
):
    totals = jnp.sum(dots_ref[...], axis=0)
    gram = [[totals[:, 4 * i + k : 4 * i + k + 1] for k in range(4)] for i in range(4)]
    with_r = [totals[:, 16 + i : 17 + i] for i in range(3)]

    def form(first, second):
        total = None
        for i, left in first.items():
            row = None
            for k, right in second.items():
                term = gram[i][k] * right
                row = term if row is None else row + term
            total = left * row if total is None else total + left * row
        return total

    norm = with_r[0]
    beta = norm / scalars_ref[0:1, 0:1]
    one = jnp.ones_like(norm)
    turned = {0: one, 3: beta}
    alpha = norm / form(turned, turned)
    stepped = {0: one, 1: -alpha, 2: -alpha * beta}
    norm_next = with_r[0] + stepped[1] * with_r[1] + stepped[2] * with_r[2] - alpha * form(stepped, turned)
    beta_next = norm_next / norm
    turned_next = {0: one + beta_next, 1: stepped[1], 2: stepped[2], 3: beta_next * beta}
    alpha_next = norm_next / form(turned_next, turned_next)

    odd = lax.axis_index("sub") % 2 == 1
    n, _ = arrived(odd, far_ref, near_ref, from_far_ref, from_near_ref, r_ref.shape[0])
    p = u_ref[...] + beta * p_ref[...]
    s = w_ref[0] + beta * s_ref[...]
    u = u_ref[...] - alpha * (m_ref[...] + beta * q_ref[...])
    w = w_ref[0] - alpha * (n + beta * z_ref[0])
    x_out[...] = x_ref[...] + alpha * p + alpha_next * (u + beta_next * p)
    r_out[...] = r_ref[...] - alpha * s - alpha_next * (w + beta_next * s)


def shifted(block, distance):
    count = lax.axis_size("sub")
    route = [(i, i + distance) for i in range(count) if 0 <= i + distance < count]
    return lax.ppermute(block, "sub", route)


def swapped(block, bit):
    return lax.ppermute(block, "sub", [(i, i ^ bit) for i in range(lax.axis_size("sub"))])


def swapped_far(block):
    inner = range(1, lax.axis_size("sub") - 1)
    return lax.ppermute(block, "sub", [(i, i + 1 if i % 2 else i - 1) for i in inner])


def exchanged(block, distance):
    return lax.ppermute(block, "grp", [(i, i ^ distance) for i in range(lax.axis_size("grp"))])


def shape(*dims, dtype=F32):
    return jax.ShapeDtypeStruct(dims, dtype)


def call(kernel, out_shape, count=0, kept=0, scratch=(), flops=0, moved=0, name=None):
    specs = [pl.BlockSpec(memory_space=pltpu.VMEM)] * count + [pl.BlockSpec(memory_space=pltpu.HBM)] * kept
    out_specs = jax.tree.map(lambda _: pl.BlockSpec(memory_space=pltpu.VMEM), out_shape)
    return pl.pallas_call(
        kernel,
        out_shape=out_shape,
        in_specs=specs,
        out_specs=out_specs,
        scratch_shapes=list(scratch),
        compiler_params=pltpu.CompilerParams(vmem_limit_bytes=24 * 1024 * 1024),
        cost_estimate=pl.CostEstimate(flops=flops, bytes_accessed=moved, transcendentals=0),
        name=name,
    )


def on_device(
    gap_data,
    local_inverse,
    stiffness,
    stiff_column,
    neighbour,
    corner_ops,
    corner_index,
    coarse_inverse,
):
    iface, _, cells = gap_data.shape
    ranks = lax.axis_size("grp")
    sub_count = lax.axis_size("sub")
    right_side = gap_data[:, 0, :]
    inverse = local_inverse[:, :, 0, :]
    stiff = stiffness[:, :, :, 0, :]
    operators = corner_ops[:, :, 0, :]
    blocks_own, order = coarse_inverse.shape[:2]
    owned = blocks_own * (order // CORNER_DOF)
    group = owned * ranks
    corners = corner_index.reshape(1, CORNERS_SUB * cells)

    previous = shifted(right_side, 1)
    indices = (neighbour, stiff_column, corners)
    large = (stiff, operators, right_side)
    selector, swap, table, stiff, operators, right_side = call(
        table_kernel,
        (
            shape(2 * cells, cells, dtype=BF16),
            shape(cells, cells, dtype=BF16),
            shape(group, CORNERS_SUB * cells, dtype=BF16),
        )
        + tuple(jax.ShapeDtypeStruct(array.shape, array.dtype) for array in large),
        kept=3 + LOADED,
        scratch=[pltpu.VMEM(array.shape, jnp.int32) for array in indices] + [pltpu.SemaphoreType.DMA((3 + LOADED,))],
        moved=4 * iface * iface * cells,
        name="tables",
    )(*(pltpu.with_memory_space_constraint(array, pltpu.HBM) for array in indices + large))

    field = shape(iface, cells)
    pair = shape(2, iface, cells)
    message = shape(iface + ROWS, cells)
    rows = shape(ROWS, cells)
    piece = shape(ROWS, owned)
    stiff_scratch = [pltpu.VMEM((iface, cells), F32)]
    stiff_cost = dict(flops=4 * iface * iface * cells, moved=4 * iface * iface * cells)

    def apply_operator(near, far, extra):
        from_far, from_near = swapped_far(far), swapped(near, 1)
        m, gap, sent, *parts, dots = call(
            lambda *refs: corner_kernel(ranks, *refs),
            (field, field) + (piece,) * (ranks + 1) + (rows,),
            count=7,
            scratch=[pltpu.VMEM((ROWS, group), F32)],
            flops=2 * 24 * iface * cells,
            moved=2 * 24 * iface * cells + group * CORNERS_SUB * cells * 2,
            name="corners",
        )(far, near, from_far, from_near, selector, operators, table)
        arrivals = [exchanged(parts[ranks - 1 - d], d) for d in range(ranks - 1, 0, -1)] + [parts[ranks - 1]]
        local = call(
            local_kernel,
            field,
            count=2,
            flops=2 * iface * iface * cells,
            moved=2 * iface * iface * cells,
            name="local",
        )(gap, inverse)
        other = swapped(sent, 2) if extra == "dots" else sent
        solved = call(
            lambda *refs: coarse_kernel(ranks, *refs),
            piece,
            count=3 + ranks,
            scratch=[pltpu.VMEM((ranks, ROWS, owned), F32)],
            flops=2 * blocks_own * order * order,
            moved=2 * blocks_own * order * order,
            name="coarse",
        )(coarse_inverse, dots, other, *arrivals)
        values = [solved] + [exchanged(solved, d) for d in range(1, ranks)]
        far, near, *result = call(
            lambda *refs: lift_kernel(ranks, extra, *refs),
            (field, field) + {"": (), "dots": (rows,), "lifted": (field,)}[extra],
            count=4 + ranks,
            scratch=[pltpu.VMEM((ROWS, group), F32)],
            flops=2 * 24 * iface * cells,
            moved=2 * 24 * iface * cells + group * CORNERS_SUB * cells * 2,
            name="lift",
        )(local, operators, table, selector, *values)
        return m, gap, near, far, *result

    far, near = call(
        first_kernel, (message, message), count=5, scratch=stiff_scratch, name="first", **stiff_cost
    )(right_side, previous, selector, swap, stiff)
    u, gap_u, near, far = apply_operator(near, far, "")
    r = right_side
    from_far, from_near = swapped_far(far), swapped(near, 1)
    far, near, w = call(
        second_kernel,
        (message, message, pair),
        count=9,
        scratch=stiff_scratch,
        name="second",
        **stiff_cost,
    )(far, near, from_far, from_near, r, u, selector, swap, stiff)

    states = (jnp.zeros((ROWS, cells), F32), r, r, u, w, r, r, r, w, gap_u, r, r)
    outs = (rows, field, field, field, pair, field, field, field, pair, field, field, field, message, message)
    for step in range(ITERS - 2):
        m, gap, near, far, dots = apply_operator(near, far, "dots")
        from_far, from_near, other = swapped_far(far), swapped(near, 1), swapped(dots, 4)
        bit = 8
        while bit < sub_count:
            dots = dots + other
            other = swapped(dots, bit)
            bit *= 2
        *states, far, near = call(
            lambda *refs, first=step == 0: middle_kernel(first, *refs),
            outs,
            count=11 + STATES,
            scratch=stiff_scratch,
            name="middle",
            **stiff_cost,
        )(far, near, from_far, from_near, dots, other, m, gap, selector, swap, stiff, *states)
    scalars, x, r, u, w, p, s, q, z, gap_u, gap_p, gap_q = states
    m, gap, near, far, lifted = apply_operator(near, far, "lifted")
    from_far, from_near = swapped_far(far), swapped(near, 1)
    parts = call(gram_kernel, shape(sub_count * ranks, 1, cells), count=13, name="gram")(
        r, u, w, p, s, q, z, m, gap_u, gap_p, gap_q, gap, lifted
    )
    everyone = lax.all_to_all(parts, ("sub", "grp"), 0, 0, tiled=True)
    x, r = call(final_kernel, (field, field), count=15, name="final")(
        everyone, scalars, x, r, u, w, p, s, q, z, m, far, near, from_far, from_near
    )
    return (x[:, None, :], r[:, None, :])


def solution(mesh):
    in_specs = (
        P(None, "grp", "sub"),
        P(None, None, "grp", "sub"),
        P(None, None, None, "grp", "sub"),
        P("grp", "sub"),
        P("grp", "sub"),
        P(None, None, "grp", "sub"),
        P(None, "grp", "sub"),
        P("grp", None, "sub"),
    )
    out_specs = (P(None, "grp", "sub"), P(None, "grp", "sub"))
    return jax.shard_map(
        on_device, mesh=mesh, in_specs=in_specs, out_specs=out_specs, check_vma=False
    )
```

```python
import jax
import jax.numpy as jnp
from jax import lax
from jax.experimental import pallas as pl
from jax.experimental.pallas import tpu as pltpu
from jax.sharding import PartitionSpec as P

CORNER_DOF = 6
CORNERS_SUB = 4
ITERS = 5
ROWS = 8
STATES = 12
LOADED = 3
NN = (((1,), (0,)), ((), ()))
NT = (((1,), (1,)), ((), ()))
F32 = jnp.float32
BF16 = jnp.bfloat16


def pieces_of(value):
    high = value.astype(BF16).astype(F32)
    rest = value - high
    middle = rest.astype(BF16).astype(F32)
    return [high, middle, rest - middle]


def exact_dot(value, table, dims):
    rows = value.shape[0]
    stacked = jnp.concatenate(pieces_of(value), axis=0).astype(BF16)
    product = lax.dot_general(stacked, table, dims, preferred_element_type=F32)
    return product[:rows] + product[rows : 2 * rows] + product[2 * rows :]


def lane_total(rows):
    return jnp.sum(rows, axis=1, keepdims=True)


def dot_rows(r, u, w, s=None, p=None):
    rows = [jnp.sum(r * u, axis=0, keepdims=True), jnp.sum(u * w, axis=0, keepdims=True)]
    if s is None:
        rows.append(jnp.zeros((ROWS - 2, r.shape[1]), F32))
    else:
        rows.append(jnp.sum(u * s, axis=0, keepdims=True))
        rows.append(jnp.sum(p * w, axis=0, keepdims=True))
        rows.append(jnp.zeros((ROWS - 4, r.shape[1]), F32))
    return jnp.concatenate(rows, axis=0)


def packed(rows):
    row = lax.broadcasted_iota(jnp.int32, rows.shape, 0)
    lane = lax.broadcasted_iota(jnp.int32, rows.shape, 1)
    return jnp.sum(jnp.where(row == lane, lane_total(rows), 0.0), axis=0, keepdims=True)


def step_sizes(sums, before):
    norm, curvature, crossed, other = sums
    if before is None:
        beta = None
    else:
        beta = norm / before[0:1, 0:1]
        curvature = curvature + beta * (crossed + other) + beta * beta * before[1:2, 0:1]
    return norm / curvature, beta, norm, curvature


def collect_to(odd, vector, selector, near_ref, far_ref):
    iface, cells = vector.shape
    moved = exact_dot(vector, selector, NT)
    low = moved[:, :cells]
    high = vector - moved[:, cells:]
    near_ref[:iface] = jnp.where(odd, low, high)
    far_ref[:iface] = jnp.where(odd, high, low)


def spread_of(own, previous, selector):
    return own - exact_dot(jnp.concatenate([previous, own], axis=1), selector, NN)


def apply_blocks(blocks, vectors, out_ref):
    def step(index, carry):
        at = pl.ds(index * ROWS, ROWS)
        total = None
        for block, vector in zip(blocks, vectors):
            term = block[at].astype(F32) * vector[None]
            total = term if total is None else total + term
        out_ref[pl.ds(pl.multiple_of(index * ROWS, ROWS), ROWS)] = jnp.sum(total, axis=1)
        return carry

    lax.fori_loop(0, out_ref.shape[0] // ROWS, step, 0, unroll=True)


def table_kernel(*refs):
    sources, (selector_ref, swap_ref, table_ref), sems = refs[: LOADED + 3], refs[LOADED + 3 : LOADED + 6], refs[-1]
    neighbour_ref, column_ref, corner_ref = refs[-4:-1]
    targets = refs[-4:-1] + refs[LOADED + 6 : -4]
    copies = [pltpu.make_async_copy(sources[k], targets[k], sems.at[k]) for k in range(LOADED + 3)]
    for copy in copies:
        copy.start()
    for copy in copies[:3]:
        copy.wait()
    cells = swap_ref.shape[0]
    start = lax.axis_index("sub") * cells

    def one_hot(row, count):
        places = lax.broadcasted_iota(jnp.int32, (count, row.shape[1]), 0)
        return jnp.where(places == row, 1.0, 0.0).astype(BF16)

    neighbour = neighbour_ref[...]
    slots = jnp.where(neighbour < 0, -1, neighbour - (start - cells))
    selector_ref[...] = one_hot(slots, selector_ref.shape[0])
    swap_ref[...] = one_hot(column_ref[...] - start, swap_ref.shape[0])
    chunk = 128

    def step(index, carry):
        row = corner_ref[...] - index * chunk
        table_ref[pl.ds(pl.multiple_of(index * chunk, chunk), chunk)] = one_hot(row, chunk)
        return carry

    lax.fori_loop(0, table_ref.shape[0] // chunk, step, 0)
    for copy in copies[3:]:
        copy.wait()


def stiffen(odd, own, previous, selector_ref, swap_ref, stiffness_ref, stiff_ref, near_ref, far_ref):
    gap = spread_of(own, previous, selector_ref[...])
    taken = exact_dot(gap, swap_ref[...], NN)
    apply_blocks([stiffness_ref.at[0], stiffness_ref.at[1]], [gap, taken], stiff_ref)
    collect_to(odd, stiff_ref[...], selector_ref[...], near_ref, far_ref)


def first_kernel(
    own_ref, previous_ref, selector_ref, swap_ref, stiffness_ref, far_ref, near_ref, stiff_ref
):
    iface, cells = own_ref.shape
    odd = lax.axis_index("sub") % 2 == 1
    stiffen(
        odd, own_ref[...], previous_ref[...], selector_ref, swap_ref, stiffness_ref, stiff_ref, near_ref, far_ref
    )
    near_ref[iface:] = jnp.zeros((ROWS, cells), F32)


def arrived(odd, near_ref, far_ref, from_far_ref, from_near_ref, iface):
    near, far = near_ref[:iface], far_ref[:iface]
    from_near, from_far = from_near_ref[:iface], from_far_ref[:iface]
    own = jnp.where(odd, far - from_far, near - from_near)
    previous = jnp.where(odd, from_near - near, from_far - far)
    return own, previous


def second_kernel(
    near_ref, far_ref, from_far_ref, from_near_ref, r_ref, u_ref, selector_ref, swap_ref, stiffness_ref,
    far_out, near_out, w_out, stiff_ref,
):
    iface = r_ref.shape[0]
    odd = lax.axis_index("sub") % 2 == 1
    w, w_previous = arrived(odd, near_ref, far_ref, from_far_ref, from_near_ref, iface)
    w_out[0] = w
    w_out[1] = w_previous
    dots = dot_rows(r_ref[...], u_ref[...], w)
    near_out[iface:] = dots
    stiffen(odd, w, w_previous, selector_ref, swap_ref, stiffness_ref, stiff_ref, near_out, far_out)


def update(first, refs, m, gap, n, n_previous, totals):
    scalars_in, x_in, r_in, u_in, w_in, p_in, s_in, q_in, z_in, gap_u_in, gap_p_in, gap_q_in = refs[:STATES]
    scalars_out, x_out, r_out, u_out, w_out, p_out, s_out, q_out, z_out, gap_u_out, gap_p_out, gap_q_out = refs[STATES:]
    sums = lane_total(totals)
    sums = [sums[k : k + 1] for k in range(4)]
    alpha, beta, norm, curvature = step_sizes(sums, None if first else scalars_in[...])
    cells = m.shape[1]
    scalars_out[...] = jnp.concatenate(
        [
            jnp.broadcast_to(norm, (1, cells)),
            jnp.broadcast_to(curvature, (1, cells)),
            jnp.zeros((ROWS - 2, cells), F32),
        ],
        axis=0,
    )

    def turned(fresh, kept):
        return fresh if first else fresh + beta * kept[...]

    u, w = u_in[...], w_in[0]
    p = turned(u, p_in)
    s = turned(w, s_in)
    q = turned(m, q_in)
    z = turned(n, None if first else z_in.at[0])
    p_out[...] = p
    s_out[...] = s
    x_out[...] = alpha * p if first else x_in[...] + alpha * p
    r = r_in[...] - alpha * s
    u = u - alpha * q
    w = w - alpha * z
    r_out[...] = r
    u_out[...] = u
    w_out[0] = w
    z_previous = turned(n_previous, None if first else z_in.at[1])
    previous = w_in[1] - alpha * z_previous
    q_out[...] = q
    z_out[0] = z
    z_out[1] = z_previous
    w_out[1] = previous
    gap_u = gap_u_in[...]
    gap_q = turned(gap, gap_q_in)
    gap_p_out[...] = turned(gap_u, gap_p_in)
    gap_q_out[...] = gap_q
    gap_u_out[...] = gap_u - alpha * gap_q
    return dot_rows(r, u, w, s, p), w, previous


def middle_kernel(first, *refs):
    (near_ref, far_ref, from_far_ref, from_near_ref, dots_ref, dots_other_ref, m_ref, gap_ref) = refs[:8]
    (selector_ref, swap_ref, stiffness_ref) = refs[8:11]
    states = list(refs[11 : 11 + 2 * STATES])
    far_out, near_out, stiff_ref = refs[11 + 2 * STATES :]
    m = m_ref[...]
    iface = m.shape[0]
    odd = lax.axis_index("sub") % 2 == 1
    n, n_previous = arrived(odd, near_ref, far_ref, from_far_ref, from_near_ref, iface)
    dots, w, previous = update(
        first, states, m, gap_ref[...], n, n_previous, dots_ref[...] + dots_other_ref[...]
    )
    near_out[iface:] = dots
    stiffen(odd, w, previous, selector_ref, swap_ref, stiffness_ref, stiff_ref, near_out, far_out)


def corner_kernel(
    ranks, near_ref, far_ref, from_far_ref, from_near_ref, selector_ref, operators_ref, table_ref,
    m_out, gap_out, *rest,
):
    dots_sent, outs, (dots_out, sums_ref) = rest[0], rest[1 : ranks + 1], rest[ranks + 1 :]
    iface, cells = m_out.shape
    odd = lax.axis_index("sub") % 2 == 1
    own, previous = arrived(odd, near_ref, far_ref, from_far_ref, from_near_ref, iface)
    m_out[...] = own
    dots_sent[...] = jnp.zeros_like(dots_sent)
    dots = near_ref[iface:] + from_near_ref[iface:]
    dots_out[...] = dots
    dots_sent[:, :cells] = dots
    gap = spread_of(own, previous, selector_ref[...])
    gap_out[...] = gap
    parts = []
    for corner in range(CORNERS_SUB):
        at = slice(corner * CORNER_DOF, (corner + 1) * CORNER_DOF)
        part = jnp.sum(operators_ref[at].astype(F32) * gap[None], axis=1)
        parts.append(jnp.concatenate([part, jnp.zeros((ROWS - CORNER_DOF, cells), F32)], axis=0))
    sums_ref[...] = exact_dot(jnp.concatenate(parts, axis=1), table_ref[...], NT)
    owned = sums_ref.shape[1] // ranks
    for distance in range(ranks):
        rank = lax.axis_index("grp") ^ (ranks - 1 - distance)
        outs[distance][...] = sums_ref[:, pl.ds(pl.multiple_of(rank * owned, 128), owned)]


def local_kernel(gap_ref, inverse_ref, local_ref):
    apply_blocks([inverse_ref], [gap_ref[...]], local_ref)


def coarse_kernel(ranks, coarse_ref, dots_ref, other_ref, *rest):
    pieces, (solved_ref, sums_ref) = rest[:ranks], rest[ranks:]
    cells = dots_ref.shape[1]
    for distance in range(ranks):
        rank = lax.axis_index("grp") ^ distance
        sums_ref[rank] = pieces[ranks - 1 - distance][...]
    total = sums_ref[0]
    for rank in range(1, ranks):
        total = total + sums_ref[rank]
    blocks, order = coarse_ref.shape[0], coarse_ref.shape[1]
    width = order // CORNER_DOF
    columns = []
    for block in range(blocks):
        lanes = slice(block * width, (block + 1) * width)
        row = jnp.concatenate([total[j : j + 1, lanes] for j in range(CORNER_DOF)], axis=1)
        parts = pieces_of(row) + [jnp.zeros((ROWS - 3, order), F32)]
        stacked = jnp.concatenate(parts, axis=0).astype(BF16)
        product = lax.dot_general(stacked, coarse_ref[block], NT, preferred_element_type=F32)
        result = product[0:1] + product[1:2] + product[2:3]
        rows = [result[:, j * width : (j + 1) * width] for j in range(CORNER_DOF)]
        columns.append(jnp.concatenate(rows, axis=0))
    solved = jnp.concatenate(columns, axis=1)
    dots = dots_ref[...] + other_ref[:, :cells]
    rows = [solved]
    for first in (0, 2):
        lanes = [dots[first : first + 1], dots[first + 1 : first + 2]]
        if solved.shape[1] > 2 * cells:
            lanes.append(jnp.zeros((1, solved.shape[1] - 2 * cells), F32))
        rows.append(jnp.concatenate(lanes, axis=1))
    solved_ref[...] = jnp.concatenate(rows, axis=0)


def lift_kernel(ranks, extra, local_ref, operators_ref, table_ref, selector_ref, *rest):
    pieces, (far_ref, near_ref), (*extra_out, values_ref) = rest[:ranks], rest[ranks : ranks + 2], rest[ranks + 2 :]
    cells = local_ref.shape[1]
    owned = values_ref.shape[1] // ranks
    for distance in range(ranks):
        rank = lax.axis_index("grp") ^ distance
        values_ref[:, pl.ds(pl.multiple_of(rank * owned, 128), owned)] = pieces[distance][...]
    values = values_ref[...]
    if extra == "dots":
        tail = values[CORNER_DOF:, :owned]
        for rank in range(1, ranks):
            tail = tail + values[CORNER_DOF:, rank * owned : (rank + 1) * owned]
        extra_out[0][...] = jnp.concatenate(
            [
                tail[0:1, :cells],
                tail[0:1, cells : 2 * cells],
                tail[1:2, :cells],
                tail[1:2, cells : 2 * cells],
                jnp.zeros((ROWS - 4, cells), F32),
            ],
            axis=0,
        )
    picked = exact_dot(values, table_ref[...], NN)
    lifted = local_ref[...]
    for corner in range(CORNERS_SUB):
        lanes = slice(corner * cells, (corner + 1) * cells)
        for dof in range(CORNER_DOF):
            operator = operators_ref[corner * CORNER_DOF + dof].astype(F32)
            lifted = lifted + operator * picked[dof : dof + 1, lanes]
    if extra == "lifted":
        extra_out[0][...] = lifted
    collect_to(lax.axis_index("sub") % 2 == 1, lifted, selector_ref[...], near_ref, far_ref)


def gram_kernel(
    r_ref, u_ref, w_ref, p_ref, s_ref, q_ref, z_ref, m_ref, gap_u_ref, gap_p_ref, gap_q_ref, gap_ref, lifted_ref, out_ref
):
    left = [u_ref[...], m_ref[...], q_ref[...], p_ref[...]]
    gaps = [gap_u_ref[...], gap_ref[...], gap_q_ref[...], gap_p_ref[...]]
    w, z, s = w_ref[0], z_ref[0], s_ref[...]
    r, lifted = r_ref[...], lifted_ref[...]
    products = []
    for v, gap in zip(left, gaps):
        products += [v * w, gap * lifted, v * z, v * s]
    products += [r * v for v in left[:3]]
    rows = [jnp.sum(product, axis=0, keepdims=True) for product in products]
    rows.append(jnp.zeros((-len(rows) % ROWS, r.shape[1]), F32))
    out_ref[...] = jnp.broadcast_to(packed(jnp.concatenate(rows, axis=0))[None], out_ref.shape)


def final_kernel(
    dots_ref, scalars_ref, x_ref, r_ref, u_ref, w_ref, p_ref, s_ref, q_ref, z_ref, m_ref,
    near_ref, far_ref, from_far_ref, from_near_ref, x_out, r_out,
):
    totals = jnp.sum(dots_ref[...], axis=0)
    gram = [[totals[:, 4 * i + k : 4 * i + k + 1] for k in range(4)] for i in range(4)]
    with_r = [totals[:, 16 + i : 17 + i] for i in range(3)]

    def form(first, second):
        total = None
        for i, left in first.items():
            row = None
            for k, right in second.items():
                term = gram[i][k] * right
                row = term if row is None else row + term
            total = left * row if total is None else total + left * row
        return total

    norm = with_r[0]
    beta = norm / scalars_ref[0:1, 0:1]
    one = jnp.ones_like(norm)
    turned = {0: one, 3: beta}
    alpha = norm / form(turned, turned)
    stepped = {0: one, 1: -alpha, 2: -alpha * beta}
    norm_next = with_r[0] + stepped[1] * with_r[1] + stepped[2] * with_r[2] - alpha * form(stepped, turned)
    beta_next = norm_next / norm
    turned_next = {0: one + beta_next, 1: stepped[1], 2: stepped[2], 3: beta_next * beta}
    alpha_next = norm_next / form(turned_next, turned_next)

    odd = lax.axis_index("sub") % 2 == 1
    n, _ = arrived(odd, near_ref, far_ref, from_far_ref, from_near_ref, r_ref.shape[0])
    p = u_ref[...] + beta * p_ref[...]
    s = w_ref[0] + beta * s_ref[...]
    u = u_ref[...] - alpha * (m_ref[...] + beta * q_ref[...])
    w = w_ref[0] - alpha * (n + beta * z_ref[0])
    x_out[...] = x_ref[...] + alpha * p + alpha_next * (u + beta_next * p)
    r_out[...] = r_ref[...] - alpha * s - alpha_next * (w + beta_next * s)


def shifted(block, distance):
    count = lax.axis_size("sub")
    route = [(i, i + distance) for i in range(count) if 0 <= i + distance < count]
    return lax.ppermute(block, "sub", route)


def swapped(block, bit):
    return lax.ppermute(block, "sub", [(i, i ^ bit) for i in range(lax.axis_size("sub"))])


def swapped_far(block):
    inner = range(1, lax.axis_size("sub") - 1)
    return lax.ppermute(block, "sub", [(i, i + 1 if i % 2 else i - 1) for i in inner])


def exchanged(block, distance):
    return lax.ppermute(block, "grp", [(i, i ^ distance) for i in range(lax.axis_size("grp"))])


def shape(*dims, dtype=F32):
    return jax.ShapeDtypeStruct(dims, dtype)


def call(kernel, out_shape, count=0, kept=0, scratch=(), flops=0, moved=0, name=None):
    specs = [pl.BlockSpec(memory_space=pltpu.VMEM)] * count + [pl.BlockSpec(memory_space=pltpu.HBM)] * kept
    out_specs = jax.tree.map(lambda _: pl.BlockSpec(memory_space=pltpu.VMEM), out_shape)
    return pl.pallas_call(
        kernel,
        out_shape=out_shape,
        in_specs=specs,
        out_specs=out_specs,
        scratch_shapes=list(scratch),
        compiler_params=pltpu.CompilerParams(vmem_limit_bytes=24 * 1024 * 1024),
        cost_estimate=pl.CostEstimate(flops=flops, bytes_accessed=moved, transcendentals=0),
        name=name,
    )


def on_device(
    gap_data,
    local_inverse,
    stiffness,
    stiff_column,
    neighbour,
    corner_ops,
    corner_index,
    coarse_inverse,
):
    iface, _, cells = gap_data.shape
    ranks = lax.axis_size("grp")
    sub_count = lax.axis_size("sub")
    right_side = gap_data[:, 0, :]
    inverse = local_inverse[:, :, 0, :]
    stiff = stiffness[:, :, :, 0, :]
    operators = corner_ops[:, :, 0, :]
    blocks_own, order = coarse_inverse.shape[:2]
    owned = blocks_own * (order // CORNER_DOF)
    group = owned * ranks
    corners = corner_index.reshape(1, CORNERS_SUB * cells)

    previous = shifted(right_side, 1)
    indices = (neighbour, stiff_column, corners)
    large = (stiff, operators, right_side)
    selector, swap, table, stiff, operators, right_side = call(
        table_kernel,
        (
            shape(2 * cells, cells, dtype=BF16),
            shape(cells, cells, dtype=BF16),
            shape(group, CORNERS_SUB * cells, dtype=BF16),
        )
        + tuple(jax.ShapeDtypeStruct(array.shape, array.dtype) for array in large),
        kept=3 + LOADED,
        scratch=[pltpu.VMEM(array.shape, jnp.int32) for array in indices] + [pltpu.SemaphoreType.DMA((3 + LOADED,))],
        moved=4 * iface * iface * cells,
        name="tables",
    )(*(pltpu.with_memory_space_constraint(array, pltpu.HBM) for array in indices + large))

    field = shape(iface, cells)
    pair = shape(2, iface, cells)
    message = shape(iface + ROWS, cells)
    rows = shape(ROWS, cells)
    piece = shape(ROWS, owned)
    stiff_scratch = [pltpu.VMEM((iface, cells), F32)]
    stiff_cost = dict(flops=4 * iface * iface * cells, moved=4 * iface * iface * cells)

    def apply_operator(near, far, extra):
        from_far, from_near = swapped_far(far), swapped(near, 1)
        m, gap, sent, *parts, dots = call(
            lambda *refs: corner_kernel(ranks, *refs),
            (field, field) + (piece,) * (ranks + 1) + (rows,),
            count=7,
            scratch=[pltpu.VMEM((ROWS, group), F32)],
            flops=2 * 24 * iface * cells,
            moved=2 * 24 * iface * cells + group * CORNERS_SUB * cells * 2,
            name="corners",
        )(near, far, from_far, from_near, selector, operators, table)
        arrivals = [exchanged(parts[ranks - 1 - d], d) for d in range(ranks - 1, 0, -1)] + [parts[ranks - 1]]
        local = call(
            local_kernel,
            field,
            count=2,
            flops=2 * iface * iface * cells,
            moved=2 * iface * iface * cells,
            name="local",
        )(gap, inverse)
        other = swapped(sent, 2) if extra == "dots" else sent
        solved = call(
            lambda *refs: coarse_kernel(ranks, *refs),
            piece,
            count=3 + ranks,
            scratch=[pltpu.VMEM((ranks, ROWS, owned), F32)],
            flops=2 * blocks_own * order * order,
            moved=2 * blocks_own * order * order,
            name="coarse",
        )(coarse_inverse, dots, other, *arrivals)
        values = [solved] + [exchanged(solved, d) for d in range(1, ranks)]
        far, near, *result = call(
            lambda *refs: lift_kernel(ranks, extra, *refs),
            (field, field) + {"": (), "dots": (rows,), "lifted": (field,)}[extra],
            count=4 + ranks,
            scratch=[pltpu.VMEM((ROWS, group), F32)],
            flops=2 * 24 * iface * cells,
            moved=2 * 24 * iface * cells + group * CORNERS_SUB * cells * 2,
            name="lift",
        )(local, operators, table, selector, *values)
        return m, gap, near, far, *result

    far, near = call(
        first_kernel, (field, message), count=5, scratch=stiff_scratch, name="first", **stiff_cost
    )(right_side, previous, selector, swap, stiff)
    u, gap_u, near, far = apply_operator(near, far, "")
    r = right_side
    from_far, from_near = swapped_far(far), swapped(near, 1)
    far, near, w = call(
        second_kernel,
        (field, message, pair),
        count=9,
        scratch=stiff_scratch,
        name="second",
        **stiff_cost,
    )(near, far, from_far, from_near, r, u, selector, swap, stiff)

    states = (jnp.zeros((ROWS, cells), F32), r, r, u, w, r, r, r, w, gap_u, r, r)
    outs = (rows, field, field, field, pair, field, field, field, pair, field, field, field, field, message)
    for step in range(ITERS - 2):
        m, gap, near, far, dots = apply_operator(near, far, "dots")
        from_far, from_near, other = swapped_far(far), swapped(near, 1), swapped(dots, 4)
        bit = 8
        while bit < sub_count:
            dots = dots + other
            other = swapped(dots, bit)
            bit *= 2
        *states, far, near = call(
            lambda *refs, first=step == 0: middle_kernel(first, *refs),
            outs,
            count=11 + STATES,
            scratch=stiff_scratch,
            name="middle",
            **stiff_cost,
        )(near, far, from_far, from_near, dots, other, m, gap, selector, swap, stiff, *states)
    scalars, x, r, u, w, p, s, q, z, gap_u, gap_p, gap_q = states
    m, gap, near, far, lifted = apply_operator(near, far, "lifted")
    from_far, from_near = swapped_far(far), swapped(near, 1)
    parts = call(gram_kernel, shape(sub_count * ranks, 1, cells), count=13, name="gram")(
        r, u, w, p, s, q, z, m, gap_u, gap_p, gap_q, gap, lifted
    )
    everyone = lax.all_to_all(parts, ("sub", "grp"), 0, 0, tiled=True)
    x, r = call(final_kernel, (field, field), count=15, name="final")(
        everyone, scalars, x, r, u, w, p, s, q, z, m, near, far, from_far, from_near
    )
    return (x[:, None, :], r[:, None, :])


def solution(mesh):
    in_specs = (
        P(None, "grp", "sub"),
        P(None, None, "grp", "sub"),
        P(None, None, None, "grp", "sub"),
        P("grp", "sub"),
        P("grp", "sub"),
        P(None, None, "grp", "sub"),
        P(None, "grp", "sub"),
        P("grp", None, "sub"),
    )
    out_specs = (P(None, "grp", "sub"), P(None, "grp", "sub"))
    return jax.shard_map(
        on_device, mesh=mesh, in_specs=in_specs, out_specs=out_specs, check_vma=False
    )
```

```python
import jax
import jax.numpy as jnp
from jax import lax
from jax.experimental import pallas as pl
from jax.experimental.pallas import tpu as pltpu
from jax.sharding import PartitionSpec as P

CORNER_DOF = 6
CORNERS_SUB = 4
ITERS = 5
ROWS = 8
STATES = 12
LOADED = 3
NN = (((1,), (0,)), ((), ()))
NT = (((1,), (1,)), ((), ()))
F32 = jnp.float32
BF16 = jnp.bfloat16


def pieces_of(value):
    high = value.astype(BF16).astype(F32)
    rest = value - high
    middle = rest.astype(BF16).astype(F32)
    return [high, middle, rest - middle]


def exact_dot(value, table, dims):
    rows = value.shape[0]
    stacked = jnp.concatenate(pieces_of(value), axis=0).astype(BF16)
    product = lax.dot_general(stacked, table, dims, preferred_element_type=F32)
    return product[:rows] + product[rows : 2 * rows] + product[2 * rows :]


def lane_total(rows):
    return jnp.sum(rows, axis=1, keepdims=True)


def dot_rows(r, u, w, s=None, p=None):
    rows = [jnp.sum(r * u, axis=0, keepdims=True), jnp.sum(u * w, axis=0, keepdims=True)]
    if s is None:
        rows.append(jnp.zeros((ROWS - 2, r.shape[1]), F32))
    else:
        rows.append(jnp.sum(u * s, axis=0, keepdims=True))
        rows.append(jnp.sum(p * w, axis=0, keepdims=True))
        rows.append(jnp.zeros((ROWS - 4, r.shape[1]), F32))
    return jnp.concatenate(rows, axis=0)


def packed(rows):
    row = lax.broadcasted_iota(jnp.int32, rows.shape, 0)
    lane = lax.broadcasted_iota(jnp.int32, rows.shape, 1)
    return jnp.sum(jnp.where(row == lane, lane_total(rows), 0.0), axis=0, keepdims=True)


def step_sizes(sums, before):
    norm, curvature, crossed, other = sums
    if before is None:
        beta = None
    else:
        beta = norm / before[0:1, 0:1]
        curvature = curvature + beta * (crossed + other) + beta * beta * before[1:2, 0:1]
    return norm / curvature, beta, norm, curvature


def collect_to(odd, vector, selector, near_ref, far_ref):
    iface, cells = vector.shape
    moved = exact_dot(vector, selector, NT)
    low = moved[:, :cells]
    high = vector - moved[:, cells:]
    near_ref[:iface] = jnp.where(odd, low, high)
    far_ref[:iface] = jnp.where(odd, high, low)


def spread_of(own, previous, selector):
    return own - exact_dot(jnp.concatenate([previous, own], axis=1), selector, NN)


def apply_blocks(blocks, vectors, out_ref):
    def step(index, carry):
        at = pl.ds(index * ROWS, ROWS)
        total = None
        for block, vector in zip(blocks, vectors):
            term = block[at].astype(F32) * vector[None]
            total = term if total is None else total + term
        out_ref[pl.ds(pl.multiple_of(index * ROWS, ROWS), ROWS)] = jnp.sum(total, axis=1)
        return carry

    lax.fori_loop(0, out_ref.shape[0] // ROWS, step, 0, unroll=True)


def table_kernel(*refs):
    sources, (selector_ref, swap_ref, table_ref), sems = refs[: LOADED + 3], refs[LOADED + 3 : LOADED + 6], refs[-1]
    neighbour_ref, column_ref, corner_ref = refs[-4:-1]
    targets = refs[-4:-1] + refs[LOADED + 6 : -4]
    copies = [pltpu.make_async_copy(sources[k], targets[k], sems.at[k]) for k in range(LOADED + 3)]
    for copy in copies:
        copy.start()
    for copy in copies[:3]:
        copy.wait()
    cells = swap_ref.shape[0]
    start = lax.axis_index("sub") * cells

    def one_hot(row, count):
        places = lax.broadcasted_iota(jnp.int32, (count, row.shape[1]), 0)
        return jnp.where(places == row, 1.0, 0.0).astype(BF16)

    neighbour = neighbour_ref[...]
    slots = jnp.where(neighbour < 0, -1, neighbour - (start - cells))
    selector_ref[...] = one_hot(slots, selector_ref.shape[0])
    swap_ref[...] = one_hot(column_ref[...] - start, swap_ref.shape[0])
    chunk = 128

    def step(index, carry):
        row = corner_ref[...] - index * chunk
        table_ref[pl.ds(pl.multiple_of(index * chunk, chunk), chunk)] = one_hot(row, chunk)
        return carry

    lax.fori_loop(0, table_ref.shape[0] // chunk, step, 0)
    for copy in copies[3:]:
        copy.wait()


def stiffen(odd, own, previous, selector_ref, swap_ref, stiffness_ref, stiff_ref, near_ref, far_ref):
    gap = spread_of(own, previous, selector_ref[...])
    taken = exact_dot(gap, swap_ref[...], NN)
    apply_blocks([stiffness_ref.at[0], stiffness_ref.at[1]], [gap, taken], stiff_ref)
    collect_to(odd, stiff_ref[...], selector_ref[...], near_ref, far_ref)


def first_kernel(
    own_ref, previous_ref, selector_ref, swap_ref, stiffness_ref, far_ref, near_ref, stiff_ref
):
    iface, cells = own_ref.shape
    odd = lax.axis_index("sub") % 2 == 1
    stiffen(
        odd, own_ref[...], previous_ref[...], selector_ref, swap_ref, stiffness_ref, stiff_ref, near_ref, far_ref
    )
    near_ref[iface:] = jnp.zeros((ROWS, cells), F32)


def arrived(odd, near_ref, far_ref, from_far_ref, from_near_ref, iface):
    near, far = near_ref[:iface], far_ref[:iface]
    from_near, from_far = from_near_ref[:iface], from_far_ref[:iface]
    own = jnp.where(odd, far - from_far, near - from_near)
    previous = jnp.where(odd, from_near - near, from_far - far)
    return own, previous


def second_kernel(
    near_ref, far_ref, from_far_ref, from_near_ref, r_ref, u_ref, selector_ref, swap_ref, stiffness_ref,
    far_out, near_out, w_out, stiff_ref,
):
    iface = r_ref.shape[0]
    odd = lax.axis_index("sub") % 2 == 1
    w, w_previous = arrived(odd, near_ref, far_ref, from_far_ref, from_near_ref, iface)
    w_out[0] = w
    w_out[1] = w_previous
    dots = dot_rows(r_ref[...], u_ref[...], w)
    near_out[iface:] = dots
    stiffen(odd, w, w_previous, selector_ref, swap_ref, stiffness_ref, stiff_ref, near_out, far_out)


def update(first, refs, m, gap, n, n_previous, totals):
    scalars_in, x_in, r_in, u_in, w_in, p_in, s_in, q_in, z_in, gap_u_in, gap_p_in, gap_q_in = refs[:STATES]
    scalars_out, x_out, r_out, u_out, w_out, p_out, s_out, q_out, z_out, gap_u_out, gap_p_out, gap_q_out = refs[STATES:]
    sums = lane_total(totals)
    sums = [sums[k : k + 1] for k in range(4)]
    alpha, beta, norm, curvature = step_sizes(sums, None if first else scalars_in[...])
    cells = m.shape[1]
    scalars_out[...] = jnp.concatenate(
        [
            jnp.broadcast_to(norm, (1, cells)),
            jnp.broadcast_to(curvature, (1, cells)),
            jnp.zeros((ROWS - 2, cells), F32),
        ],
        axis=0,
    )

    def turned(fresh, kept):
        return fresh if first else fresh + beta * kept[...]

    u, w = u_in[...], w_in[0]
    p = turned(u, p_in)
    s = turned(w, s_in)
    q = turned(m, q_in)
    z = turned(n, None if first else z_in.at[0])
    p_out[...] = p
    s_out[...] = s
    x_out[...] = alpha * p if first else x_in[...] + alpha * p
    r = r_in[...] - alpha * s
    u = u - alpha * q
    w = w - alpha * z
    r_out[...] = r
    u_out[...] = u
    w_out[0] = w
    z_previous = turned(n_previous, None if first else z_in.at[1])
    previous = w_in[1] - alpha * z_previous
    q_out[...] = q
    z_out[0] = z
    z_out[1] = z_previous
    w_out[1] = previous
    gap_u = gap_u_in[...]
    gap_q = turned(gap, gap_q_in)
    gap_p_out[...] = turned(gap_u, gap_p_in)
    gap_q_out[...] = gap_q
    gap_u_out[...] = gap_u - alpha * gap_q
    return dot_rows(r, u, w, s, p), w, previous


def middle_kernel(first, *refs):
    (near_ref, far_ref, from_far_ref, from_near_ref, dots_ref, dots_other_ref, m_ref, gap_ref) = refs[:8]
    (selector_ref, swap_ref, stiffness_ref) = refs[8:11]
    states = list(refs[11 : 11 + 2 * STATES])
    far_out, near_out, stiff_ref = refs[11 + 2 * STATES :]
    m = m_ref[...]
    iface = m.shape[0]
    odd = lax.axis_index("sub") % 2 == 1
    n, n_previous = arrived(odd, near_ref, far_ref, from_far_ref, from_near_ref, iface)
    dots, w, previous = update(
        first, states, m, gap_ref[...], n, n_previous, dots_ref[...] + dots_other_ref[...]
    )
    near_out[iface:] = dots
    stiffen(odd, w, previous, selector_ref, swap_ref, stiffness_ref, stiff_ref, near_out, far_out)


def corner_kernel(
    ranks, near_ref, far_ref, from_far_ref, from_near_ref, selector_ref, operators_ref, table_ref,
    m_out, gap_out, *rest,
):
    outs, (dots_out, sums_ref) = (rest[0], *rest[2 : ranks + 1]), rest[ranks + 1 :]
    dots_sent = rest[1]
    iface, cells = m_out.shape
    odd = lax.axis_index("sub") % 2 == 1
    own, previous = arrived(odd, near_ref, far_ref, from_far_ref, from_near_ref, iface)
    m_out[...] = own
    dots_sent[...] = jnp.zeros_like(dots_sent)
    dots = near_ref[iface:] + from_near_ref[iface:]
    dots_out[...] = dots
    dots_sent[:, :cells] = dots
    gap = spread_of(own, previous, selector_ref[...])
    gap_out[...] = gap
    parts = []
    for corner in range(CORNERS_SUB):
        at = slice(corner * CORNER_DOF, (corner + 1) * CORNER_DOF)
        part = jnp.sum(operators_ref[at].astype(F32) * gap[None], axis=1)
        parts.append(jnp.concatenate([part, jnp.zeros((ROWS - CORNER_DOF, cells), F32)], axis=0))
    sums_ref[...] = exact_dot(jnp.concatenate(parts, axis=1), table_ref[...], NT)
    owned = sums_ref.shape[1] // ranks
    for distance in range(ranks):
        rank = lax.axis_index("grp") ^ (ranks - 1 - distance)
        outs[distance][...] = sums_ref[:, pl.ds(pl.multiple_of(rank * owned, 128), owned)]


def local_kernel(gap_ref, inverse_ref, local_ref):
    apply_blocks([inverse_ref], [gap_ref[...]], local_ref)


def coarse_kernel(ranks, coarse_ref, dots_ref, farthest_ref, other_ref, *rest):
    pieces, (solved_ref, sums_ref) = (farthest_ref, *rest[: ranks - 1]), rest[ranks - 1 :]
    cells = dots_ref.shape[1]
    for distance in range(ranks):
        rank = lax.axis_index("grp") ^ distance
        sums_ref[rank] = pieces[ranks - 1 - distance][...]
    total = sums_ref[0]
    for rank in range(1, ranks):
        total = total + sums_ref[rank]
    blocks, order = coarse_ref.shape[0], coarse_ref.shape[1]
    width = order // CORNER_DOF
    columns = []
    for block in range(blocks):
        lanes = slice(block * width, (block + 1) * width)
        row = jnp.concatenate([total[j : j + 1, lanes] for j in range(CORNER_DOF)], axis=1)
        parts = pieces_of(row) + [jnp.zeros((ROWS - 3, order), F32)]
        stacked = jnp.concatenate(parts, axis=0).astype(BF16)
        product = lax.dot_general(stacked, coarse_ref[block], NT, preferred_element_type=F32)
        result = product[0:1] + product[1:2] + product[2:3]
        rows = [result[:, j * width : (j + 1) * width] for j in range(CORNER_DOF)]
        columns.append(jnp.concatenate(rows, axis=0))
    solved = jnp.concatenate(columns, axis=1)
    dots = dots_ref[...] + other_ref[:, :cells]
    rows = [solved]
    for first in (0, 2):
        lanes = [dots[first : first + 1], dots[first + 1 : first + 2]]
        if solved.shape[1] > 2 * cells:
            lanes.append(jnp.zeros((1, solved.shape[1] - 2 * cells), F32))
        rows.append(jnp.concatenate(lanes, axis=1))
    solved_ref[...] = jnp.concatenate(rows, axis=0)


def lift_kernel(ranks, extra, local_ref, operators_ref, table_ref, selector_ref, *rest):
    pieces, (far_ref, near_ref), (*extra_out, values_ref) = rest[:ranks], rest[ranks : ranks + 2], rest[ranks + 2 :]
    cells = local_ref.shape[1]
    owned = values_ref.shape[1] // ranks
    for distance in range(ranks):
        rank = lax.axis_index("grp") ^ distance
        values_ref[:, pl.ds(pl.multiple_of(rank * owned, 128), owned)] = pieces[distance][...]
    values = values_ref[...]
    if extra == "dots":
        tail = values[CORNER_DOF:, :owned]
        for rank in range(1, ranks):
            tail = tail + values[CORNER_DOF:, rank * owned : (rank + 1) * owned]
        extra_out[0][...] = jnp.concatenate(
            [
                tail[0:1, :cells],
                tail[0:1, cells : 2 * cells],
                tail[1:2, :cells],
                tail[1:2, cells : 2 * cells],
                jnp.zeros((ROWS - 4, cells), F32),
            ],
            axis=0,
        )
    picked = exact_dot(values, table_ref[...], NN)
    lifted = local_ref[...]
    for corner in range(CORNERS_SUB):
        lanes = slice(corner * cells, (corner + 1) * cells)
        for dof in range(CORNER_DOF):
            operator = operators_ref[corner * CORNER_DOF + dof].astype(F32)
            lifted = lifted + operator * picked[dof : dof + 1, lanes]
    if extra == "lifted":
        extra_out[0][...] = lifted
    collect_to(lax.axis_index("sub") % 2 == 1, lifted, selector_ref[...], near_ref, far_ref)


def gram_kernel(
    r_ref, u_ref, w_ref, p_ref, s_ref, q_ref, z_ref, m_ref, gap_u_ref, gap_p_ref, gap_q_ref, gap_ref, lifted_ref, out_ref
):
    left = [u_ref[...], m_ref[...], q_ref[...], p_ref[...]]
    gaps = [gap_u_ref[...], gap_ref[...], gap_q_ref[...], gap_p_ref[...]]
    w, z, s = w_ref[0], z_ref[0], s_ref[...]
    r, lifted = r_ref[...], lifted_ref[...]
    products = []
    for v, gap in zip(left, gaps):
        products += [v * w, gap * lifted, v * z, v * s]
    products += [r * v for v in left[:3]]
    rows = [jnp.sum(product, axis=0, keepdims=True) for product in products]
    rows.append(jnp.zeros((-len(rows) % ROWS, r.shape[1]), F32))
    out_ref[...] = jnp.broadcast_to(packed(jnp.concatenate(rows, axis=0))[None], out_ref.shape)


def final_kernel(
    dots_ref, scalars_ref, x_ref, r_ref, u_ref, w_ref, p_ref, s_ref, q_ref, z_ref, m_ref,
    near_ref, far_ref, from_far_ref, from_near_ref, x_out, r_out,
):
    totals = jnp.sum(dots_ref[...], axis=0)
    gram = [[totals[:, 4 * i + k : 4 * i + k + 1] for k in range(4)] for i in range(4)]
    with_r = [totals[:, 16 + i : 17 + i] for i in range(3)]

    def form(first, second):
        total = None
        for i, left in first.items():
            row = None
            for k, right in second.items():
                term = gram[i][k] * right
                row = term if row is None else row + term
            total = left * row if total is None else total + left * row
        return total

    norm = with_r[0]
    beta = norm / scalars_ref[0:1, 0:1]
    one = jnp.ones_like(norm)
    turned = {0: one, 3: beta}
    alpha = norm / form(turned, turned)
    stepped = {0: one, 1: -alpha, 2: -alpha * beta}
    norm_next = with_r[0] + stepped[1] * with_r[1] + stepped[2] * with_r[2] - alpha * form(stepped, turned)
    beta_next = norm_next / norm
    turned_next = {0: one + beta_next, 1: stepped[1], 2: stepped[2], 3: beta_next * beta}
    alpha_next = norm_next / form(turned_next, turned_next)

    odd = lax.axis_index("sub") % 2 == 1
    n, _ = arrived(odd, near_ref, far_ref, from_far_ref, from_near_ref, r_ref.shape[0])
    p = u_ref[...] + beta * p_ref[...]
    s = w_ref[0] + beta * s_ref[...]
    u = u_ref[...] - alpha * (m_ref[...] + beta * q_ref[...])
    w = w_ref[0] - alpha * (n + beta * z_ref[0])
    x_out[...] = x_ref[...] + alpha * p + alpha_next * (u + beta_next * p)
    r_out[...] = r_ref[...] - alpha * s - alpha_next * (w + beta_next * s)


def shifted(block, distance):
    count = lax.axis_size("sub")
    route = [(i, i + distance) for i in range(count) if 0 <= i + distance < count]
    return lax.ppermute(block, "sub", route)


def swapped(block, bit):
    return lax.ppermute(block, "sub", [(i, i ^ bit) for i in range(lax.axis_size("sub"))])


def swapped_far(block):
    inner = range(1, lax.axis_size("sub") - 1)
    return lax.ppermute(block, "sub", [(i, i + 1 if i % 2 else i - 1) for i in inner])


def exchanged(block, distance):
    return lax.ppermute(block, "grp", [(i, i ^ distance) for i in range(lax.axis_size("grp"))])


def shape(*dims, dtype=F32):
    return jax.ShapeDtypeStruct(dims, dtype)


def call(kernel, out_shape, count=0, kept=0, scratch=(), flops=0, moved=0, name=None):
    specs = [pl.BlockSpec(memory_space=pltpu.VMEM)] * count + [pl.BlockSpec(memory_space=pltpu.HBM)] * kept
    out_specs = jax.tree.map(lambda _: pl.BlockSpec(memory_space=pltpu.VMEM), out_shape)
    return pl.pallas_call(
        kernel,
        out_shape=out_shape,
        in_specs=specs,
        out_specs=out_specs,
        scratch_shapes=list(scratch),
        compiler_params=pltpu.CompilerParams(vmem_limit_bytes=24 * 1024 * 1024),
        cost_estimate=pl.CostEstimate(flops=flops, bytes_accessed=moved, transcendentals=0),
        name=name,
    )


def on_device(
    gap_data,
    local_inverse,
    stiffness,
    stiff_column,
    neighbour,
    corner_ops,
    corner_index,
    coarse_inverse,
):
    iface, _, cells = gap_data.shape
    ranks = lax.axis_size("grp")
    sub_count = lax.axis_size("sub")
    right_side = gap_data[:, 0, :]
    inverse = local_inverse[:, :, 0, :]
    stiff = stiffness[:, :, :, 0, :]
    operators = corner_ops[:, :, 0, :]
    blocks_own, order = coarse_inverse.shape[:2]
    owned = blocks_own * (order // CORNER_DOF)
    group = owned * ranks
    corners = corner_index.reshape(1, CORNERS_SUB * cells)

    previous = shifted(right_side, 1)
    indices = (neighbour, stiff_column, corners)
    large = (stiff, operators, right_side)
    selector, swap, table, stiff, operators, right_side = call(
        table_kernel,
        (
            shape(2 * cells, cells, dtype=BF16),
            shape(cells, cells, dtype=BF16),
            shape(group, CORNERS_SUB * cells, dtype=BF16),
        )
        + tuple(jax.ShapeDtypeStruct(array.shape, array.dtype) for array in large),
        kept=3 + LOADED,
        scratch=[pltpu.VMEM(array.shape, jnp.int32) for array in indices] + [pltpu.SemaphoreType.DMA((3 + LOADED,))],
        moved=4 * iface * iface * cells,
        name="tables",
    )(*(pltpu.with_memory_space_constraint(array, pltpu.HBM) for array in indices + large))

    field = shape(iface, cells)
    pair = shape(2, iface, cells)
    message = shape(iface + ROWS, cells)
    rows = shape(ROWS, cells)
    piece = shape(ROWS, owned)
    stiff_scratch = [pltpu.VMEM((iface, cells), F32)]
    stiff_cost = dict(flops=4 * iface * iface * cells, moved=4 * iface * iface * cells)

    def apply_operator(near, far, extra):
        from_far, from_near = swapped_far(far), swapped(near, 1)
        m, gap, farthest, sent, *parts, dots = call(
            lambda *refs: corner_kernel(ranks, *refs),
            (field, field) + (piece,) * (ranks + 1) + (rows,),
            count=7,
            scratch=[pltpu.VMEM((ROWS, group), F32)],
            flops=2 * 24 * iface * cells,
            moved=2 * 24 * iface * cells + group * CORNERS_SUB * cells * 2,
            name="corners",
        )(near, far, from_far, from_near, selector, operators, table)
        parts = [farthest, *parts]
        arrivals = [exchanged(parts[ranks - 1 - d], d) for d in range(ranks - 1, 0, -1)] + [parts[ranks - 1]]
        local = call(
            local_kernel,
            field,
            count=2,
            flops=2 * iface * iface * cells,
            moved=2 * iface * iface * cells,
            name="local",
        )(gap, inverse)
        other = swapped(sent, 2) if extra == "dots" else sent
        solved = call(
            lambda *refs: coarse_kernel(ranks, *refs),
            piece,
            count=3 + ranks,
            scratch=[pltpu.VMEM((ranks, ROWS, owned), F32)],
            flops=2 * blocks_own * order * order,
            moved=2 * blocks_own * order * order,
            name="coarse",
        )(coarse_inverse, dots, arrivals[0], other, *arrivals[1:])
        values = [solved] + [exchanged(solved, d) for d in range(1, ranks)]
        far, near, *result = call(
            lambda *refs: lift_kernel(ranks, extra, *refs),
            (field, field) + {"": (), "dots": (rows,), "lifted": (field,)}[extra],
            count=4 + ranks,
            scratch=[pltpu.VMEM((ROWS, group), F32)],
            flops=2 * 24 * iface * cells,
            moved=2 * 24 * iface * cells + group * CORNERS_SUB * cells * 2,
            name="lift",
        )(local, operators, table, selector, *values)
        return m, gap, near, far, *result

    far, near = call(
        first_kernel, (field, message), count=5, scratch=stiff_scratch, name="first", **stiff_cost
    )(right_side, previous, selector, swap, stiff)
    u, gap_u, near, far = apply_operator(near, far, "")
    r = right_side
    from_far, from_near = swapped_far(far), swapped(near, 1)
    far, near, w = call(
        second_kernel,
        (field, message, pair),
        count=9,
        scratch=stiff_scratch,
        name="second",
        **stiff_cost,
    )(near, far, from_far, from_near, r, u, selector, swap, stiff)

    states = (jnp.zeros((ROWS, cells), F32), r, r, u, w, r, r, r, w, gap_u, r, r)
    outs = (rows, field, field, field, pair, field, field, field, pair, field, field, field, field, message)
    for step in range(ITERS - 2):
        m, gap, near, far, dots = apply_operator(near, far, "dots")
        from_far, from_near, other = swapped_far(far), swapped(near, 1), swapped(dots, 4)
        bit = 8
        while bit < sub_count:
            dots = dots + other
            other = swapped(dots, bit)
            bit *= 2
        *states, far, near = call(
            lambda *refs, first=step == 0: middle_kernel(first, *refs),
            outs,
            count=11 + STATES,
            scratch=stiff_scratch,
            name="middle",
            **stiff_cost,
        )(near, far, from_far, from_near, dots, other, m, gap, selector, swap, stiff, *states)
    scalars, x, r, u, w, p, s, q, z, gap_u, gap_p, gap_q = states
    m, gap, near, far, lifted = apply_operator(near, far, "lifted")
    from_far, from_near = swapped_far(far), swapped(near, 1)
    parts = call(gram_kernel, shape(sub_count * ranks, 1, cells), count=13, name="gram")(
        r, u, w, p, s, q, z, m, gap_u, gap_p, gap_q, gap, lifted
    )
    everyone = lax.all_to_all(parts, ("sub", "grp"), 0, 0, tiled=True)
    x, r = call(final_kernel, (field, field), count=15, name="final")(
        everyone, scalars, x, r, u, w, p, s, q, z, m, near, far, from_far, from_near
    )
    return (x[:, None, :], r[:, None, :])


def solution(mesh):
    in_specs = (
        P(None, "grp", "sub"),
        P(None, None, "grp", "sub"),
        P(None, None, None, "grp", "sub"),
        P("grp", "sub"),
        P("grp", "sub"),
        P(None, None, "grp", "sub"),
        P(None, "grp", "sub"),
        P("grp", None, "sub"),
    )
    out_specs = (P(None, "grp", "sub"), P(None, "grp", "sub"))
    return jax.shard_map(
        on_device, mesh=mesh, in_specs=in_specs, out_specs=out_specs, check_vma=False
    )
```
